256 devices in a mesh: master: 8 (over x, core), region: 32 (over z, y).
Axes of the slice: x: 4, y: 4, z: 8, core: 2. Of those that a mesh axis runs over, the one named last changes fastest.
Arguments:
- masters: float32 [1024, 128, 128], P('master'), may hold values from 0 to 1
- inst_master: int32 [8, 32, 16], P(None, 'region'), may hold values from 0 to 127
- inst_row: int32 [8, 32, 16], P(None, 'region'), may hold values from 0 to 256
- inst_col: int32 [8, 32, 16], P(None, 'region'), may hold values from 0 to 896
- def_index: int32 [32], P('region'), may hold values from 0 to 7
- def_weights: float32 [8, 12], replicated, may hold values from 0.1 to 1
- kernels: bfloat16 [24, 225], replicated, may hold values from -0.375 to 0.375
- target: bfloat16 [32, 384, 1024], P('region', 'master'), may hold values from 0 to 1
Outputs:
- master_grad: float32 [1024, 128, 128], P('master')
- resist: bfloat16 [32, 384, 1024], P('region', 'master')
The draws below stay inside these ranges and needn't reach their ends.
Inputs may be any that keep to these rules, and one draw needn't show every extreme that they name: inst_master[s, r, i] names master s * 128 + inst_master[s, r, i], an instance in the tile of region r; panels of one tile may intersect. `inst_row`: every placed panel lies wholly inside its tile. `inst_col`: every placed panel lies wholly inside its tile.
All inputs are finite; a program needn't handle non-finite values.
Results may differ from the reference program's by a relative error of at most 0.0061.
Values may be sent and summed in bfloat16 or wider, within the bound.
No kernel may reach another device: no remote copies, remote signals or barrier semaphores. Data moves between devices by JAX's collectives and lax.ppermute only.
A program may use at most 128 MiB of HBM per device.

```python
import math
import jax
import jax.numpy as jnp
from jax import lax

TC = 1024
TR = 48
KS = 15
KERN = 12
LEVELS = 8
P_SIZE = 128
MAS_DEV = 128
INST_DEV = 16
SHARDS = 8
REGIONS = 32
MASTERS = 1024
TILE_ROWS = 384
N_MASTER = 8
N_REGION = 32


def touch_ends(drawn, stream_key, low, high):
    index_at = [jax.random.randint(jax.random.fold_in(stream_key, axis), (), 0, length) for axis, length in enumerate(drawn.shape)]
    widest = drawn.shape.index(max(drawn.shape))
    next_to = index_at[:widest] + [(index_at[widest] + 1) % drawn.shape[widest]] + index_at[widest + 1:]
    return drawn.at[tuple(index_at)].set(low).at[tuple(next_to)].set(high)


def steps_of(key, shape, shards, low, largest):
    gain, own = 1.0, jax.random.fold_in(key, 6)
    for dim, blocks in shards:
        draws = jnp.exp(jax.random.uniform(jax.random.fold_in(own, dim), (blocks,), jnp.float32, low / len(shards), largest / len(shards)))
        gain = gain * jnp.repeat(draws, shape[dim] // blocks).reshape([-1 if axis == dim else 1 for axis in range(len(shape))])
    return gain


def noise(own_key, extent, deviation, reach, held_as=jnp.bfloat16):
    drawn = deviation * jax.random.normal(own_key, extent, jnp.float32)
    return jnp.clip(drawn, min=-reach, max=reach).astype(held_as)


def setup_inputs(seed: int = 0) -> dict:
    splits = jax.random.split(jax.random.key(seed), 9)
    masters = jnp.clip(1.0 * jax.random.uniform(splits[0], (MASTERS, P_SIZE, P_SIZE), jnp.float32) ** steps_of(splits[0], (MASTERS, P_SIZE, P_SIZE), ((0, 8),), -0.2, 0.2), 0.0, 1.0)
    inst_master = touch_ends(jax.random.randint(splits[1], (SHARDS, REGIONS, INST_DEV), 0, MAS_DEV), jax.random.fold_in(splits[1], 1), 0, MAS_DEV - 1).astype(jnp.int32)
    inst_row = touch_ends(jax.random.randint(splits[2], (SHARDS, REGIONS, INST_DEV), 0, TR * N_MASTER - P_SIZE + 1), jax.random.fold_in(splits[2], 1), 0, TR * N_MASTER - P_SIZE).astype(jnp.int32)
    inst_col = touch_ends(jax.random.randint(splits[3], (SHARDS, REGIONS, INST_DEV), 0, TC - P_SIZE + 1), jax.random.fold_in(splits[3], 1), 0, TC - P_SIZE).astype(jnp.int32)
    def_index = touch_ends(jax.random.randint(splits[4], (REGIONS,), 0, LEVELS), jax.random.fold_in(splits[4], 1), 0, LEVELS - 1).astype(jnp.int32)
    def_weights = jnp.clip(jnp.exp(jax.random.uniform(splits[5], (LEVELS, KERN), jnp.float32, math.log(0.1), math.log(1.0))), 0.1, 1.0)
    kernels = noise(splits[6], (2 * KERN, KS * KS), (KS * KS) ** -0.5, 0.375)
    target = jnp.clip(1.0 * jax.random.uniform(splits[7], (REGIONS, TILE_ROWS, TC), jnp.float32) ** steps_of(splits[7], (REGIONS, TILE_ROWS, TC), ((0, 32), (1, 8)), -0.2, 0.2), 0.0, 1.0).astype(jnp.bfloat16)
    return dict(masters=masters, inst_master=inst_master, inst_row=inst_row, inst_col=inst_col, def_index=def_index, def_weights=def_weights, kernels=kernels, target=target)


STEEP = 1.5
THRESH = 3.0

def image_region(mask_tile, focus_weights, target_tile, kernels):
    margin = (KS - 1) // 2
    kernel_grid = kernels.astype(jnp.float32).reshape(2 * KERN, 1, KS, KS)

    def forward(field):
        return lax.conv_general_dilated(field, kernel_grid, (1, 1), [(margin, margin), (margin, margin)], precision=lax.Precision.HIGHEST)
    layout_field = mask_tile.astype(jnp.float32)[None, None]
    fields, pullback = jax.vjp(forward, layout_field)
    fields = fields[0]
    doubled = jnp.concatenate([focus_weights, focus_weights])
    intensity = lax.optimization_barrier(jnp.sum(doubled[:, None, None] * fields * fields, axis=0))
    resist_level = 1.0 / (1.0 + jnp.exp(-STEEP * (intensity - THRESH)))
    slope_term = STEEP * (resist_level - target_tile.astype(jnp.float32)) * resist_level * (1.0 - resist_level)
    cotangent = (2.0 * doubled[:, None, None] * slope_term[None] * fields).astype(jnp.bfloat16)
    cotangent = lax.optimization_barrier(cotangent)
    mask_grad = pullback(cotangent.astype(jnp.float32)[None])[0][0, 0]
    return (resist_level.astype(jnp.bfloat16), mask_grad)

def reference(masters, inst_master, inst_row, inst_col, def_index, def_weights, kernels, target):
    panel_values = lax.optimization_barrier(masters.astype(jnp.bfloat16)).astype(jnp.float32)
    slot_total = N_MASTER * INST_DEV
    shard_base = jnp.arange(N_MASTER, dtype=jnp.int32)[:, None] * MAS_DEV

    def one_region(region):
        master_ids = (inst_master[:, region, :] + shard_base).reshape(-1).astype(jnp.int32)
        rows_at = inst_row[:, region, :].reshape(-1).astype(jnp.int32)
        cols_at = inst_col[:, region, :].reshape(-1).astype(jnp.int32)

        def place(slot_index, canvas):
            corner = (rows_at[slot_index], cols_at[slot_index])
            patch_sum = lax.dynamic_slice(canvas, corner, (P_SIZE, P_SIZE)) + panel_values[master_ids[slot_index]]
            return lax.dynamic_update_slice(canvas, patch_sum, corner)
        layout = lax.fori_loop(0, slot_total, place, jnp.zeros((TR * N_MASTER, TC), jnp.float32))
        mask_tile = lax.optimization_barrier(layout.astype(jnp.bfloat16))
        level_pick = (jnp.arange(LEVELS, dtype=jnp.int32) == def_index[region]).astype(jnp.float32)
        focus_weights = lax.optimization_barrier(jnp.sum(level_pick[:, None] * def_weights, axis=0))
        resist_tile, mask_grad = image_region(mask_tile, focus_weights, target[region], kernels)

        def cut_block(row_first, col_first):
            return lax.dynamic_slice(mask_grad, (row_first, col_first), (P_SIZE, P_SIZE))
        panels_grad = jax.vmap(cut_block)(rows_at, cols_at)
        return (resist_tile, master_ids, panels_grad)
    resist, all_ids, all_panels = lax.map(one_region, jnp.arange(N_REGION, dtype=jnp.int32))
    master_grad = jax.ops.segment_sum(all_panels.reshape(-1, P_SIZE, P_SIZE), all_ids.reshape(-1), num_segments=MAS_DEV * N_MASTER)
    return (master_grad, resist)
```

```python
import functools
import jax, jax.numpy as jnp
from jax import lax
from jax.experimental import pallas as pl
from jax.sharding import PartitionSpec as P
from jax.experimental.pallas import tpu as pltpu

TC = 1024; TR = 48; KS = 15; KERN = 12; P_SIZE = 128; MAS_DEV = 128; INST_DEV = 16
STEEP = 1.5; THRESH = 3.0
BR, BC = 8, 16
H = 7
ROWB = 8
MROWB = ROWB + 2
COLB = TC // BC
M = ROWB * COLB
K = 6 * 128
F32, BF = jnp.float32, jnp.bfloat16


def swap_chunks(x):
    n = x.shape[0]
    row = lax.broadcasted_iota(jnp.int32, (n, 128), 0)
    chunk = lax.broadcasted_iota(jnp.int32, (n, 128), 1) // BC

    def sub(v, k):
        return pltpu.roll(v.reshape(n // 8, 8, 128), k, 1).reshape(n, 128)

    for k in (1, 2, 4):
        rbit = (row & k) != 0
        cbit = (chunk & k) != 0
        up = sub(pltpu.roll(x, 128 - BC * k, 1), k)
        if k == 4:
            dn = up
        else:
            dn = sub(pltpu.roll(x, BC * k, 1), 8 - k)
        x = jnp.where(rbit == cbit, x, jnp.where(rbit, up, dn))
    return x


def to_blocks(x):
    a, b = x.shape[0] // 8, x.shape[1] // 128
    tiles = [x[8 * i : 8 * i + 8, 128 * t : 128 * t + 128] for i in range(a) for t in range(b)]
    return swap_chunks(jnp.concatenate(tiles, axis=0))


def from_blocks(v, a, b):
    x = swap_chunks(v)
    rows = []
    for i in range(a):
        rows.append(jnp.concatenate([x[(i * b + t) * 8 : (i * b + t) * 8 + 8] for t in range(b)], axis=1))
    return jnp.concatenate(rows, axis=0)


def table_kernel(v_ref, w_ref):
    lane = lax.broadcasted_iota(jnp.int32, (16, 512), 1) % BC
    row = lax.broadcasted_iota(jnp.int32, (16, 512), 0)
    low = lane <= row

    def one(c, carry):
        x = jnp.broadcast_to(v_ref[c], (16, 512))
        r = pltpu.roll(x, 1, 1, stride=1, stride_axis=0)
        lo = jnp.where(low, r, 0.0)
        hi = jnp.where(low, 0.0, r)
        for p in range(8):
            lp = (pltpu.roll(lo, 512 - 16 * p, 1) if p else lo).astype(BF)
            hp = (pltpu.roll(hi, 512 - 16 * p, 1) if p else hi).astype(BF)
            for wy in range(24):
                dy, yw = wy // 8, wy % 8
                if (24 - wy) % 8 == p:
                    q = (24 - wy) // 8
                    w_ref[c, (dy * 2) * 128 + yw * 16 : (dy * 2) * 128 + yw * 16 + 16, :] = lp[:, 128 * q : 128 * q + 128]
                if (23 - wy) % 8 == p:
                    q = (23 - wy) // 8
                    w_ref[c, (dy * 2 + 1) * 128 + yw * 16 : (dy * 2 + 1) * 128 + yw * 16 + 16, :] = hp[:, 128 * q : 128 * q + 128]
        return carry

    lax.fori_loop(0, 2 * KERN, one, 0)


def taps_rows(kernels):
    k = kernels.astype(F32).reshape(2 * KERN, KS, KS)
    k = k[:, ::-1, ::-1]
    k = jnp.pad(k, ((0, 0), (9, 32 - 9 - KS), (1, 0)))
    return k.reshape(2 * KERN, 1, 512)


def make_table(kernels):
    return pl.pallas_call(
        table_kernel,
        out_shape=jax.ShapeDtypeStruct((2 * KERN, K, 128), BF),
        in_specs=[pl.BlockSpec(memory_space=pltpu.VMEM)],
        out_specs=pl.BlockSpec(memory_space=pltpu.VMEM),
        compiler_params=pltpu.CompilerParams(vmem_limit_bytes=32 * 1024 * 1024),
        name="taps_table",
    )(taps_rows(kernels))


def image_kernel(level_ref, shard_ref, wgt_ref, above_ref, mid_ref, below_ref, tabove_ref, tmid_ref, tbelow_ref, w_ref,
                 resist_ref, grad_ref, lhs_ref, fields_ref, cot_ref):
    level_at = level_ref[0]
    x = jnp.concatenate([above_ref[...].astype(F32), mid_ref[...].astype(BF).astype(F32), below_ref[...].astype(F32)], axis=0)
    x = pltpu.roll(x, 8 * MROWB - 1, 0)
    x = jnp.concatenate([x, jnp.zeros((8 * MROWB, 128), F32)], axis=1)
    x = pltpu.roll(x, H, 1)
    mb = to_blocks(x).reshape(MROWB, 72, 128)
    for dy in range(3):
        for dx in range(2):
            part = mb[dy : dy + ROWB, dx : dx + COLB, :]
            lhs_ref[:, (dy * 2 + dx) * 128 : (dy * 2 + dx) * 128 + 128] = part.reshape(M, 128).astype(BF)
    intensity = jnp.zeros((M, 128), F32)
    for c in range(KERN):
        acc = None
        for part in range(2):
            f = jnp.dot(lhs_ref[...], w_ref[part * KERN + c], preferred_element_type=F32)
            fields_ref[part * KERN + c] = f
            acc = f * f if acc is None else acc + f * f
        intensity = intensity + wgt_ref[level_at, c] * acc
    level = 1.0 / (1.0 + jnp.exp(-STEEP * (intensity - THRESH)))
    resist_ref[...] = from_blocks(level, ROWB, 8)[8 : 8 + TR].astype(BF)
    goal = jnp.concatenate([tabove_ref[...].astype(F32)[8:], tmid_ref[...].astype(F32), tbelow_ref[...].astype(F32)[:8]], axis=0)
    goal = to_blocks(goal)
    slope = STEEP * (level - goal) * level * (1.0 - level)
    row_block = lax.broadcasted_iota(jnp.int32, (M, 128), 0) // COLB
    in_block = lax.broadcasted_iota(jnp.int32, (M, 128), 1) // BC
    at = shard_ref[0] * TR - 8 + row_block * 8 + in_block
    slope = jnp.where((at >= 0) & (at < 8 * TR), slope, 0.0)
    for c in range(KERN):
        s = 2.0 * wgt_ref[level_at, c] * slope
        for part in range(2):
            i = part * KERN + c
            cot_ref[:, i * 128 : i * 128 + 128] = (s * fields_ref[i]).astype(BF)
    out = [None] * 7
    for dy in range(3):
        for dx in range(2):
            q = dy * 2 + dx
            acc = jnp.zeros((M, 128), F32)
            for c in range(2 * KERN):
                acc = acc + lax.dot_general(cot_ref[:, c * 128 : c * 128 + 128], w_ref[c, q * 128 : q * 128 + 128, :],
                                            (((1,), (1,)), ((), ())), preferred_element_type=F32)
            for i in range(ROWB):
                j = i + dy
                if 1 <= j <= 7:
                    piece = acc[i * COLB : i * COLB + COLB]
                    z8 = jnp.zeros((8, 128), F32)
                    piece = jnp.concatenate([piece, z8], axis=0)
                    if dx:
                        piece = pltpu.roll(piece, 1, 0)
                    out[j - 1] = piece if out[j - 1] is None else out[j - 1] + piece
    nat = from_blocks(jnp.concatenate(out, axis=0), 7, 9)
    nat = pltpu.roll(nat, 9 * 128 - H, 1)
    grad_ref[...] = nat[H : H + TR, :TC].astype(grad_ref.dtype)


def image(level, shard, weights, above, mid, below, tabove, tmid, tbelow, table):
    vm = pl.BlockSpec(memory_space=pltpu.VMEM)
    sm = pl.BlockSpec(memory_space=pltpu.SMEM)
    return pl.pallas_call(
        image_kernel,
        out_shape=(jax.ShapeDtypeStruct((TR, TC), BF), jax.ShapeDtypeStruct((TR, TC), BF)),
        in_specs=[sm] * 3 + [vm] * 7,
        out_specs=(vm, vm),
        scratch_shapes=[pltpu.VMEM((M, K), BF), pltpu.VMEM((2 * KERN, M, 128), F32), pltpu.VMEM((M, 2 * KERN * 128), BF)],
        compiler_params=pltpu.CompilerParams(vmem_limit_bytes=48 * 1024 * 1024),
        name="image",
    )(level, shard, weights, above, mid, below, tabove, tmid, tbelow, table)


def own(shard_ref, *refs):
    s = shard_ref[0]
    return [[ref[s, 0, i] for i in range(INST_DEV)] for ref in refs]


WIDE = TC + 128
LEAD = 16

def place_kernel(shard_ref, ids_ref, rows_ref, cols_ref, masters_ref, out_ref, panels, canvas, sem):
    ids, rows, cols = own(shard_ref, ids_ref, rows_ref, cols_ref)
    copies = []
    for i in range(INST_DEV):
        cp = pltpu.make_async_copy(masters_ref.at[ids[i]], panels.at[i], sem.at[i])
        cp.start()
        copies.append(cp)
    canvas[...] = jnp.zeros(canvas.shape, F32)
    lane = lax.broadcasted_iota(jnp.int32, (P_SIZE, 128), 1)
    for i in range(INST_DEV):
        copies[i].wait()
        p = panels[i].astype(BF).astype(F32)
        c = cols[i]
        c0 = (c // 128) * 128
        d = c - c0
        p = pltpu.roll(p, d, 1)
        left = jnp.where(lane >= d, p, 0.0)
        right = jnp.where(lane >= d, 0.0, p)
        full = jnp.concatenate([jnp.concatenate([left, right], axis=1), jnp.zeros((8, 256), F32)], axis=0)
        r = rows[i] + LEAD
        r0 = (r // 8) * 8
        full = pltpu.roll(full, r - r0, 0)
        at = (pl.ds(pl.multiple_of(r0, 8), P_SIZE + 8), pl.ds(pl.multiple_of(c0, 128), 256))
        canvas[at] = canvas[at] + full
    out_ref[...] = canvas[LEAD : LEAD + 8 * TR, :TC].reshape(8, TR, TC).astype(out_ref.dtype)


def place(shard, ids, rows, cols, masters):
    return pl.pallas_call(
        place_kernel,
        out_shape=jax.ShapeDtypeStruct((8, TR, TC), F32),
        in_specs=[pl.BlockSpec(memory_space=pltpu.SMEM)] * 4 + [pl.BlockSpec(memory_space=pl.ANY)],
        out_specs=pl.BlockSpec(memory_space=pltpu.VMEM),
        scratch_shapes=[pltpu.VMEM((INST_DEV, P_SIZE, P_SIZE), F32), pltpu.VMEM((LEAD + 8 * TR + 16, WIDE), F32), pltpu.SemaphoreType.DMA((INST_DEV,))],
        compiler_params=pltpu.CompilerParams(vmem_limit_bytes=32 * 1024 * 1024),
        name="place",
    )(shard, ids, rows, cols, masters)


def cut_kernel(shard_ref, ids_ref, rows_ref, cols_ref, grad_ref, out_ref, canvas, sums):
    ids, rows, cols = own(shard_ref, ids_ref, rows_ref, cols_ref)
    canvas[: 8 * TR, :TC] = grad_ref[...].astype(F32)
    lane = lax.broadcasted_iota(jnp.int32, (P_SIZE, 128), 1)
    out_ref[...] = jnp.zeros(out_ref.shape, out_ref.dtype)
    sums[...] = jnp.zeros(sums.shape, F32)
    slots = []
    for i in range(INST_DEV):
        c = cols[i]
        c0 = (c // 128) * 128
        d = c - c0
        r = rows[i]
        r0 = (r // 8) * 8
        full = canvas[pl.ds(pl.multiple_of(r0, 8), P_SIZE + 8), pl.ds(pl.multiple_of(c0, 128), 256)]
        full = pltpu.roll(full, P_SIZE + 8 - (r - r0), 0)[:P_SIZE]
        full = pltpu.roll(full, 256 - d, 1)[:, :128]
        slot = jnp.int32(i)
        for j in range(i - 1, -1, -1):
            slot = jnp.where(ids[j] == ids[i], jnp.int32(j), slot)
        slots.append(slot)
        sums[slot] = sums[slot] + full
    for i in range(INST_DEV):
        out_ref[ids[i]] = sums[slots[i]].astype(out_ref.dtype)


def cut(shard, ids, rows, cols, grad):
    vm = pl.BlockSpec(memory_space=pltpu.VMEM)
    return pl.pallas_call(
        cut_kernel,
        out_shape=jax.ShapeDtypeStruct((MAS_DEV, P_SIZE, P_SIZE), BF),
        in_specs=[pl.BlockSpec(memory_space=pltpu.SMEM)] * 4 + [vm],
        out_specs=vm,
        scratch_shapes=[pltpu.VMEM((8 * TR + 8, WIDE), F32), pltpu.VMEM((INST_DEV, P_SIZE, P_SIZE), F32)],
        compiler_params=pltpu.CompilerParams(vmem_limit_bytes=32 * 1024 * 1024),
        name="cut",
    )(shard, ids, rows, cols, grad)


def halo(x, axis, width):
    n = lax.axis_size(axis)
    above = lax.ppermute(x[-width:], axis, [(i, i + 1) for i in range(n - 1)])
    below = lax.ppermute(x[:width], axis, [(i + 1, i) for i in range(n - 1)])
    return above, below


def body(masters, inst_master, inst_row, inst_col, def_index, def_weights, kernels, target):
    shard = lax.axis_index("master").reshape(1)
    tmid = target[0]
    tabove, tbelow = halo(tmid, "master", 16)
    layout = place(shard, inst_master, inst_row, inst_col, masters)
    mid = lax.psum_scatter(layout.reshape(8 * TR, TC), "master", scatter_dimension=0, tiled=True)
    table = make_table(kernels)
    above, below = halo(mid.astype(BF), "master", 16)
    resist, grad = image(def_index, shard, def_weights, above, mid, below, tabove, tmid, tbelow, table)
    full = lax.all_gather(grad, "master", axis=0, tiled=True)
    summed = cut(shard, inst_master, inst_row, inst_col, full)
    master_grad = lax.psum(summed.astype(F32), "region")
    return (master_grad, resist[None])


def solution(mesh):
    return jax.shard_map(
        body,
        mesh=mesh,
        in_specs=(
            P("master", None, None),
            P(None, "region", None),
            P(None, "region", None),
            P(None, "region", None),
            P("region"),
            P(),
            P(),
            P("region", "master", None),
        ),
        out_specs=(P("master", None, None), P("region", "master", None)),
        check_vma=False,
    )
```

```python
import functools
import jax, jax.numpy as jnp
from jax import lax
from jax.experimental import pallas as pl
from jax.sharding import Mesh, PartitionSpec as P
from jax.experimental.pallas import tpu as pltpu

TC = 1024; TR = 48; KS = 15; KERN = 12; P_SIZE = 128; MAS_DEV = 128; INST_DEV = 16
STEEP = 1.5; THRESH = 3.0
BR, BC = 8, 16
H = 7
ROWB = 8
MROWB = ROWB + 2
COLB = TC // BC
M = ROWB * COLB
K = 6 * 128
F32, BF = jnp.float32, jnp.bfloat16


def swap_chunks(x):
    n = x.shape[0]
    row = lax.broadcasted_iota(jnp.int32, (n, 128), 0)
    chunk = lax.broadcasted_iota(jnp.int32, (n, 128), 1) // BC

    def sub(v, k):
        return pltpu.roll(v.reshape(n // 8, 8, 128), k, 1).reshape(n, 128)

    for k in (1, 2, 4):
        rbit = (row & k) != 0
        cbit = (chunk & k) != 0
        up = sub(pltpu.roll(x, 128 - BC * k, 1), k)
        if k == 4:
            dn = up
        else:
            dn = sub(pltpu.roll(x, BC * k, 1), 8 - k)
        x = jnp.where(rbit == cbit, x, jnp.where(rbit, up, dn))
    return x


def to_blocks(x):
    a, b = x.shape[0] // 8, x.shape[1] // 128
    tiles = [x[8 * i : 8 * i + 8, 128 * t : 128 * t + 128] for i in range(a) for t in range(b)]
    return swap_chunks(jnp.concatenate(tiles, axis=0))


def from_blocks(v, a, b):
    x = swap_chunks(v)
    rows = []
    for i in range(a):
        rows.append(jnp.concatenate([x[(i * b + t) * 8 : (i * b + t) * 8 + 8] for t in range(b)], axis=1))
    return jnp.concatenate(rows, axis=0)


def table_kernel(v_ref, w_ref):
    lane = lax.broadcasted_iota(jnp.int32, (16, 512), 1) % BC
    row = lax.broadcasted_iota(jnp.int32, (16, 512), 0)
    low = lane <= row

    def one(c, carry):
        at = pl.ds(pl.multiple_of(c * 128, 128), 128)
        x = jnp.broadcast_to(v_ref[c], (16, 512))
        r = pltpu.roll(x, 1, 1, stride=1, stride_axis=0)
        lo = jnp.where(low, r, 0.0)
        hi = jnp.where(low, 0.0, r)
        for p in range(8):
            lp = (pltpu.roll(lo, 512 - 16 * p, 1) if p else lo).astype(BF)
            hp = (pltpu.roll(hi, 512 - 16 * p, 1) if p else hi).astype(BF)
            for wy in range(24):
                dy, yw = wy // 8, wy % 8
                if (24 - wy) % 8 == p:
                    q = (24 - wy) // 8
                    w_ref[(dy * 2) * 128 + yw * 16 : (dy * 2) * 128 + yw * 16 + 16, at] = lp[:, 128 * q : 128 * q + 128]
                if (23 - wy) % 8 == p:
                    q = (23 - wy) // 8
                    w_ref[(dy * 2 + 1) * 128 + yw * 16 : (dy * 2 + 1) * 128 + yw * 16 + 16, at] = hp[:, 128 * q : 128 * q + 128]
        return carry

    lax.fori_loop(0, 2 * KERN, one, 0)


def taps_rows(kernels):
    k = kernels.astype(F32).reshape(2, KERN, KS, KS).swapaxes(0, 1).reshape(2 * KERN, KS, KS)
    k = k[:, ::-1, ::-1]
    k = jnp.pad(k, ((0, 0), (9, 32 - 9 - KS), (1, 0)))
    return k.reshape(2 * KERN, 1, 512)


def make_table(kernels):
    return pl.pallas_call(
        table_kernel,
        out_shape=jax.ShapeDtypeStruct((K, 2 * KERN * 128), BF),
        in_specs=[pl.BlockSpec(memory_space=pltpu.VMEM)],
        out_specs=pl.BlockSpec(memory_space=pltpu.VMEM),
        compiler_params=pltpu.CompilerParams(vmem_limit_bytes=32 * 1024 * 1024),
        cost_estimate=pl.CostEstimate(flops=20_000_000, bytes_accessed=10_000_000, transcendentals=0),
        name="taps_table",
    )(taps_rows(kernels))


def image_kernel(level_ref, shard_ref, wgt_ref, m0_ref, m1_ref, m2_ref, m3_ref, tabove_ref, tmid_ref, tbelow_ref, w_ref,
                 resist_ref, grad_ref, lhs_ref, fields_ref, cot_ref):
    level_at = level_ref[0]
    x = (m0_ref[...] + m1_ref[...] + m2_ref[...] + m3_ref[...]).astype(BF).astype(F32)
    x = pltpu.roll(x, 8 * MROWB - 1, 0)
    x = jnp.concatenate([x, jnp.zeros((8 * MROWB, 128), F32)], axis=1)
    x = pltpu.roll(x, H, 1)
    mb = to_blocks(x).reshape(MROWB, 72, 128)
    for dy in range(3):
        for dx in range(2):
            part = mb[dy : dy + ROWB, dx : dx + COLB, :]
            lhs_ref[:, (dy * 2 + dx) * 128 : (dy * 2 + dx) * 128 + 128] = part.reshape(M, 128).astype(BF)
    intensity = jnp.zeros((M, 128), F32)
    for c in range(KERN):
        f = jnp.dot(lhs_ref[...], w_ref[:, c * 256 : c * 256 + 256], preferred_element_type=F32)
        fields_ref[c] = f
        f = f * f
        intensity = intensity + wgt_ref[level_at, c] * (f[:, :128] + f[:, 128:])
    level = 1.0 / (1.0 + jnp.exp(-STEEP * (intensity - THRESH)))
    resist_ref[...] = from_blocks(level, ROWB, 8)[8 : 8 + TR].astype(BF)
    goal = jnp.concatenate([tabove_ref[...].astype(F32)[8:], tmid_ref[...].astype(F32), tbelow_ref[...].astype(F32)[:8]], axis=0)
    goal = to_blocks(goal)
    slope = STEEP * (level - goal) * level * (1.0 - level)
    row_block = lax.broadcasted_iota(jnp.int32, (M, 128), 0) // COLB
    in_block = lax.broadcasted_iota(jnp.int32, (M, 128), 1) // BC
    at = shard_ref[0] * TR - 8 + row_block * 8 + in_block
    slope = jnp.where((at >= 0) & (at < 8 * TR), slope, 0.0)
    for c in range(KERN):
        s = 2.0 * wgt_ref[level_at, c] * slope
        cot_ref[:, c * 256 : c * 256 + 256] = (jnp.concatenate([s, s], axis=1) * fields_ref[c]).astype(BF)
    out = [None] * 7
    for dy in range(3):
        acc = lax.dot_general(cot_ref[...], w_ref[dy * 256 : dy * 256 + 256, :], (((1,), (1,)), ((), ())), preferred_element_type=F32)
        for dx in range(2):
            for i in range(ROWB):
                j = i + dy
                if 1 <= j <= 7:
                    piece = acc[i * COLB : i * COLB + COLB, dx * 128 : dx * 128 + 128]
                    piece = jnp.concatenate([piece, jnp.zeros((8, 128), F32)], axis=0)
                    if dx:
                        piece = pltpu.roll(piece, 1, 0)
                    out[j - 1] = piece if out[j - 1] is None else out[j - 1] + piece
    nat = from_blocks(jnp.concatenate(out, axis=0), 7, 9)
    nat = pltpu.roll(nat, 9 * 128 - H, 1)
    grad_ref[...] = nat[H : H + TR, :TC].astype(grad_ref.dtype)


def image(level, shard, weights, parts, tabove, tmid, tbelow, table):
    vm = pl.BlockSpec(memory_space=pltpu.VMEM)
    sm = pl.BlockSpec(memory_space=pltpu.SMEM)
    return pl.pallas_call(
        image_kernel,
        out_shape=(jax.ShapeDtypeStruct((TR, TC), BF), jax.ShapeDtypeStruct((TR, TC), BF)),
        in_specs=[sm] * 3 + [vm] * 8,
        out_specs=(vm, vm),
        scratch_shapes=[pltpu.VMEM((M, K), BF), pltpu.VMEM((KERN, M, 256), F32), pltpu.VMEM((M, 2 * KERN * 128), BF)],
        compiler_params=pltpu.CompilerParams(vmem_limit_bytes=48 * 1024 * 1024),
        cost_estimate=pl.CostEstimate(flops=5_000_000_000, bytes_accessed=8_000_000, transcendentals=65536),
        name="image",
    )(level, shard, weights, *parts, tabove, tmid, tbelow, table)


NX, NC, NY, NZ = 4, 2, 4, 8
WIDE = TC + 128
LEAD = 16
EXT = TR + 2 * LEAD
INFO = 64


def place_kernel(shard_ref, ids_hbm, rows_hbm, cols_hbm, masters_hbm, mine_ref, theirs_ref, info_ref, scalars, panels, canvas, sem, info_sem):
    shard = shard_ref[0]
    loads = [pltpu.make_async_copy(ref.at[shard], scalars.at[j], info_sem.at[j]) for j, ref in enumerate((ids_hbm, rows_hbm, cols_hbm))]
    for cp in loads:
        cp.start()
    for cp in loads:
        cp.wait()
    copies = []
    for i in range(INST_DEV):
        cp = pltpu.make_async_copy(masters_hbm.at[scalars[0, 0, i]], panels.at[i], sem.at[i])
        cp.start()
        copies.append(cp)
        for j in range(3):
            info_ref[0, j * INST_DEV + i] = scalars[j, 0, i]
    for i in range(3 * INST_DEV, INFO):
        info_ref[0, i] = 0
    canvas[...] = jnp.zeros(canvas.shape, F32)
    lane = lax.broadcasted_iota(jnp.int32, (P_SIZE, 128), 1)
    for i in range(INST_DEV):
        copies[i].wait()
        p = panels[i].astype(BF).astype(F32)
        c = scalars[2, 0, i]
        c0 = (c // 128) * 128
        d = c - c0
        p = pltpu.roll(p, d, 1)
        left = jnp.where(lane >= d, p, 0.0)
        right = jnp.where(lane >= d, 0.0, p)
        full = jnp.concatenate([jnp.concatenate([left, right], axis=1), jnp.zeros((8, 256), F32)], axis=0)
        r = scalars[1, 0, i] + LEAD
        r0 = (r // 8) * 8
        full = pltpu.roll(full, r - r0, 0)
        at = (pl.ds(pl.multiple_of(r0, 8), P_SIZE + 8), pl.ds(pl.multiple_of(c0, 128), 256))
        canvas[at] = canvas[at] + full
    core = shard % NC
    for d in range(NX):
        x = (shard // NC + d) % NX
        mine_ref[d] = canvas[pl.ds(pl.multiple_of((x * NC + core) * TR, 8), EXT), :TC]
        theirs_ref[d] = canvas[pl.ds(pl.multiple_of((x * NC + 1 - core) * TR, 8), EXT), :TC]


def place(shard, ids, rows, cols, masters):
    vm = pl.BlockSpec(memory_space=pltpu.VMEM)
    sm = pl.BlockSpec(memory_space=pltpu.SMEM)
    hbm = pl.BlockSpec(memory_space=pltpu.HBM)
    bands = jax.ShapeDtypeStruct((NX, EXT, TC), F32)
    return pl.pallas_call(
        place_kernel,
        out_shape=(bands, bands, jax.ShapeDtypeStruct((1, INFO), jnp.int32)),
        in_specs=[sm] + [hbm] * 4,
        out_specs=(vm, vm, sm),
        scratch_shapes=[
            pltpu.SMEM((3, 1, INST_DEV), jnp.int32),
            pltpu.VMEM((INST_DEV, P_SIZE, P_SIZE), F32),
            pltpu.VMEM((LEAD + 8 * TR + LEAD, WIDE), F32),
            pltpu.SemaphoreType.DMA((INST_DEV,)),
            pltpu.SemaphoreType.DMA((3,)),
        ],
        compiler_params=pltpu.CompilerParams(vmem_limit_bytes=32 * 1024 * 1024),
        cost_estimate=pl.CostEstimate(flops=1_000_000, bytes_accessed=12_000_000, transcendentals=0),
        name="place",
    )(shard, ids, rows, cols, masters)


def cut_kernel(shard_ref, region_ref, i0, i1, i2, i3, own_ref, up_ref, down_ref, far0_ref, far1_ref, out_ref, canvas):
    x = shard_ref[0] // NC
    z, y = region_ref[0] // NY, region_ref[0] % NY
    out_ref[...] = jnp.zeros(out_ref.shape, F32)

    def lay(ref, n, at, k):
        for core in range(NC):
            row = ((x + n) % NX * NC + core) * TR
            canvas[at, pl.ds(pl.multiple_of(row, 8), TR), :TC] = ref[core, k].astype(F32)

    for k in range(NY):
        lay(own_ref, 0, k, k)
        lay(up_ref, 3, k, k)
        lay(down_ref, 1, k, k)
        lay(far0_ref if k < 2 else far1_ref, 2, k, k % 2)
    for k, info in enumerate((i0, i1, i2, i3)):

        def one(i, carry, k=k, info=info):
            m = info[0, i]

            @pl.when((m // 4) % NY == y)
            def _():
                r, c = info[0, INST_DEV + i], info[0, 2 * INST_DEV + i]
                r0, c0 = (r // 8) * 8, (c // 128) * 128
                full = canvas[k, pl.ds(pl.multiple_of(r0, 8), P_SIZE + 8), pl.ds(pl.multiple_of(c0, 128), 256)]
                full = pltpu.roll(full, P_SIZE + 8 - (r - r0), 0)[:P_SIZE]
                full = pltpu.roll(full, 256 - (c - c0), 1)[:, :128]
                slot = (m // 16 - z + NZ) % NZ
                out_ref[slot, m % 4] = out_ref[slot, m % 4] + full

            return carry

        lax.fori_loop(0, INST_DEV, one, 0)


def cut(shard, region, infos, bands):
    vm = pl.BlockSpec(memory_space=pltpu.VMEM)
    sm = pl.BlockSpec(memory_space=pltpu.SMEM)
    return pl.pallas_call(
        cut_kernel,
        out_shape=jax.ShapeDtypeStruct((NZ, 4, P_SIZE, P_SIZE), F32),
        in_specs=[sm] * 6 + [vm] * 5,
        out_specs=vm,
        scratch_shapes=[pltpu.VMEM((NY, 8 * TR + 8, WIDE), F32)],
        compiler_params=pltpu.CompilerParams(vmem_limit_bytes=40 * 1024 * 1024),
        cost_estimate=pl.CostEstimate(flops=1_000_000, bytes_accessed=12_000_000, transcendentals=0),
        name="cut",
    )(shard, region, *infos, *bands)


def deposit_kernel(region_ref, own_ref, out_ref, wide, sem):
    wide[...] = own_ref[...].astype(F32)
    cp = pltpu.make_async_copy(wide, out_ref.at[region_ref[0] // NY], sem)
    cp.start()
    cp.wait()


def deposit(region, own):
    return pl.pallas_call(
        deposit_kernel,
        out_shape=jax.ShapeDtypeStruct((NZ, 16, P_SIZE, P_SIZE), F32),
        in_specs=[pl.BlockSpec(memory_space=pltpu.SMEM), pl.BlockSpec(memory_space=pltpu.VMEM)],
        out_specs=pl.BlockSpec(memory_space=pltpu.HBM),
        scratch_shapes=[pltpu.VMEM((16, P_SIZE, P_SIZE), F32), pltpu.SemaphoreType.DMA],
        compiler_params=pltpu.CompilerParams(vmem_limit_bytes=8 * 1024 * 1024),
        cost_estimate=pl.CostEstimate(flops=1_000_000, bytes_accessed=1_500_000, transcendentals=0),
        name="deposit",
    )(region, own)


def shift(v, axis, by):
    n = lax.axis_size(axis)
    return lax.ppermute(v, axis, [(i, (i + by) % n) for i in range(n)])


def halo(v, axis, width):
    n = lax.axis_size(axis)
    above = lax.ppermute(v[-width:], axis, [(i, i + 1) for i in range(n - 1)])
    below = lax.ppermute(v[:width], axis, [(i + 1, i) for i in range(n - 1)])
    return above, below


def sum_along_z(g):
    up = shift(g[4, :2].astype(BF), "z", 1)
    down = shift(g[4, 2:].astype(BF), "z", -1)
    for d in (3, 2, 1):
        if d == 3:
            mine_up = jnp.concatenate([g[3, :2] + up.astype(F32), g[3, 2:]])
            mine_down = jnp.concatenate([g[5, :2], g[5, 2:] + down.astype(F32)])
        else:
            mine_up = g[d] + up.astype(F32)
            mine_down = g[NZ - d] + down.astype(F32)
        up = shift(mine_up.astype(BF), "z", 1)
        down = shift(mine_down.astype(BF), "z", -1)
    return g[0] + up.astype(F32) + down.astype(F32)


def body(masters, inst_master, inst_row, inst_col, def_index, def_weights, kernels, target):
    shard = lax.axis_index(("x", "core")).reshape(1)
    region = lax.axis_index(("z", "y")).reshape(1)
    x, z, y = lax.axis_index("x"), lax.axis_index("z"), lax.axis_index("y")
    mine, theirs, info = place(shard, inst_master, inst_row, inst_col, masters)
    other = shift(theirs, "core", 1)
    sums = [mine[d] + other[d] for d in range(NX)]
    parts = [sums[0]] + [shift(sums[d], "x", d) for d in (1, 2, 3)]
    tmid = target[0]
    tabove, tbelow = halo(tmid, ("x", "core"), 16)
    infos = [info] + [shift(info, "y", k) for k in (1, 2, 3)]
    table = make_table(kernels)
    resist, grad = image(def_index, shard, def_weights, parts, tabove, tmid, tbelow, table)
    own = jnp.stack([grad] + [shift(grad, "y", k) for k in (1, 2, 3)])
    up, down = shift(own, "x", 1), shift(own, "x", -1)
    far0, far1 = shift(up[:2], "x", 1), shift(down[2:], "x", -1)
    bands = [lax.all_gather(v, "core") for v in (own, up, down, far0, far1)]
    summed = cut(shard, region, infos, bands)
    part = sum_along_z(summed).astype(BF)
    block = jnp.zeros((NY, 4, P_SIZE, P_SIZE), BF)
    for k, v in enumerate([part] + [shift(part, "y", k) for k in (1, 2, 3)]):
        block = lax.dynamic_update_slice(block, v[None], ((y + NY - k) % NY, 0, 0, 0))
    block = block.reshape(16, P_SIZE, P_SIZE)
    out = deposit(region, block)
    halves = (block[:8], block[8:])
    ups, downs = list(halves), list(halves)
    for d in (1, 2, 3, 4):
        for h in range(2):
            if d < 4 or h == 0:
                ups[h] = shift(ups[h], "z", 1)
                out = lax.dynamic_update_slice(out, ups[h].astype(F32)[None], ((z + NZ - d) % NZ, 8 * h, 0, 0))
            if d < 4 or h == 1:
                downs[h] = shift(downs[h], "z", -1)
                out = lax.dynamic_update_slice(out, downs[h].astype(F32)[None], ((z + d) % NZ, 8 * h, 0, 0))
    return (out.reshape(MAS_DEV, P_SIZE, P_SIZE), resist[None])


def solution(mesh):
    fine = Mesh(mesh.devices.reshape(NX, NC, NZ, NY), ("x", "core", "z", "y"))
    master, region = ("x", "core"), ("z", "y")
    return jax.shard_map(
        body,
        mesh=fine,
        in_specs=(
            P(master, None, None),
            P(None, region, None),
            P(None, region, None),
            P(None, region, None),
            P(region),
            P(),
            P(),
            P(region, master, None),
        ),
        out_specs=(P(master, None, None), P(region, master, None)),
        check_vma=False,
    )
```

```python
import functools
import jax, jax.numpy as jnp
from jax import lax
from jax.experimental import pallas as pl
from jax.sharding import Mesh, PartitionSpec as P
from jax.experimental.pallas import tpu as pltpu

TC = 1024; TR = 48; KS = 15; KERN = 12; P_SIZE = 128; MAS_DEV = 128; INST_DEV = 16
STEEP = 1.5; THRESH = 3.0
BR, BC = 8, 16
H = 7
ROWB = 8
MROWB = ROWB + 2
COLB = TC // BC
M = ROWB * COLB
K = 6 * 128
F32, BF = jnp.float32, jnp.bfloat16


def swap_chunks(x):
    n = x.shape[0]
    row = lax.broadcasted_iota(jnp.int32, (n, 128), 0)
    chunk = lax.broadcasted_iota(jnp.int32, (n, 128), 1) // BC

    def sub(v, k):
        return pltpu.roll(v.reshape(n // 8, 8, 128), k, 1).reshape(n, 128)

    for k in (1, 2, 4):
        rbit = (row & k) != 0
        cbit = (chunk & k) != 0
        up = sub(pltpu.roll(x, 128 - BC * k, 1), k)
        if k == 4:
            dn = up
        else:
            dn = sub(pltpu.roll(x, BC * k, 1), 8 - k)
        x = jnp.where(rbit == cbit, x, jnp.where(rbit, up, dn))
    return x


def to_blocks(x):
    a, b = x.shape[0] // 8, x.shape[1] // 128
    tiles = [x[8 * i : 8 * i + 8, 128 * t : 128 * t + 128] for i in range(a) for t in range(b)]
    return swap_chunks(jnp.concatenate(tiles, axis=0))


def from_blocks(v, a, b):
    x = swap_chunks(v)
    rows = []
    for i in range(a):
        rows.append(jnp.concatenate([x[(i * b + t) * 8 : (i * b + t) * 8 + 8] for t in range(b)], axis=1))
    return jnp.concatenate(rows, axis=0)


def table_kernel(v_ref, w_ref):
    lane = lax.broadcasted_iota(jnp.int32, (16, 512), 1) % BC
    row = lax.broadcasted_iota(jnp.int32, (16, 512), 0)
    low = lane <= row

    def one(c, carry):
        at = pl.ds(pl.multiple_of(c * 128, 128), 128)
        x = jnp.broadcast_to(v_ref[c], (16, 512))
        r = pltpu.roll(x, 1, 1, stride=1, stride_axis=0)
        lo = jnp.where(low, r, 0.0)
        hi = jnp.where(low, 0.0, r)
        for p in range(8):
            lp = (pltpu.roll(lo, 512 - 16 * p, 1) if p else lo).astype(BF)
            hp = (pltpu.roll(hi, 512 - 16 * p, 1) if p else hi).astype(BF)
            for wy in range(24):
                dy, yw = wy // 8, wy % 8
                if (24 - wy) % 8 == p:
                    q = (24 - wy) // 8
                    w_ref[(dy * 2) * 128 + yw * 16 : (dy * 2) * 128 + yw * 16 + 16, at] = lp[:, 128 * q : 128 * q + 128]
                if (23 - wy) % 8 == p:
                    q = (23 - wy) // 8
                    w_ref[(dy * 2 + 1) * 128 + yw * 16 : (dy * 2 + 1) * 128 + yw * 16 + 16, at] = hp[:, 128 * q : 128 * q + 128]
        return carry

    lax.fori_loop(0, 2 * KERN, one, 0)


def taps_rows(kernels):
    k = kernels.astype(F32).reshape(2, KERN, KS, KS).swapaxes(0, 1).reshape(2 * KERN, KS, KS)
    k = k[:, ::-1, ::-1]
    k = jnp.pad(k, ((0, 0), (9, 32 - 9 - KS), (1, 0)))
    return k.reshape(2 * KERN, 1, 512)


def make_table(kernels):
    return pl.pallas_call(
        table_kernel,
        out_shape=jax.ShapeDtypeStruct((K, 2 * KERN * 128), BF),
        in_specs=[pl.BlockSpec(memory_space=pltpu.VMEM)],
        out_specs=pl.BlockSpec(memory_space=pltpu.VMEM),
        compiler_params=pltpu.CompilerParams(vmem_limit_bytes=32 * 1024 * 1024),
        cost_estimate=pl.CostEstimate(flops=20_000_000, bytes_accessed=10_000_000, transcendentals=0),
        name="taps_table",
    )(taps_rows(kernels))


def image_kernel(level_ref, shard_ref, wgt_ref, m0_ref, m1_ref, m2_ref, m3_ref, tabove_ref, tmid_ref, tbelow_ref, w_ref,
                 resist_ref, grad_ref, lhs_ref, fields_ref, cot_ref):
    level_at = level_ref[0]
    x = (m0_ref[...] + m1_ref[...] + m2_ref[...] + m3_ref[...]).astype(BF).astype(F32)
    x = pltpu.roll(x, 8 * MROWB - 1, 0)
    x = jnp.concatenate([x, jnp.zeros((8 * MROWB, 128), F32)], axis=1)
    x = pltpu.roll(x, H, 1)
    mb = to_blocks(x).reshape(MROWB, 72, 128)
    for dy in range(3):
        for dx in range(2):
            part = mb[dy : dy + ROWB, dx : dx + COLB, :]
            lhs_ref[:, (dy * 2 + dx) * 128 : (dy * 2 + dx) * 128 + 128] = part.reshape(M, 128).astype(BF)
    intensity = jnp.zeros((M, 128), F32)
    for c in range(KERN):
        f = jnp.dot(lhs_ref[...], w_ref[:, c * 256 : c * 256 + 256], preferred_element_type=F32)
        fields_ref[c] = f
        f = f * f
        intensity = intensity + wgt_ref[level_at, c] * (f[:, :128] + f[:, 128:])
    level = 1.0 / (1.0 + jnp.exp(-STEEP * (intensity - THRESH)))
    resist_ref[...] = from_blocks(level, ROWB, 8)[8 : 8 + TR].astype(BF)
    goal = jnp.concatenate([tabove_ref[...].astype(F32)[8:], tmid_ref[...].astype(F32), tbelow_ref[...].astype(F32)[:8]], axis=0)
    goal = to_blocks(goal)
    slope = STEEP * (level - goal) * level * (1.0 - level)
    row_block = lax.broadcasted_iota(jnp.int32, (M, 128), 0) // COLB
    in_block = lax.broadcasted_iota(jnp.int32, (M, 128), 1) // BC
    at = shard_ref[0] * TR - 8 + row_block * 8 + in_block
    slope = jnp.where((at >= 0) & (at < 8 * TR), slope, 0.0)
    for c in range(KERN):
        s = 2.0 * wgt_ref[level_at, c] * slope
        cot_ref[:, c * 256 : c * 256 + 256] = (jnp.concatenate([s, s], axis=1) * fields_ref[c]).astype(BF)
    out = [None] * 7
    for dy in range(3):
        acc = lax.dot_general(cot_ref[...], w_ref[dy * 256 : dy * 256 + 256, :], (((1,), (1,)), ((), ())), preferred_element_type=F32)
        for dx in range(2):
            for i in range(ROWB):
                j = i + dy
                if 1 <= j <= 7:
                    piece = acc[i * COLB : i * COLB + COLB, dx * 128 : dx * 128 + 128]
                    piece = jnp.concatenate([piece, jnp.zeros((8, 128), F32)], axis=0)
                    if dx:
                        piece = pltpu.roll(piece, 1, 0)
                    out[j - 1] = piece if out[j - 1] is None else out[j - 1] + piece
    nat = from_blocks(jnp.concatenate(out, axis=0), 7, 9)
    nat = pltpu.roll(nat, 9 * 128 - H, 1)
    grad_ref[...] = nat[H : H + TR, :TC].astype(grad_ref.dtype)


def image(level, shard, weights, parts, tabove, tmid, tbelow, table):
    vm = pl.BlockSpec(memory_space=pltpu.VMEM)
    sm = pl.BlockSpec(memory_space=pltpu.SMEM)
    return pl.pallas_call(
        image_kernel,
        out_shape=(jax.ShapeDtypeStruct((TR, TC), BF), jax.ShapeDtypeStruct((TR, TC), BF)),
        in_specs=[sm] * 3 + [vm] * 8,
        out_specs=(vm, vm),
        scratch_shapes=[pltpu.VMEM((M, K), BF), pltpu.VMEM((KERN, M, 256), F32), pltpu.VMEM((M, 2 * KERN * 128), BF)],
        compiler_params=pltpu.CompilerParams(vmem_limit_bytes=28 * 1024 * 1024),
        cost_estimate=pl.CostEstimate(flops=5_000_000_000, bytes_accessed=8_000_000, transcendentals=65536),
        name="image",
    )(level, shard, weights, *parts, tabove, tmid, tbelow, table)


NX, NC, NY, NZ = 4, 2, 4, 8
WIDE = TC + 128
LEAD = 16
EXT = TR + 2 * LEAD
INFO = 64
PLACE_GRANT = 58


def place_kernel(shard_ref, ids_hbm, rows_hbm, cols_hbm, masters_hbm, mine_ref, theirs_ref, info_ref, scalars, panels, canvas, sem, info_sem):
    shard = shard_ref[0]
    loads = [pltpu.make_async_copy(ref.at[shard], scalars.at[j], info_sem.at[j]) for j, ref in enumerate((ids_hbm, rows_hbm, cols_hbm))]
    for cp in loads:
        cp.start()
    for cp in loads:
        cp.wait()
    copies = []
    for i in range(INST_DEV):
        cp = pltpu.make_async_copy(masters_hbm.at[scalars[0, 0, i]], panels.at[i], sem.at[i])
        cp.start()
        copies.append(cp)
        for j in range(3):
            info_ref[0, j * INST_DEV + i] = scalars[j, 0, i]
    for i in range(3 * INST_DEV, INFO):
        info_ref[0, i] = 0
    canvas[...] = jnp.zeros(canvas.shape, F32)
    lane = lax.broadcasted_iota(jnp.int32, (P_SIZE, 128), 1)
    for i in range(INST_DEV):
        copies[i].wait()
        p = panels[i].astype(BF).astype(F32)
        c = scalars[2, 0, i]
        c0 = (c // 128) * 128
        d = c - c0
        p = pltpu.roll(p, d, 1)
        left = jnp.where(lane >= d, p, 0.0)
        right = jnp.where(lane >= d, 0.0, p)
        full = jnp.concatenate([jnp.concatenate([left, right], axis=1), jnp.zeros((8, 256), F32)], axis=0)
        r = scalars[1, 0, i] + LEAD
        r0 = (r // 8) * 8
        full = pltpu.roll(full, r - r0, 0)
        at = (pl.ds(pl.multiple_of(r0, 8), P_SIZE + 8), pl.ds(pl.multiple_of(c0, 128), 256))
        canvas[at] = canvas[at] + full
    core = shard % NC
    for d in range(NX):
        x = (shard // NC + d) % NX
        mine_ref[d] = canvas[pl.ds(pl.multiple_of((x * NC + core) * TR, 8), EXT), :TC]
        theirs_ref[d] = canvas[pl.ds(pl.multiple_of((x * NC + 1 - core) * TR, 8), EXT), :TC]


def place(shard, ids, rows, cols, masters):
    vm = pl.BlockSpec(memory_space=pltpu.VMEM)
    sm = pl.BlockSpec(memory_space=pltpu.SMEM)
    hbm = pl.BlockSpec(memory_space=pltpu.HBM)
    bands = jax.ShapeDtypeStruct((NX, EXT, TC), F32)
    return pl.pallas_call(
        place_kernel,
        out_shape=(bands, bands, jax.ShapeDtypeStruct((1, INFO), jnp.int32)),
        in_specs=[sm] + [hbm] * 4,
        out_specs=(vm, vm, sm),
        scratch_shapes=[
            pltpu.SMEM((3, 1, INST_DEV), jnp.int32),
            pltpu.VMEM((INST_DEV, P_SIZE, P_SIZE), F32),
            pltpu.VMEM((LEAD + 8 * TR + LEAD, WIDE), F32),
            pltpu.SemaphoreType.DMA((INST_DEV,)),
            pltpu.SemaphoreType.DMA((3,)),
        ],
        compiler_params=pltpu.CompilerParams(vmem_limit_bytes=PLACE_GRANT * 1024 * 1024),
        cost_estimate=pl.CostEstimate(flops=1_000_000, bytes_accessed=12_000_000, transcendentals=0),
        name="place",
    )(shard, ids, rows, cols, masters)


def cut_kernel(shard_ref, region_ref, i0, i1, i2, i3, own_ref, up_ref, down_ref, far_ref, sum_ref, up_out, down_out, canvas, sums):
    x = shard_ref[0] // NC
    z, y = region_ref[0] // NY, region_ref[0] % NY
    sums[...] = jnp.zeros(sums.shape, F32)

    def lay(ref, n, at):
        for core in range(NC):
            row = ((x + n) % NX * NC + core) * TR
            canvas[at, pl.ds(pl.multiple_of(row, 8), TR), :TC] = ref[core, at].astype(F32)

    for k in range(NY):
        lay(own_ref, 0, k)
        lay(up_ref, 3, k)
        lay(down_ref, 1, k)
        lay(far_ref, 2, k)
    for k, info in enumerate((i0, i1, i2, i3)):

        def one(i, carry, k=k, info=info):
            m = info[0, i]

            @pl.when((m // 4) % NY == y)
            def _():
                r, c = info[0, INST_DEV + i], info[0, 2 * INST_DEV + i]
                r0, c0 = (r // 8) * 8, (c // 128) * 128
                full = canvas[k, pl.ds(pl.multiple_of(r0, 8), P_SIZE + 8), pl.ds(pl.multiple_of(c0, 128), 256)]
                full = pltpu.roll(full, P_SIZE + 8 - (r - r0), 0)[:P_SIZE]
                full = pltpu.roll(full, 256 - (c - c0), 1)[:, :128]
                slot = (m // 16 - z + NZ) % NZ
                sums[slot, m % 4] = sums[slot, m % 4] + full

            return carry

        lax.fori_loop(0, INST_DEV, one, 0)
    sum_ref[0] = sums[0]
    for j in range(4):
        sum_ref[1 + j] = sums[1 + 2 * j]
    up_out[:2] = sums[4, :2].astype(BF)
    up_out[2:] = sums[2].astype(BF)
    down_out[:2] = sums[4, 2:].astype(BF)
    down_out[2:] = sums[6].astype(BF)


def cut(shard, region, infos, bands):
    vm = pl.BlockSpec(memory_space=pltpu.VMEM)
    sm = pl.BlockSpec(memory_space=pltpu.SMEM)
    send = jax.ShapeDtypeStruct((6, P_SIZE, P_SIZE), BF)
    return pl.pallas_call(
        cut_kernel,
        out_shape=(jax.ShapeDtypeStruct((5, 4, P_SIZE, P_SIZE), F32), send, send),
        in_specs=[sm] * 6 + [vm] * 4,
        out_specs=(vm, vm, vm),
        scratch_shapes=[pltpu.VMEM((NY, 8 * TR + 8, WIDE), F32), pltpu.VMEM((NZ, 4, P_SIZE, P_SIZE), F32)],
        compiler_params=pltpu.CompilerParams(vmem_limit_bytes=40 * 1024 * 1024),
        cost_estimate=pl.CostEstimate(flops=1_000_000, bytes_accessed=12_000_000, transcendentals=0),
        name="cut",
    )(shard, region, *infos, *bands)


def deposit_kernel(places, n_in, region_ref, *refs):
    blocks, (out_ref, wide, sem) = refs[: len(places)], refs[n_in:]
    z, y = region_ref[0] // NY, region_ref[0] % NY
    copies = []
    for n, (dz, ys) in enumerate(places):
        wide[n] = blocks[n][...].astype(F32)
        for j, k in enumerate(ys):
            cp = pltpu.make_async_copy(wide.at[n, pl.ds(4 * j, 4)], out_ref.at[(z + dz + NZ) % NZ, (y - k + NY) % NY], sem.at[n, j])
            cp.start()
            copies.append(cp)
    for cp in copies:
        cp.wait()


def deposit(region, out, items):
    places = [item[1:] for item in items]
    blocks = [item[0] for item in items]
    n = len(items)
    hbm = pl.BlockSpec(memory_space=pltpu.HBM)
    old = [] if out is None else [out]
    return pl.pallas_call(
        functools.partial(deposit_kernel, places, n + len(old)),
        out_shape=jax.ShapeDtypeStruct((NZ, NY, 4, P_SIZE, P_SIZE), F32),
        in_specs=[pl.BlockSpec(memory_space=pltpu.SMEM)] + [pl.BlockSpec(memory_space=pltpu.VMEM)] * n + [hbm] * len(old),
        out_specs=hbm,
        input_output_aliases={n + 1: 0} if old else {},
        scratch_shapes=[pltpu.VMEM((n, 8, P_SIZE, P_SIZE), F32), pltpu.SemaphoreType.DMA((n, 2))],
        compiler_params=pltpu.CompilerParams(vmem_limit_bytes=16 * 1024 * 1024),
        cost_estimate=pl.CostEstimate(flops=500_000 * n, bytes_accessed=800_000 * n, transcendentals=0),
        name="deposit",
    )(region, *blocks, *old)


def shift(v, axis, by):
    n = lax.axis_size(axis)
    return lax.ppermute(v, axis, [(i, (i + by) % n) for i in range(n)])


def halo(v, axis, width):
    n = lax.axis_size(axis)
    above = lax.ppermute(v[-width:], axis, [(i, i + 1) for i in range(n - 1)])
    below = lax.ppermute(v[:width], axis, [(i + 1, i) for i in range(n - 1)])
    return above, below


def sum_along_z(slots, up, down):
    up, down = shift(up, "z", 1).astype(F32), shift(down, "z", -1).astype(F32)
    one = slots[1] + up[2:]
    three = jnp.concatenate([slots[2, :2] + up[:2], slots[2, 2:]])
    five = jnp.concatenate([slots[3, :2], slots[3, 2:] + down[:2]])
    seven = slots[4] + down[2:]
    total = slots[0]
    for v, by in ((three, 3), (five, -3), (one, 1), (seven, -1)):
        total = total + shift(v.astype(BF), "z", by).astype(F32)
    return total


def spread(part, region):
    before, after, across = shift(part, "y", 1), shift(part, "y", 3), shift(part, "y", 2)
    chunks = (jnp.concatenate([part, before]), jnp.concatenate([after, across]))
    backs = ((0, 1), (3, 2))
    out = deposit(region, None, [(chunks[h], 0, backs[h]) for h in range(2)])
    ups, downs = list(chunks), list(chunks)
    got = []
    for d in (1, 2, 3, 4):
        if d > 1:
            ups[0], downs[0], out = lax.optimization_barrier((ups[0], downs[0], out))
        came, got = got, []
        for h in range(2):
            if d < 4 or h == 0:
                ups[h] = shift(ups[h], "z", 1)
                got.append((ups[h], -d, backs[h]))
            if d < 4 or h == 1:
                downs[h] = shift(downs[h], "z", -1)
                got.append((downs[h], d, backs[h]))
        if came:
            out = deposit(region, out, came)
    out = deposit(region, out, got)
    return out.reshape(MAS_DEV, P_SIZE, P_SIZE)


def body(masters, inst_master, inst_row, inst_col, def_index, def_weights, kernels, target):
    shard = lax.axis_index(("x", "core")).reshape(1)
    region = lax.axis_index(("z", "y")).reshape(1)
    mine, theirs, info = place(shard, inst_master, inst_row, inst_col, masters)
    other = shift(theirs, "core", 1)
    sums = [mine[d] + other[d] for d in range(NX)]
    parts = [sums[0]] + [shift(sums[d], "x", d) for d in (2, 1, 3)]
    tmid = target[0]
    tabove, tbelow = halo(tmid, ("x", "core"), 16)
    infos = [info] + [shift(info, "y", k) for k in (1, 2, 3)]
    table = make_table(kernels)
    parts[0], tmid, infos = lax.optimization_barrier((parts[0], tmid, infos))
    resist, grad = image(def_index, shard, def_weights, parts, tabove, tmid, tbelow, table)
    own = jnp.stack([grad] + [shift(grad, "y", k) for k in (1, 2, 3)])
    up, down = shift(own, "x", 1), shift(own, "x", -1)
    far = jnp.concatenate([shift(up[:2], "x", 1), shift(down[2:], "x", -1)])
    bands = [lax.all_gather(v, "core") for v in (own, up, down, far)]
    part = sum_along_z(*cut(shard, region, infos, bands)).astype(BF)
    return (spread(part, region), resist[None])


def solution(mesh):
    fine = Mesh(mesh.devices.reshape(NX, NC, NZ, NY), ("x", "core", "z", "y"))
    master, region = ("x", "core"), ("z", "y")
    return jax.shard_map(
        body,
        mesh=fine,
        in_specs=(
            P(master, None, None),
            P(None, region, None),
            P(None, region, None),
            P(None, region, None),
            P(region),
            P(),
            P(),
            P(region, master, None),
        ),
        out_specs=(P(master, None, None), P(region, master, None)),
        check_vma=False,
    )
```

```python
import functools
import jax, jax.numpy as jnp
from jax import lax
from jax.experimental import pallas as pl
from jax.sharding import Mesh, PartitionSpec as P
from jax.experimental.pallas import tpu as pltpu

TC = 1024; TR = 48; KS = 15; KERN = 12; P_SIZE = 128; MAS_DEV = 128; INST_DEV = 16
STEEP = 1.5; THRESH = 3.0
BR, BC = 8, 16
H = 7
ROWB = 8
MROWB = ROWB + 2
COLB = TC // BC
M = ROWB * COLB
K = 6 * 128
F32, BF = jnp.float32, jnp.bfloat16


def swap_chunks(x):
    n = x.shape[0]
    row = lax.broadcasted_iota(jnp.int32, (n, 128), 0)
    chunk = lax.broadcasted_iota(jnp.int32, (n, 128), 1) // BC

    def sub(v, k):
        return pltpu.roll(v.reshape(n // 8, 8, 128), k, 1).reshape(n, 128)

    for k in (1, 2, 4):
        rbit = (row & k) != 0
        cbit = (chunk & k) != 0
        up = sub(pltpu.roll(x, 128 - BC * k, 1), k)
        if k == 4:
            dn = up
        else:
            dn = sub(pltpu.roll(x, BC * k, 1), 8 - k)
        x = jnp.where(rbit == cbit, x, jnp.where(rbit, up, dn))
    return x


def to_blocks(x):
    a, b = x.shape[0] // 8, x.shape[1] // 128
    tiles = [x[8 * i : 8 * i + 8, 128 * t : 128 * t + 128] for i in range(a) for t in range(b)]
    return swap_chunks(jnp.concatenate(tiles, axis=0))


def from_blocks(v, a, b):
    x = swap_chunks(v)
    rows = []
    for i in range(a):
        rows.append(jnp.concatenate([x[(i * b + t) * 8 : (i * b + t) * 8 + 8] for t in range(b)], axis=1))
    return jnp.concatenate(rows, axis=0)


def table_kernel(v_ref, w_ref):
    lane = lax.broadcasted_iota(jnp.int32, (16, 512), 1) % BC
    row = lax.broadcasted_iota(jnp.int32, (16, 512), 0)
    low = lane <= row

    def one(c, carry):
        at = pl.ds(pl.multiple_of(c * 128, 128), 128)
        x = jnp.broadcast_to(v_ref[c], (16, 512))
        r = pltpu.roll(x, 1, 1, stride=1, stride_axis=0)
        lo = jnp.where(low, r, 0.0)
        hi = jnp.where(low, 0.0, r)
        for p in range(8):
            lp = (pltpu.roll(lo, 512 - 16 * p, 1) if p else lo).astype(BF)
            hp = (pltpu.roll(hi, 512 - 16 * p, 1) if p else hi).astype(BF)
            for wy in range(24):
                dy, yw = wy // 8, wy % 8
                if (24 - wy) % 8 == p:
                    q = (24 - wy) // 8
                    w_ref[(dy * 2) * 128 + yw * 16 : (dy * 2) * 128 + yw * 16 + 16, at] = lp[:, 128 * q : 128 * q + 128]
                if (23 - wy) % 8 == p:
                    q = (23 - wy) // 8
                    w_ref[(dy * 2 + 1) * 128 + yw * 16 : (dy * 2 + 1) * 128 + yw * 16 + 16, at] = hp[:, 128 * q : 128 * q + 128]
        return carry

    lax.fori_loop(0, 2 * KERN, one, 0)


def taps_rows(kernels):
    k = kernels.astype(F32).reshape(2, KERN, KS, KS).swapaxes(0, 1).reshape(2 * KERN, KS, KS)
    k = k[:, ::-1, ::-1]
    k = jnp.pad(k, ((0, 0), (9, 32 - 9 - KS), (1, 0)))
    return k.reshape(2 * KERN, 1, 512)


def make_table(kernels):
    return pl.pallas_call(
        table_kernel,
        out_shape=jax.ShapeDtypeStruct((K, 2 * KERN * 128), BF),
        in_specs=[pl.BlockSpec(memory_space=pltpu.VMEM)],
        out_specs=pl.BlockSpec(memory_space=pltpu.VMEM),
        compiler_params=pltpu.CompilerParams(vmem_limit_bytes=32 * 1024 * 1024),
        cost_estimate=pl.CostEstimate(flops=20_000_000, bytes_accessed=10_000_000, transcendentals=0),
        name="taps_table",
    )(taps_rows(kernels))


def image_kernel(level_ref, shard_ref, wgt_ref, m0_ref, m1_ref, m2_ref, m3_ref, tabove_ref, tmid_ref, tbelow_ref, info_ref, w_ref,
                 resist_ref, grad_ref, lhs_ref, fields_ref, cot_ref):
    level_at = level_ref[0]
    x = (m0_ref[...] + m1_ref[...] + m2_ref[...] + m3_ref[...]).astype(BF).astype(F32)
    x = pltpu.roll(x, 8 * MROWB - 1, 0)
    x = jnp.concatenate([x, jnp.zeros((8 * MROWB, 128), F32)], axis=1)
    x = pltpu.roll(x, H, 1)
    mb = to_blocks(x).reshape(MROWB, 72, 128)
    for dy in range(3):
        for dx in range(2):
            part = mb[dy : dy + ROWB, dx : dx + COLB, :]
            lhs_ref[:, (dy * 2 + dx) * 128 : (dy * 2 + dx) * 128 + 128] = part.reshape(M, 128).astype(BF)
    intensity = jnp.zeros((M, 128), F32)
    for c in range(KERN):
        f = jnp.dot(lhs_ref[...], w_ref[:, c * 256 : c * 256 + 256], preferred_element_type=F32)
        fields_ref[c] = f
        f = f * f
        intensity = intensity + wgt_ref[level_at, c] * (f[:, :128] + f[:, 128:])
    level = 1.0 / (1.0 + jnp.exp(-STEEP * (intensity - THRESH)))
    resist_ref[...] = from_blocks(level, ROWB, 8)[8 : 8 + TR].astype(BF)
    goal = jnp.concatenate([tabove_ref[...].astype(F32)[8:], tmid_ref[...].astype(F32), tbelow_ref[...].astype(F32)[:8]], axis=0)
    goal = to_blocks(goal)
    slope = STEEP * (level - goal) * level * (1.0 - level)
    row_block = lax.broadcasted_iota(jnp.int32, (M, 128), 0) // COLB
    in_block = lax.broadcasted_iota(jnp.int32, (M, 128), 1) // BC
    at = shard_ref[0] * TR - 8 + row_block * 8 + in_block
    slope = jnp.where((at >= 0) & (at < 8 * TR), slope, 0.0)
    for c in range(KERN):
        s = 2.0 * wgt_ref[level_at, c] * slope
        cot_ref[:, c * 256 : c * 256 + 256] = (jnp.concatenate([s, s], axis=1) * fields_ref[c]).astype(BF)
    out = [None] * 7
    for dy in range(3):
        acc = lax.dot_general(cot_ref[...], w_ref[dy * 256 : dy * 256 + 256, :], (((1,), (1,)), ((), ())), preferred_element_type=F32)
        for dx in range(2):
            for i in range(ROWB):
                j = i + dy
                if 1 <= j <= 7:
                    piece = acc[i * COLB : i * COLB + COLB, dx * 128 : dx * 128 + 128]
                    piece = jnp.concatenate([piece, jnp.zeros((8, 128), F32)], axis=0)
                    if dx:
                        piece = pltpu.roll(piece, 1, 0)
                    out[j - 1] = piece if out[j - 1] is None else out[j - 1] + piece
    nat = from_blocks(jnp.concatenate(out, axis=0), 7, 9)
    nat = pltpu.roll(nat, 9 * 128 - H, 1)
    grad_ref[:TR] = nat[H : H + TR, :TC].astype(BF)
    info = jnp.broadcast_to(info_ref[...], (16, 128))
    row = lax.broadcasted_iota(jnp.int32, (16, 128), 0)
    digits = jnp.where(row == 0, info >> 7, jnp.where(row == 1, info & 127, 0)).astype(F32)
    grad_ref[TR:] = jnp.concatenate([digits, jnp.zeros((16, TC - 128), F32)], axis=1).astype(BF)


def image(level, shard, weights, parts, tabove, tmid, tbelow, info, table):
    vm = pl.BlockSpec(memory_space=pltpu.VMEM)
    sm = pl.BlockSpec(memory_space=pltpu.SMEM)
    return pl.pallas_call(
        image_kernel,
        out_shape=(jax.ShapeDtypeStruct((TR, TC), BF), jax.ShapeDtypeStruct((TR + 16, TC), BF)),
        in_specs=[sm] * 3 + [vm] * 9,
        out_specs=(vm, vm),
        scratch_shapes=[pltpu.VMEM((M, K), BF), pltpu.VMEM((KERN, M, 256), F32), pltpu.VMEM((M, 2 * KERN * 128), BF)],
        compiler_params=pltpu.CompilerParams(vmem_limit_bytes=28 * 1024 * 1024),
        cost_estimate=pl.CostEstimate(flops=5_000_000_000, bytes_accessed=8_000_000, transcendentals=65536),
        name="image",
    )(level, shard, weights, *parts, tabove, tmid, tbelow, info, table)


NX, NC, NY, NZ = 4, 2, 4, 8
WIDE = TC + 128
LEAD = 16
EXT = TR + 2 * LEAD
INFO = 128
PLACE_GRANT = 58


def place_kernel(shard_ref, ids_hbm, rows_hbm, cols_hbm, masters_hbm, mine_ref, theirs_ref, info_ref, scalars, panels, canvas, sem, info_sem):
    shard = shard_ref[0]
    loads = [pltpu.make_async_copy(ref.at[shard], scalars.at[j], info_sem.at[j]) for j, ref in enumerate((ids_hbm, rows_hbm, cols_hbm))]
    for cp in loads:
        cp.start()
    for cp in loads:
        cp.wait()
    copies = []
    for i in range(INST_DEV):
        cp = pltpu.make_async_copy(masters_hbm.at[scalars[0, 0, i]], panels.at[i], sem.at[i])
        cp.start()
        copies.append(cp)
        for j in range(3):
            info_ref[0, j * INST_DEV + i] = scalars[j, 0, i]
    for i in range(3 * INST_DEV, INFO):
        info_ref[0, i] = 0
    canvas[...] = jnp.zeros(canvas.shape, F32)
    lane = lax.broadcasted_iota(jnp.int32, (P_SIZE, 128), 1)
    for i in range(INST_DEV):
        copies[i].wait()
        p = panels[i].astype(BF).astype(F32)
        c = scalars[2, 0, i]
        c0 = (c // 128) * 128
        d = c - c0
        p = pltpu.roll(p, d, 1)
        left = jnp.where(lane >= d, p, 0.0)
        right = jnp.where(lane >= d, 0.0, p)
        full = jnp.concatenate([jnp.concatenate([left, right], axis=1), jnp.zeros((8, 256), F32)], axis=0)
        r = scalars[1, 0, i] + LEAD
        r0 = (r // 8) * 8
        full = pltpu.roll(full, r - r0, 0)
        at = (pl.ds(pl.multiple_of(r0, 8), P_SIZE + 8), pl.ds(pl.multiple_of(c0, 128), 256))
        canvas[at] = canvas[at] + full
    core = shard % NC
    for d in range(NX):
        x = (shard // NC + d) % NX
        mine_ref[d] = canvas[pl.ds(pl.multiple_of((x * NC + core) * TR, 8), EXT), :TC]
        theirs_ref[d] = canvas[pl.ds(pl.multiple_of((x * NC + 1 - core) * TR, 8), EXT), :TC]


def place(shard, ids, rows, cols, masters):
    vm = pl.BlockSpec(memory_space=pltpu.VMEM)
    sm = pl.BlockSpec(memory_space=pltpu.SMEM)
    hbm = pl.BlockSpec(memory_space=pltpu.HBM)
    bands = jax.ShapeDtypeStruct((NX, EXT, TC), F32)
    return pl.pallas_call(
        place_kernel,
        out_shape=(bands, bands, jax.ShapeDtypeStruct((1, INFO), jnp.int32)),
        in_specs=[sm] + [hbm] * 4,
        out_specs=(vm, vm, sm),
        scratch_shapes=[
            pltpu.SMEM((3, 1, INST_DEV), jnp.int32),
            pltpu.VMEM((INST_DEV, P_SIZE, P_SIZE), F32),
            pltpu.VMEM((LEAD + 8 * TR + LEAD, WIDE), F32),
            pltpu.SemaphoreType.DMA((INST_DEV,)),
            pltpu.SemaphoreType.DMA((3,)),
        ],
        compiler_params=pltpu.CompilerParams(vmem_limit_bytes=PLACE_GRANT * 1024 * 1024),
        cost_estimate=pl.CostEstimate(flops=1_000_000, bytes_accessed=12_000_000, transcendentals=0),
        name="place",
    )(shard, ids, rows, cols, masters)


def cut_kernel(shard_ref, region_ref, g0, g1, g2, g3, own_ref, up_ref, down_ref, far_ref, *rest):
    outs, (canvas, sums, digits, lists, list_sem) = rest[:NZ], rest[NZ:]
    digits[...] = jnp.zeros(digits.shape, jnp.int32)
    for k, g in enumerate((g0, g1, g2, g3)):
        tile = g[TR:, :128].astype(F32)
        digits[k : k + 1] = (tile[0:1] * 128.0 + tile[1:2]).astype(jnp.int32)
    load = pltpu.make_async_copy(digits, lists, list_sem)
    load.start()
    x = shard_ref[0] // NC
    z, y = region_ref[0] // NY, region_ref[0] % NY
    sums[...] = jnp.zeros(sums.shape, F32)

    def lay(ref, n, at):
        for core in range(NC):
            row = ((x + n) % NX * NC + core) * TR
            canvas[at, pl.ds(pl.multiple_of(row, 8), TR), :TC] = ref[core, at].astype(F32)

    for k in range(NY):
        lay(own_ref, 0, k)
        lay(up_ref, 3, k)
        lay(down_ref, 1, k)
        lay(far_ref, 2, k)
    load.wait()
    for k in range(NY):

        def one(i, carry, k=k):
            m = lists[k, i]

            @pl.when((m // 4) % NY == y)
            def _():
                r, c = lists[k, INST_DEV + i], lists[k, 2 * INST_DEV + i]
                r0, c0 = (r // 8) * 8, (c // 128) * 128
                full = canvas[k, pl.ds(pl.multiple_of(r0, 8), P_SIZE + 8), pl.ds(pl.multiple_of(c0, 128), 256)]
                full = pltpu.roll(full, P_SIZE + 8 - (r - r0), 0)[:P_SIZE]
                full = pltpu.roll(full, 256 - (c - c0), 1)[:, :128]
                slot = (m // 16 - z + NZ) % NZ
                sums[slot, m % 4] = sums[slot, m % 4] + full

            return carry

        lax.fori_loop(0, INST_DEV, one, 0)
    for d in range(NZ):
        outs[d][...] = sums[d].astype(outs[d].dtype)


def cut(shard, region, grads, bands):
    vm = pl.BlockSpec(memory_space=pltpu.VMEM)
    sm = pl.BlockSpec(memory_space=pltpu.SMEM)
    slot = (4, P_SIZE, P_SIZE)
    return pl.pallas_call(
        cut_kernel,
        out_shape=[jax.ShapeDtypeStruct(slot, F32)] + [jax.ShapeDtypeStruct(slot, BF)] * (NZ - 1),
        in_specs=[sm] * 2 + [vm] * 8,
        out_specs=[vm] * NZ,
        scratch_shapes=[
            pltpu.VMEM((NY, 8 * TR + 8, WIDE), F32),
            pltpu.VMEM((NZ, 4, P_SIZE, P_SIZE), F32),
            pltpu.VMEM((8, 128), jnp.int32),
            pltpu.SMEM((8, 128), jnp.int32),
            pltpu.SemaphoreType.DMA,
        ],
        compiler_params=pltpu.CompilerParams(vmem_limit_bytes=40 * 1024 * 1024),
        cost_estimate=pl.CostEstimate(flops=1_000_000, bytes_accessed=12_000_000, transcendentals=0),
        name="cut",
    )(shard, region, *grads, *bands)


def deposit_kernel(places, n_in, region_ref, *refs):
    blocks, (out_ref, wide, sem) = refs[: len(places)], refs[n_in:]
    z, y = region_ref[0] // NY, region_ref[0] % NY
    copies = []
    for n, (dz, ys) in enumerate(places):
        wide[n] = blocks[n][...].astype(F32)
        for j, k in enumerate(ys):
            cp = pltpu.make_async_copy(wide.at[n, pl.ds(4 * j, 4)], out_ref.at[(z + dz + NZ) % NZ, (y - k + NY) % NY], sem.at[n, j])
            cp.start()
            copies.append(cp)
    for cp in copies:
        cp.wait()


def deposit(region, out, items):
    places = [item[1:] for item in items]
    blocks = [item[0] for item in items]
    n = len(items)
    hbm = pl.BlockSpec(memory_space=pltpu.HBM)
    old = [] if out is None else [out]
    return pl.pallas_call(
        functools.partial(deposit_kernel, places, n + len(old)),
        out_shape=jax.ShapeDtypeStruct((NZ, NY, 4, P_SIZE, P_SIZE), F32),
        in_specs=[pl.BlockSpec(memory_space=pltpu.SMEM)] + [pl.BlockSpec(memory_space=pltpu.VMEM)] * n + [hbm] * len(old),
        out_specs=hbm,
        input_output_aliases={n + 1: 0} if old else {},
        scratch_shapes=[pltpu.VMEM((n, 8, P_SIZE, P_SIZE), F32), pltpu.SemaphoreType.DMA((n, 2))],
        compiler_params=pltpu.CompilerParams(vmem_limit_bytes=16 * 1024 * 1024),
        cost_estimate=pl.CostEstimate(flops=500_000 * n, bytes_accessed=800_000 * n, transcendentals=0),
        name="deposit",
    )(region, *blocks, *old)


def shift(v, axis, by):
    n = lax.axis_size(axis)
    return lax.ppermute(v, axis, [(i, (i + by) % n) for i in range(n)])


def halo(v, axis, width):
    n = lax.axis_size(axis)
    above = lax.ppermute(v[-width:], axis, [(i, i + 1) for i in range(n - 1)])
    below = lax.ppermute(v[:width], axis, [(i + 1, i) for i in range(n - 1)])
    return above, below


def sum_along_z(slots):
    total = slots[0]
    for d in (4, 3, 5, 2, 6, 1, 7):
        total = total + shift(slots[d], "z", d).astype(F32)
    return total


def spread(part, region):
    before, after, across = shift(part, "y", 1), shift(part, "y", 3), shift(part, "y", 2)
    chunks = (jnp.concatenate([part, before]), jnp.concatenate([after, across]))
    backs = ((0, 1), (3, 2))
    out = deposit(region, None, [(chunks[h], 0, backs[h]) for h in range(2)])
    ups, downs = list(chunks), list(chunks)
    got = []
    for d in (1, 2, 3, 4):
        if d > 1:
            ups[0], downs[0], out = lax.optimization_barrier((ups[0], downs[0], out))
        came, got = got, []
        for h in range(2):
            if d < 4 or h == 0:
                ups[h] = shift(ups[h], "z", 1)
                got.append((ups[h], -d, backs[h]))
            if d < 4 or h == 1:
                downs[h] = shift(downs[h], "z", -1)
                got.append((downs[h], d, backs[h]))
        if came:
            out = deposit(region, out, came)
    out = deposit(region, out, got)
    return out.reshape(MAS_DEV, P_SIZE, P_SIZE)


def body(masters, inst_master, inst_row, inst_col, def_index, def_weights, kernels, target):
    shard = lax.axis_index(("x", "core")).reshape(1)
    region = lax.axis_index(("z", "y")).reshape(1)
    mine, theirs, info = place(shard, inst_master, inst_row, inst_col, masters)
    other = shift(theirs, "core", 1)
    sums = [mine[d] + other[d] for d in range(NX)]
    parts = [sums[0]] + [shift(sums[d], "x", d) for d in (2, 1, 3)]
    tmid = target[0]
    tabove, tbelow = halo(tmid, ("x", "core"), 16)
    table = make_table(kernels)
    resist, grad = image(def_index, shard, def_weights, parts, tabove, tmid, tbelow, info, table)
    grads = [grad] + [shift(grad, "y", k) for k in (1, 2, 3)]
    own = jnp.stack([g[:TR] for g in grads])
    up, down, far = [shift(own, "x", by) for by in (1, 3, 2)]
    bands = [lax.all_gather(v, "core") for v in (own, up, down, far)]
    part = sum_along_z(cut(shard, region, grads, bands)).astype(BF)
    return (spread(part, region), resist[None])


def solution(mesh):
    fine = Mesh(mesh.devices.reshape(NX, NC, NZ, NY), ("x", "core", "z", "y"))
    master, region = ("x", "core"), ("z", "y")
    return jax.shard_map(
        body,
        mesh=fine,
        in_specs=(
            P(master, None, None),
            P(None, region, None),
            P(None, region, None),
            P(None, region, None),
            P(region),
            P(),
            P(),
            P(region, master, None),
        ),
        out_specs=(P(master, None, None), P(region, master, None)),
        check_vma=False,
    )
```

```python
import functools
import jax, jax.numpy as jnp
from jax import lax
from jax.experimental import pallas as pl
from jax.sharding import Mesh, PartitionSpec as P
from jax.experimental.pallas import tpu as pltpu

TC = 1024; TR = 48; KS = 15; KERN = 12; P_SIZE = 128; MAS_DEV = 128; INST_DEV = 16
STEEP = 1.5; THRESH = 3.0
BR, BC = 8, 16
H = 7
ROWB = 8
MROWB = ROWB + 2
COLB = TC // BC
M = ROWB * COLB
K = 6 * 128
F32, BF = jnp.float32, jnp.bfloat16


def swap_chunks(x):
    n = x.shape[0]
    row = lax.broadcasted_iota(jnp.int32, (n, 128), 0)
    chunk = lax.broadcasted_iota(jnp.int32, (n, 128), 1) // BC

    def sub(v, k):
        return pltpu.roll(v.reshape(n // 8, 8, 128), k, 1).reshape(n, 128)

    for k in (1, 2, 4):
        rbit = (row & k) != 0
        cbit = (chunk & k) != 0
        up = sub(pltpu.roll(x, 128 - BC * k, 1), k)
        if k == 4:
            dn = up
        else:
            dn = sub(pltpu.roll(x, BC * k, 1), 8 - k)
        x = jnp.where(rbit == cbit, x, jnp.where(rbit, up, dn))
    return x


def to_blocks(x):
    a, b = x.shape[0] // 8, x.shape[1] // 128
    tiles = [x[8 * i : 8 * i + 8, 128 * t : 128 * t + 128] for i in range(a) for t in range(b)]
    return swap_chunks(jnp.concatenate(tiles, axis=0))


def from_blocks(v, a, b):
    x = swap_chunks(v)
    rows = []
    for i in range(a):
        rows.append(jnp.concatenate([x[(i * b + t) * 8 : (i * b + t) * 8 + 8] for t in range(b)], axis=1))
    return jnp.concatenate(rows, axis=0)


def table_kernel(v_ref, w_ref):
    lane = lax.broadcasted_iota(jnp.int32, (16, 512), 1) % BC
    row = lax.broadcasted_iota(jnp.int32, (16, 512), 0)
    low = lane <= row

    def one(c, carry):
        at = pl.ds(pl.multiple_of(c * 128, 128), 128)
        x = jnp.broadcast_to(v_ref[c], (16, 512))
        r = pltpu.roll(x, 1, 1, stride=1, stride_axis=0)
        lo = jnp.where(low, r, 0.0)
        hi = jnp.where(low, 0.0, r)
        for p in range(8):
            lp = (pltpu.roll(lo, 512 - 16 * p, 1) if p else lo).astype(BF)
            hp = (pltpu.roll(hi, 512 - 16 * p, 1) if p else hi).astype(BF)
            for wy in range(24):
                dy, yw = wy // 8, wy % 8
                if (24 - wy) % 8 == p:
                    q = (24 - wy) // 8
                    w_ref[(dy * 2) * 128 + yw * 16 : (dy * 2) * 128 + yw * 16 + 16, at] = lp[:, 128 * q : 128 * q + 128]
                if (23 - wy) % 8 == p:
                    q = (23 - wy) // 8
                    w_ref[(dy * 2 + 1) * 128 + yw * 16 : (dy * 2 + 1) * 128 + yw * 16 + 16, at] = hp[:, 128 * q : 128 * q + 128]
        return carry

    lax.fori_loop(0, 2 * KERN, one, 0)


def taps_rows(kernels):
    k = kernels.astype(F32).reshape(2, KERN, KS, KS).swapaxes(0, 1).reshape(2 * KERN, KS, KS)
    k = k[:, ::-1, ::-1]
    k = jnp.pad(k, ((0, 0), (9, 32 - 9 - KS), (1, 0)))
    return k.reshape(2 * KERN, 1, 512)


def make_table(kernels):
    return pl.pallas_call(
        table_kernel,
        out_shape=jax.ShapeDtypeStruct((K, 2 * KERN * 128), BF),
        in_specs=[pl.BlockSpec(memory_space=pltpu.VMEM)],
        out_specs=pl.BlockSpec(memory_space=pltpu.VMEM),
        compiler_params=pltpu.CompilerParams(vmem_limit_bytes=32 * 1024 * 1024),
        cost_estimate=pl.CostEstimate(flops=20_000_000, bytes_accessed=10_000_000, transcendentals=0),
        name="taps_table",
    )(taps_rows(kernels))


def image_kernel(level_ref, shard_ref, wgt_ref, m0_ref, m1_ref, m2_ref, m3_ref, tabove_ref, tmid_ref, tbelow_ref, info_ref, w_ref,
                 resist_ref, grad_ref, lhs_ref, fields_ref, cot_ref):
    level_at = level_ref[0]
    x = m0_ref[...] + m1_ref[...].astype(F32) + m2_ref[...].astype(F32) + m3_ref[...].astype(F32)
    x = x.astype(BF).astype(F32)
    x = pltpu.roll(x, 8 * MROWB - 1, 0)
    x = jnp.concatenate([x, jnp.zeros((8 * MROWB, 128), F32)], axis=1)
    x = pltpu.roll(x, H, 1)
    mb = to_blocks(x).reshape(MROWB, 72, 128)
    for dy in range(3):
        for dx in range(2):
            part = mb[dy : dy + ROWB, dx : dx + COLB, :]
            lhs_ref[:, (dy * 2 + dx) * 128 : (dy * 2 + dx) * 128 + 128] = part.reshape(M, 128).astype(BF)
    intensity = jnp.zeros((M, 128), F32)
    for c in range(KERN):
        f = jnp.dot(lhs_ref[...], w_ref[:, c * 256 : c * 256 + 256], preferred_element_type=F32)
        fields_ref[c] = f
        f = f * f
        intensity = intensity + wgt_ref[level_at, c] * (f[:, :128] + f[:, 128:])
    level = 1.0 / (1.0 + jnp.exp(-STEEP * (intensity - THRESH)))
    resist_ref[...] = from_blocks(level, ROWB, 8)[8 : 8 + TR].astype(BF)
    goal = jnp.concatenate([tabove_ref[...].astype(F32)[8:], tmid_ref[...].astype(F32), tbelow_ref[...].astype(F32)[:8]], axis=0)
    goal = to_blocks(goal)
    slope = STEEP * (level - goal) * level * (1.0 - level)
    row_block = lax.broadcasted_iota(jnp.int32, (M, 128), 0) // COLB
    in_block = lax.broadcasted_iota(jnp.int32, (M, 128), 1) // BC
    at = shard_ref[0] * TR - 8 + row_block * 8 + in_block
    slope = jnp.where((at >= 0) & (at < 8 * TR), slope, 0.0)
    for c in range(KERN):
        s = 2.0 * wgt_ref[level_at, c] * slope
        cot_ref[:, c * 256 : c * 256 + 256] = (jnp.concatenate([s, s], axis=1) * fields_ref[c]).astype(BF)
    out = [None] * 7
    for dy in range(3):
        acc = lax.dot_general(cot_ref[...], w_ref[dy * 256 : dy * 256 + 256, :], (((1,), (1,)), ((), ())), preferred_element_type=F32)
        for dx in range(2):
            for i in range(ROWB):
                j = i + dy
                if 1 <= j <= 7:
                    piece = acc[i * COLB : i * COLB + COLB, dx * 128 : dx * 128 + 128]
                    piece = jnp.concatenate([piece, jnp.zeros((8, 128), F32)], axis=0)
                    if dx:
                        piece = pltpu.roll(piece, 1, 0)
                    out[j - 1] = piece if out[j - 1] is None else out[j - 1] + piece
    nat = from_blocks(jnp.concatenate(out, axis=0), 7, 9)
    nat = pltpu.roll(nat, 9 * 128 - H, 1)
    grad_ref[:TR] = nat[H : H + TR, :TC].astype(BF)
    info = jnp.broadcast_to(info_ref[...], (16, 128))
    row = lax.broadcasted_iota(jnp.int32, (16, 128), 0)
    digits = jnp.where(row == 0, info >> 7, jnp.where(row == 1, info & 127, 0)).astype(F32)
    grad_ref[TR:] = jnp.concatenate([digits, jnp.zeros((16, TC - 128), F32)], axis=1).astype(BF)


def image(level, shard, weights, parts, tabove, tmid, tbelow, info, table):
    vm = pl.BlockSpec(memory_space=pltpu.VMEM)
    sm = pl.BlockSpec(memory_space=pltpu.SMEM)
    return pl.pallas_call(
        image_kernel,
        out_shape=(jax.ShapeDtypeStruct((TR, TC), BF), jax.ShapeDtypeStruct((TR + 16, TC), BF)),
        in_specs=[sm] * 3 + [vm] * 9,
        out_specs=(vm, vm),
        scratch_shapes=[pltpu.VMEM((M, K), BF), pltpu.VMEM((KERN, M, 256), F32), pltpu.VMEM((M, 2 * KERN * 128), BF)],
        compiler_params=pltpu.CompilerParams(vmem_limit_bytes=28 * 1024 * 1024),
        cost_estimate=pl.CostEstimate(flops=5_000_000_000, bytes_accessed=8_000_000, transcendentals=65536),
        name="image",
    )(level, shard, weights, *parts, tabove, tmid, tbelow, info, table)


NX, NC, NY, NZ = 4, 2, 4, 8
WIDE = TC + 128
LEAD = 16
EXT = TR + 2 * LEAD
INFO = 128
PLACE_GRANT = 56


def place_kernel(shard_ref, ids_hbm, rows_hbm, cols_hbm, masters_hbm, mine_ref, theirs_ref, info_ref, scalars, panels, canvas, sem, info_sem):
    shard = shard_ref[0]
    loads = [pltpu.make_async_copy(ref.at[shard], scalars.at[j], info_sem.at[j]) for j, ref in enumerate((ids_hbm, rows_hbm, cols_hbm))]
    for cp in loads:
        cp.start()
    for cp in loads:
        cp.wait()
    copies = []
    for i in range(INST_DEV):
        cp = pltpu.make_async_copy(masters_hbm.at[scalars[0, 0, i]], panels.at[i], sem.at[i])
        cp.start()
        copies.append(cp)
        for j in range(3):
            info_ref[0, j * INST_DEV + i] = scalars[j, 0, i]
    for i in range(3 * INST_DEV, INFO):
        info_ref[0, i] = 0
    canvas[...] = jnp.zeros(canvas.shape, F32)
    lane = lax.broadcasted_iota(jnp.int32, (P_SIZE, 128), 1)
    sub = lax.broadcasted_iota(jnp.int32, (P_SIZE // 8 + 1, 8, 256), 1)
    none = jnp.zeros((1, 8, 256), F32)
    for i in range(INST_DEV):
        copies[i].wait()
        p = panels[i].astype(BF).astype(F32)
        c = scalars[2, 0, i]
        c0 = (c // 128) * 128
        d = c - c0
        p = pltpu.roll(p, d, 1)
        left = jnp.where(lane >= d, p, 0.0)
        right = jnp.where(lane >= d, 0.0, p)
        r = scalars[1, 0, i] + LEAD
        r0 = (r // 8) * 8
        full = jnp.concatenate([left, right], axis=1).reshape(P_SIZE // 8, 8, 256)
        full = pltpu.roll(full, r - r0, 1)
        full = jnp.where(sub >= r - r0, jnp.concatenate([full, none], axis=0), jnp.concatenate([none, full], axis=0))
        full = full.reshape(P_SIZE + 8, 256)
        at = (pl.ds(pl.multiple_of(r0, 8), P_SIZE + 8), pl.ds(pl.multiple_of(c0, 128), 256))
        canvas[at] = canvas[at] + full
    core = shard % NC
    for d in range(NX):
        x = (shard // NC + d) % NX
        mine_ref[d] = canvas[pl.ds(pl.multiple_of((x * NC + core) * TR, 8), EXT), :TC]
        theirs_ref[d] = canvas[pl.ds(pl.multiple_of((x * NC + 1 - core) * TR, 8), EXT), :TC].astype(BF)


def place(shard, ids, rows, cols, masters):
    vm = pl.BlockSpec(memory_space=pltpu.VMEM)
    sm = pl.BlockSpec(memory_space=pltpu.SMEM)
    hbm = pl.BlockSpec(memory_space=pltpu.HBM)
    bands = (NX, EXT, TC)
    return pl.pallas_call(
        place_kernel,
        out_shape=(jax.ShapeDtypeStruct(bands, F32), jax.ShapeDtypeStruct(bands, BF), jax.ShapeDtypeStruct((1, INFO), jnp.int32)),
        in_specs=[sm] + [hbm] * 4,
        out_specs=(vm, vm, sm),
        scratch_shapes=[
            pltpu.SMEM((3, 1, INST_DEV), jnp.int32),
            pltpu.VMEM((INST_DEV, P_SIZE, P_SIZE), F32),
            pltpu.VMEM((LEAD + 8 * TR + LEAD, WIDE), F32),
            pltpu.SemaphoreType.DMA((INST_DEV,)),
            pltpu.SemaphoreType.DMA((3,)),
        ],
        compiler_params=pltpu.CompilerParams(vmem_limit_bytes=PLACE_GRANT * 1024 * 1024),
        cost_estimate=pl.CostEstimate(flops=1_000_000, bytes_accessed=12_000_000, transcendentals=0),
        name="place",
    )(shard, ids, rows, cols, masters)


def cut_kernel(shard_ref, region_ref, g0, g1, g2, g3, own_ref, up_ref, down_ref, far_ref, *rest):
    outs, (canvas, sums, digits, lists, list_sem) = rest[:NZ], rest[NZ:]
    digits[...] = jnp.zeros(digits.shape, jnp.int32)
    for k, g in enumerate((g0, g1, g2, g3)):
        tile = g[TR:, :128].astype(F32)
        digits[k : k + 1] = (tile[0:1] * 128.0 + tile[1:2]).astype(jnp.int32)
    load = pltpu.make_async_copy(digits, lists, list_sem)
    load.start()
    x = shard_ref[0] // NC
    z, y = region_ref[0] // NY, region_ref[0] % NY
    sums[...] = jnp.zeros(sums.shape, F32)

    def lay(ref, n, at):
        for core in range(NC):
            row = ((x + n) % NX * NC + core) * TR
            canvas[at, pl.ds(pl.multiple_of(row, 8), TR), :TC] = ref[core, at].astype(F32)

    for k in range(NY):
        lay(own_ref, 0, k)
        lay(up_ref, 3, k)
        lay(down_ref, 1, k)
        lay(far_ref, 2, k)
    load.wait()
    sub = lax.broadcasted_iota(jnp.int32, (P_SIZE // 8, 8, 128), 1)
    for k in range(NY):

        def one(i, carry, k=k):
            m = lists[k, i]

            @pl.when((m // 4) % NY == y)
            def _():
                r, c = lists[k, INST_DEV + i], lists[k, 2 * INST_DEV + i]
                r0, c0 = (r // 8) * 8, (c // 128) * 128
                full = canvas[k, pl.ds(pl.multiple_of(r0, 8), P_SIZE + 8), pl.ds(pl.multiple_of(c0, 128), 256)]
                full = pltpu.roll(full, 256 - (c - c0), 1)[:, :128]
                full = pltpu.roll(full.reshape(P_SIZE // 8 + 1, 8, 128), 8 - (r - r0), 1)
                full = jnp.where(sub < 8 - (r - r0), full[:-1], full[1:]).reshape(P_SIZE, 128)
                slot = (m // 16 - z + NZ) % NZ
                sums[slot, m % 4] = sums[slot, m % 4] + full

            return carry

        lax.fori_loop(0, INST_DEV, one, 0)
    for d in range(NZ):
        outs[d][...] = sums[d].astype(outs[d].dtype)


def cut(shard, region, grads, bands):
    vm = pl.BlockSpec(memory_space=pltpu.VMEM)
    sm = pl.BlockSpec(memory_space=pltpu.SMEM)
    slot = (4, P_SIZE, P_SIZE)
    return pl.pallas_call(
        cut_kernel,
        out_shape=[jax.ShapeDtypeStruct(slot, F32)] + [jax.ShapeDtypeStruct(slot, BF)] * (NZ - 1),
        in_specs=[sm] * 2 + [vm] * 8,
        out_specs=[vm] * NZ,
        scratch_shapes=[
            pltpu.VMEM((NY, 8 * TR + 8, WIDE), F32),
            pltpu.VMEM((NZ, 4, P_SIZE, P_SIZE), F32),
            pltpu.VMEM((8, 128), jnp.int32),
            pltpu.SMEM((8, 128), jnp.int32),
            pltpu.SemaphoreType.DMA,
        ],
        compiler_params=pltpu.CompilerParams(vmem_limit_bytes=40 * 1024 * 1024),
        cost_estimate=pl.CostEstimate(flops=1_000_000, bytes_accessed=12_000_000, transcendentals=0),
        name="cut",
    )(shard, region, *grads, *bands)


def deposit_kernel(places, n_in, region_ref, *refs):
    blocks, (out_ref, wide, sem) = refs[: len(places)], refs[n_in:]
    z, y = region_ref[0] // NY, region_ref[0] % NY
    copies = []
    for block, (dz, ys) in zip(blocks, places):
        for j, k in enumerate(ys):
            at = len(copies)
            wide[at] = block[4 * j : 4 * j + 4].astype(F32)
            cp = pltpu.make_async_copy(wide.at[at], out_ref.at[(z + dz + NZ) % NZ, (y - k + NY) % NY], sem.at[at])
            cp.start()
            copies.append(cp)
    for cp in copies:
        cp.wait()


def deposit(region, out, items):
    places = [item[1:] for item in items]
    blocks = [item[0] for item in items]
    n, total = len(items), sum(len(item[2]) for item in items)
    hbm = pl.BlockSpec(memory_space=pltpu.HBM)
    old = [] if out is None else [out]
    return pl.pallas_call(
        functools.partial(deposit_kernel, places, n + len(old)),
        out_shape=jax.ShapeDtypeStruct((NZ, NY, 4, P_SIZE, P_SIZE), F32),
        in_specs=[pl.BlockSpec(memory_space=pltpu.SMEM)] + [pl.BlockSpec(memory_space=pltpu.VMEM)] * n + [hbm] * len(old),
        out_specs=hbm,
        input_output_aliases={n + 1: 0} if old else {},
        scratch_shapes=[pltpu.VMEM((total, 4, P_SIZE, P_SIZE), F32), pltpu.SemaphoreType.DMA((total,))],
        compiler_params=pltpu.CompilerParams(vmem_limit_bytes=16 * 1024 * 1024),
        cost_estimate=pl.CostEstimate(flops=200_000 * total, bytes_accessed=400_000 * total, transcendentals=0),
        name="deposit",
    )(region, *blocks, *old)


def shift(v, axis, by):
    n = lax.axis_size(axis)
    return lax.ppermute(v, axis, [(i, (i + by) % n) for i in range(n)])


def halo(v, axis, width):
    n = lax.axis_size(axis)
    above = lax.ppermute(v[-width:], axis, [(i, i + 1) for i in range(n - 1)])
    below = lax.ppermute(v[:width], axis, [(i + 1, i) for i in range(n - 1)])
    return above, below


def sum_along_z(slots):
    total = slots[0]
    for d in (4, 3, 5, 2, 6, 1, 7):
        total = total + shift(slots[d], "z", d).astype(F32)
    return total


def spread(part, region):
    own = jnp.concatenate([part, shift(part, "y", 2)])
    ups, downs = shift(own, "z", 1), shift(own, "z", -1)
    came = [(shift(own, "y", 1), 0, (1, 3))]
    out = deposit(region, None, [(own, 0, (0, 2))])
    for d in (1, 2, 3):
        ups, downs, out = lax.optimization_barrier((ups, downs, out))
        here = [(ups, -d, (0, 2)), (downs, d, (0, 2))]
        if d < 3:
            ups, downs = shift(ups, "z", 1), shift(downs, "z", -1)
        else:
            ups, downs = shift(ups[:4], "z", 1), shift(downs[4:], "z", -1)
        side = [(shift(here[0][0], "y", 1), -d, (1, 3)), (shift(here[1][0], "y", -1), d, (3, 1))]
        out = deposit(region, out, here + came)
        came = side
    ups, downs, out = lax.optimization_barrier((ups, downs, out))
    side = [(shift(ups, "y", 1), -4, (1,)), (shift(ups, "y", -1), -4, (3,))]
    out = deposit(region, out, [(ups, -4, (0,)), (downs, -4, (2,))] + came)
    out = deposit(region, out, side)
    return out.reshape(MAS_DEV, P_SIZE, P_SIZE)


def body(masters, inst_master, inst_row, inst_col, def_index, def_weights, kernels, target):
    shard = lax.axis_index(("x", "core")).reshape(1)
    region = lax.axis_index(("z", "y")).reshape(1)
    mine, theirs, info = place(shard, inst_master, inst_row, inst_col, masters)
    other = shift(theirs, "core", 1)
    sums = [mine[d] + other[d].astype(F32) for d in range(NX)]
    parts = [sums[0]] + [shift(sums[d].astype(BF), "x", d) for d in (2, 1, 3)]
    tmid = target[0]
    tabove, tbelow = halo(tmid, ("x", "core"), 16)
    table = make_table(kernels)
    resist, grad = image(def_index, shard, def_weights, parts, tabove, tmid, tbelow, info, table)
    grads = [grad] + [shift(grad, "y", k) for k in (1, 2, 3)]
    own = jnp.stack([g[:TR] for g in grads])
    up, down, far = [shift(own, "x", by) for by in (1, 3, 2)]
    bands = [lax.all_gather(v, "core") for v in (own, up, down, far)]
    part = sum_along_z(cut(shard, region, grads, bands)).astype(BF)
    return (spread(part, region), resist[None])


def solution(mesh):
    fine = Mesh(mesh.devices.reshape(NX, NC, NZ, NY), ("x", "core", "z", "y"))
    master, region = ("x", "core"), ("z", "y")
    return jax.shard_map(
        body,
        mesh=fine,
        in_specs=(
            P(master, None, None),
            P(None, region, None),
            P(None, region, None),
            P(None, region, None),
            P(region),
            P(),
            P(),
            P(region, master, None),
        ),
        out_specs=(P(master, None, None), P(region, master, None)),
        check_vma=False,
    )
```

```python
import functools
import jax, jax.numpy as jnp
from jax import lax
from jax.experimental import pallas as pl
from jax.sharding import Mesh, PartitionSpec as P
from jax.experimental.pallas import tpu as pltpu

TC = 1024; TR = 48; KS = 15; KERN = 12; P_SIZE = 128; MAS_DEV = 128; INST_DEV = 16
STEEP = 1.5; THRESH = 3.0
BR, BC = 8, 16
H = 7
ROWB = 8
MROWB = ROWB + 2
COLB = TC // BC
M = ROWB * COLB
K = 6 * 128
F32, BF = jnp.float32, jnp.bfloat16


def swap_chunks(x):
    n = x.shape[0]
    row = lax.broadcasted_iota(jnp.int32, (n, 128), 0)
    chunk = lax.broadcasted_iota(jnp.int32, (n, 128), 1) // BC

    def sub(v, k):
        return pltpu.roll(v.reshape(n // 8, 8, 128), k, 1).reshape(n, 128)

    for k in (1, 2, 4):
        rbit = (row & k) != 0
        cbit = (chunk & k) != 0
        up = sub(pltpu.roll(x, 128 - BC * k, 1), k)
        if k == 4:
            dn = up
        else:
            dn = sub(pltpu.roll(x, BC * k, 1), 8 - k)
        x = jnp.where(rbit == cbit, x, jnp.where(rbit, up, dn))
    return x


def to_blocks(x):
    a, b = x.shape[0] // 8, x.shape[1] // 128
    tiles = [x[8 * i : 8 * i + 8, 128 * t : 128 * t + 128] for i in range(a) for t in range(b)]
    return swap_chunks(jnp.concatenate(tiles, axis=0))


def from_blocks(v, a, b):
    x = swap_chunks(v)
    rows = []
    for i in range(a):
        rows.append(jnp.concatenate([x[(i * b + t) * 8 : (i * b + t) * 8 + 8] for t in range(b)], axis=1))
    return jnp.concatenate(rows, axis=0)


def table_kernel(v_ref, w_ref):
    lane = lax.broadcasted_iota(jnp.int32, (16, 512), 1) % BC
    row = lax.broadcasted_iota(jnp.int32, (16, 512), 0)
    low = lane <= row

    def one(c, carry):
        at = pl.ds(pl.multiple_of(c * 128, 128), 128)
        x = jnp.broadcast_to(v_ref[c], (16, 512))
        r = pltpu.roll(x, 1, 1, stride=1, stride_axis=0)
        for p in range(8):
            rp = pltpu.roll(r, 512 - 16 * p, 1) if p else r
            lp = jnp.where(low, rp, 0.0).astype(BF)
            hp = jnp.where(low, 0.0, rp).astype(BF)
            for wy in range(24):
                dy, yw = wy // 8, wy % 8
                if (24 - wy) % 8 == p:
                    q = (24 - wy) // 8
                    w_ref[(dy * 2) * 128 + yw * 16 : (dy * 2) * 128 + yw * 16 + 16, at] = lp[:, 128 * q : 128 * q + 128]
                if (23 - wy) % 8 == p:
                    q = (23 - wy) // 8
                    w_ref[(dy * 2 + 1) * 128 + yw * 16 : (dy * 2 + 1) * 128 + yw * 16 + 16, at] = hp[:, 128 * q : 128 * q + 128]
        return carry

    lax.fori_loop(0, 2 * KERN, one, 0)


def taps_rows(kernels):
    k = kernels.astype(F32).reshape(2, KERN, KS, KS).swapaxes(0, 1).reshape(2 * KERN, KS, KS)
    k = k[:, ::-1, ::-1]
    k = jnp.pad(k, ((0, 0), (9, 32 - 9 - KS), (1, 0)))
    return k.reshape(2 * KERN, 1, 512)


def make_table(kernels):
    return pl.pallas_call(
        table_kernel,
        out_shape=jax.ShapeDtypeStruct((K, 2 * KERN * 128), BF),
        in_specs=[pl.BlockSpec(memory_space=pltpu.VMEM)],
        out_specs=pl.BlockSpec(memory_space=pltpu.VMEM),
        compiler_params=pltpu.CompilerParams(vmem_limit_bytes=32 * 1024 * 1024),
        cost_estimate=pl.CostEstimate(flops=20_000_000, bytes_accessed=10_000_000, transcendentals=0),
        name="taps_table",
    )(taps_rows(kernels))


def image_kernel(level_ref, shard_ref, wgt_ref, m0_ref, m1_ref, m2_ref, m3_ref, tabove_ref, tmid_ref, tbelow_ref, info_ref, w_ref,
                 resist_ref, grad_ref, lhs_ref, fields_ref, cot_ref):
    level_at = level_ref[0]
    x = m0_ref[...] + m1_ref[...].astype(F32) + m2_ref[...].astype(F32) + m3_ref[...].astype(F32)
    x = x.astype(BF).astype(F32)
    x = pltpu.roll(x, 8 * MROWB - 1, 0)
    x = jnp.concatenate([x, jnp.zeros((8 * MROWB, 128), F32)], axis=1)
    x = pltpu.roll(x, H, 1)
    mb = to_blocks(x).reshape(MROWB, 72, 128)
    for dy in range(3):
        for dx in range(2):
            part = mb[dy : dy + ROWB, dx : dx + COLB, :]
            lhs_ref[:, (dy * 2 + dx) * 128 : (dy * 2 + dx) * 128 + 128] = part.reshape(M, 128).astype(BF)
    intensity = jnp.zeros((M, 128), F32)
    for c in range(KERN):
        f = jnp.dot(lhs_ref[...], w_ref[:, c * 256 : c * 256 + 256], preferred_element_type=F32)
        fields_ref[c] = f
        f = f * f
        intensity = intensity + wgt_ref[level_at, c] * (f[:, :128] + f[:, 128:])
    level = 1.0 / (1.0 + jnp.exp(-STEEP * (intensity - THRESH)))
    resist_ref[...] = from_blocks(level, ROWB, 8)[8 : 8 + TR].astype(BF)
    goal = jnp.concatenate([tabove_ref[...].astype(F32)[8:], tmid_ref[...].astype(F32), tbelow_ref[...].astype(F32)[:8]], axis=0)
    goal = to_blocks(goal)
    slope = STEEP * (level - goal) * level * (1.0 - level)
    row_block = lax.broadcasted_iota(jnp.int32, (M, 128), 0) // COLB
    in_block = lax.broadcasted_iota(jnp.int32, (M, 128), 1) // BC
    at = shard_ref[0] * TR - 8 + row_block * 8 + in_block
    slope = jnp.where((at >= 0) & (at < 8 * TR), slope, 0.0)
    for c in range(KERN):
        s = 2.0 * wgt_ref[level_at, c] * slope
        cot_ref[:, c * 256 : c * 256 + 256] = (jnp.concatenate([s, s], axis=1) * fields_ref[c]).astype(BF)
    out = [None] * 7
    for dy in range(3):
        acc = lax.dot_general(cot_ref[...], w_ref[dy * 256 : dy * 256 + 256, :], (((1,), (1,)), ((), ())), preferred_element_type=F32)
        for dx in range(2):
            for i in range(ROWB):
                j = i + dy
                if 1 <= j <= 7:
                    piece = acc[i * COLB : i * COLB + COLB, dx * 128 : dx * 128 + 128]
                    piece = jnp.concatenate([piece, jnp.zeros((8, 128), F32)], axis=0)
                    if dx:
                        piece = pltpu.roll(piece, 1, 0)
                    out[j - 1] = piece if out[j - 1] is None else out[j - 1] + piece
    nat = from_blocks(jnp.concatenate(out, axis=0), 7, 9)
    nat = pltpu.roll(nat, 9 * 128 - H, 1)
    grad_ref[:TR] = nat[H : H + TR, :TC].astype(BF)
    info = jnp.broadcast_to(info_ref[...], (16, 128))
    row = lax.broadcasted_iota(jnp.int32, (16, 128), 0)
    digits = jnp.where(row == 0, info >> 7, jnp.where(row == 1, info & 127, 0)).astype(F32)
    grad_ref[TR:] = jnp.concatenate([digits, jnp.zeros((16, TC - 128), F32)], axis=1).astype(BF)


def image(level, shard, weights, parts, tabove, tmid, tbelow, info, table):
    vm = pl.BlockSpec(memory_space=pltpu.VMEM)
    sm = pl.BlockSpec(memory_space=pltpu.SMEM)
    return pl.pallas_call(
        image_kernel,
        out_shape=(jax.ShapeDtypeStruct((TR, TC), BF), jax.ShapeDtypeStruct((TR + 16, TC), BF)),
        in_specs=[sm] * 3 + [vm] * 9,
        out_specs=(vm, vm),
        scratch_shapes=[pltpu.VMEM((M, K), BF), pltpu.VMEM((KERN, M, 256), F32), pltpu.VMEM((M, 2 * KERN * 128), BF)],
        compiler_params=pltpu.CompilerParams(vmem_limit_bytes=28 * 1024 * 1024),
        cost_estimate=pl.CostEstimate(flops=5_000_000_000, bytes_accessed=8_000_000, transcendentals=65536),
        name="image",
    )(level, shard, weights, *parts, tabove, tmid, tbelow, info, table)


NX, NC, NY, NZ = 4, 2, 4, 8
WIDE = TC + 128
LEAD = 16
EXT = TR + 2 * LEAD
INFO = 128
PLACE_GRANT = 56


def place_kernel(shard_ref, ids_hbm, rows_hbm, cols_hbm, masters_hbm, mine_ref, theirs_ref, info_ref, scalars, panels, canvas, sem, info_sem):
    shard = shard_ref[0]
    loads = [pltpu.make_async_copy(ref.at[shard], scalars.at[j], info_sem.at[j]) for j, ref in enumerate((ids_hbm, rows_hbm, cols_hbm))]
    for cp in loads:
        cp.start()
    for cp in loads:
        cp.wait()
    copies = []
    for i in range(INST_DEV):
        cp = pltpu.make_async_copy(masters_hbm.at[scalars[0, 0, i]], panels.at[i], sem.at[i])
        cp.start()
        copies.append(cp)
        for j in range(3):
            info_ref[0, j * INST_DEV + i] = scalars[j, 0, i]
    for i in range(3 * INST_DEV, INFO):
        info_ref[0, i] = 0
    canvas[...] = jnp.zeros(canvas.shape, F32)
    lane = lax.broadcasted_iota(jnp.int32, (P_SIZE, 128), 1)
    sub = lax.broadcasted_iota(jnp.int32, (P_SIZE // 8 + 1, 8, 256), 1)
    none = jnp.zeros((1, 8, 256), F32)
    for i in range(INST_DEV):
        copies[i].wait()
        p = panels[i].astype(BF).astype(F32)
        c = scalars[2, 0, i]
        c0 = (c // 128) * 128
        d = c - c0
        p = pltpu.roll(p, d, 1)
        left = jnp.where(lane >= d, p, 0.0)
        right = jnp.where(lane >= d, 0.0, p)
        r = scalars[1, 0, i] + LEAD
        r0 = (r // 8) * 8
        full = jnp.concatenate([left, right], axis=1).reshape(P_SIZE // 8, 8, 256)
        full = pltpu.roll(full, r - r0, 1)
        full = jnp.where(sub >= r - r0, jnp.concatenate([full, none], axis=0), jnp.concatenate([none, full], axis=0))
        full = full.reshape(P_SIZE + 8, 256)
        at = (pl.ds(pl.multiple_of(r0, 8), P_SIZE + 8), pl.ds(pl.multiple_of(c0, 128), 256))
        canvas[at] = canvas[at] + full
    core = shard % NC
    for d in range(NX):
        x = (shard // NC + d) % NX
        mine_ref[d] = canvas[pl.ds(pl.multiple_of((x * NC + core) * TR, 8), EXT), :TC]
        theirs_ref[d] = canvas[pl.ds(pl.multiple_of((x * NC + 1 - core) * TR, 8), EXT), :TC].astype(BF)


def place(shard, ids, rows, cols, masters):
    vm = pl.BlockSpec(memory_space=pltpu.VMEM)
    sm = pl.BlockSpec(memory_space=pltpu.SMEM)
    hbm = pl.BlockSpec(memory_space=pltpu.HBM)
    bands = (NX, EXT, TC)
    return pl.pallas_call(
        place_kernel,
        out_shape=(jax.ShapeDtypeStruct(bands, F32), jax.ShapeDtypeStruct(bands, BF), jax.ShapeDtypeStruct((1, INFO), jnp.int32)),
        in_specs=[sm] + [hbm] * 4,
        out_specs=(vm, vm, sm),
        scratch_shapes=[
            pltpu.SMEM((3, 1, INST_DEV), jnp.int32),
            pltpu.VMEM((INST_DEV, P_SIZE, P_SIZE), F32),
            pltpu.VMEM((LEAD + 8 * TR + LEAD, WIDE), F32),
            pltpu.SemaphoreType.DMA((INST_DEV,)),
            pltpu.SemaphoreType.DMA((3,)),
        ],
        compiler_params=pltpu.CompilerParams(vmem_limit_bytes=PLACE_GRANT * 1024 * 1024),
        cost_estimate=pl.CostEstimate(flops=1_000_000, bytes_accessed=12_000_000, transcendentals=0),
        name="place",
    )(shard, ids, rows, cols, masters)


def cut_kernel(shard_ref, region_ref, g0, g1, g2, g3, own_ref, up_ref, down_ref, far_ref, *rest):
    outs, (canvas, sums, digits, lists, list_sem) = rest[: NZ + 1], rest[NZ + 1 :]
    digits[...] = jnp.zeros(digits.shape, jnp.int32)
    for k, g in enumerate((g0, g1, g2, g3)):
        tile = g[TR:, :128].astype(F32)
        digits[k : k + 1] = (tile[0:1] * 128.0 + tile[1:2]).astype(jnp.int32)
    load = pltpu.make_async_copy(digits, lists, list_sem)
    load.start()
    x = shard_ref[0] // NC
    z, y = region_ref[0] // NY, region_ref[0] % NY
    sums[...] = jnp.zeros(sums.shape, F32)

    def lay(ref, n, at):
        for core in range(NC):
            row = ((x + n) % NX * NC + core) * TR
            canvas[at, pl.ds(pl.multiple_of(row, 8), TR), :TC] = ref[core, at].astype(F32)

    for k in range(NY):
        lay(own_ref, 0, k)
        lay(up_ref, 3, k)
        lay(down_ref, 1, k)
        lay(far_ref, 2, k)
    load.wait()
    sub = lax.broadcasted_iota(jnp.int32, (P_SIZE // 8, 8, 128), 1)
    for k in range(NY):

        def one(i, carry, k=k):
            m = lists[k, i]

            @pl.when((m // 4) % NY == y)
            def _():
                r, c = lists[k, INST_DEV + i], lists[k, 2 * INST_DEV + i]
                r0, c0 = (r // 8) * 8, (c // 128) * 128
                full = canvas[k, pl.ds(pl.multiple_of(r0, 8), P_SIZE + 8), pl.ds(pl.multiple_of(c0, 128), 256)]
                full = pltpu.roll(full, 256 - (c - c0), 1)[:, :128]
                full = pltpu.roll(full.reshape(P_SIZE // 8 + 1, 8, 128), 8 - (r - r0), 1)
                full = jnp.where(sub < 8 - (r - r0), full[:-1], full[1:]).reshape(P_SIZE, 128)
                slot = (m // 16 - z + NZ) % NZ
                sums[slot, m % 4] = sums[slot, m % 4] + full

            return carry

        lax.fori_loop(0, INST_DEV, one, 0)
    for d in range(NZ):
        if d == 4:
            outs[4][...] = sums[4, :2].astype(BF)
            outs[NZ][...] = sums[4, 2:].astype(BF)
        else:
            outs[d][...] = sums[d].astype(outs[d].dtype)


def cut(shard, region, grads, bands):
    vm = pl.BlockSpec(memory_space=pltpu.VMEM)
    sm = pl.BlockSpec(memory_space=pltpu.SMEM)
    slot = (4, P_SIZE, P_SIZE)
    half = jax.ShapeDtypeStruct((2, P_SIZE, P_SIZE), BF)
    return pl.pallas_call(
        cut_kernel,
        out_shape=[jax.ShapeDtypeStruct(slot, F32 if d in (0, 2, 6) else BF) if d != 4 else half for d in range(NZ)] + [half],
        in_specs=[sm] * 2 + [vm] * 8,
        out_specs=[vm] * (NZ + 1),
        scratch_shapes=[
            pltpu.VMEM((NY, 8 * TR + 8, WIDE), F32),
            pltpu.VMEM((NZ, 4, P_SIZE, P_SIZE), F32),
            pltpu.VMEM((8, 128), jnp.int32),
            pltpu.SMEM((8, 128), jnp.int32),
            pltpu.SemaphoreType.DMA,
        ],
        compiler_params=pltpu.CompilerParams(vmem_limit_bytes=40 * 1024 * 1024),
        cost_estimate=pl.CostEstimate(flops=1_000_000, bytes_accessed=12_000_000, transcendentals=0),
        name="cut",
    )(shard, region, *grads, *bands)


def deposit_kernel(places, n_in, region_ref, *refs):
    blocks, (out_ref, wide, sem) = refs[: len(places)], refs[n_in:]
    z, y = region_ref[0] // NY, region_ref[0] % NY
    copies = []
    for block, (dz, ys) in zip(blocks, places):
        for j, k in enumerate(ys):
            at = len(copies)
            wide[at] = block[4 * j : 4 * j + 4].astype(F32)
            cp = pltpu.make_async_copy(wide.at[at], out_ref.at[(z + dz + NZ) % NZ, (y - k + NY) % NY], sem.at[at])
            cp.start()
            copies.append(cp)
    for cp in copies:
        cp.wait()


def deposit(region, out, items):
    places = [item[1:] for item in items]
    blocks = [item[0] for item in items]
    n, total = len(items), sum(len(item[2]) for item in items)
    hbm = pl.BlockSpec(memory_space=pltpu.HBM)
    old = [] if out is None else [out]
    return pl.pallas_call(
        functools.partial(deposit_kernel, places, n + len(old)),
        out_shape=jax.ShapeDtypeStruct((NZ, NY, 4, P_SIZE, P_SIZE), F32),
        in_specs=[pl.BlockSpec(memory_space=pltpu.SMEM)] + [pl.BlockSpec(memory_space=pltpu.VMEM)] * n + [hbm] * len(old),
        out_specs=hbm,
        input_output_aliases={n + 1: 0} if old else {},
        scratch_shapes=[pltpu.VMEM((total, 4, P_SIZE, P_SIZE), F32), pltpu.SemaphoreType.DMA((total,))],
        compiler_params=pltpu.CompilerParams(vmem_limit_bytes=16 * 1024 * 1024),
        cost_estimate=pl.CostEstimate(flops=200_000 * total, bytes_accessed=400_000 * total, transcendentals=0),
        name="deposit",
    )(region, *blocks, *old)


def shift(v, axis, by):
    n = lax.axis_size(axis)
    return lax.ppermute(v, axis, [(i, (i + by) % n) for i in range(n)])


def halo(v, axis, width):
    n = lax.axis_size(axis)
    above = lax.ppermute(v[-width:], axis, [(i, i + 1) for i in range(n - 1)])
    below = lax.ppermute(v[:width], axis, [(i + 1, i) for i in range(n - 1)])
    return above, below


def sum_along_z(slots):
    own, one, two, three, low, five, six, seven, high = slots
    three, five = shift(three, "z", 1), shift(five, "z", -1)
    low, high = shift(low, "z", 2).astype(F32), shift(high, "z", -2).astype(F32)
    three, one, seven = lax.optimization_barrier((three, one, seven))
    two, six = two + three.astype(F32), six + five.astype(F32)
    two = jnp.concatenate([two[:2] + low, two[2:]])
    six = jnp.concatenate([six[:2], six[2:] + high])
    near = shift(one, "z", 1).astype(F32) + shift(seven, "z", -1).astype(F32)
    return own + near + shift(two.astype(BF), "z", 2).astype(F32) + shift(six.astype(BF), "z", -2).astype(F32)


def spread(part, region):
    own = jnp.concatenate([part, shift(part, "y", 2)])
    ups, downs = shift(own, "z", 1), shift(own, "z", -1)
    came = [(shift(own, "y", 1), 0, (1, 3))]
    out = deposit(region, None, [(own, 0, (0, 2))])
    for d in (1, 2, 3):
        ups, downs, out = lax.optimization_barrier((ups, downs, out))
        here = [(ups, -d, (0, 2)), (downs, d, (0, 2))]
        ups = shift(ups, "z", 1)
        if d < 3:
            downs = shift(downs, "z", -1)
        side = [(shift(here[0][0], "y", 1), -d, (1, 3)), (shift(here[1][0], "y", -1), d, (3, 1))]
        out = deposit(region, out, here + came)
        came = side
    ups, out = lax.optimization_barrier((ups, out))
    side = shift(ups, "y", 1)
    out = deposit(region, out, [(ups, -4, (0, 2))] + came)
    out = deposit(region, out, [(side, -4, (1, 3))])
    return out.reshape(MAS_DEV, P_SIZE, P_SIZE)


def body(masters, inst_master, inst_row, inst_col, def_index, def_weights, kernels, target):
    shard = lax.axis_index(("x", "core")).reshape(1)
    region = lax.axis_index(("z", "y")).reshape(1)
    mine, theirs, info = place(shard, inst_master, inst_row, inst_col, masters)
    other = shift(theirs, "core", 1)
    table = make_table(kernels)
    sums = [mine[d] + other[d].astype(F32) for d in range(NX)]
    parts = [sums[0]] + [shift(sums[d].astype(BF), "x", d) for d in (2, 1, 3)]
    tmid = target[0]
    tabove, tbelow = halo(tmid, ("x", "core"), 16)
    resist, grad = image(def_index, shard, def_weights, parts, tabove, tmid, tbelow, info, table)
    grads = [grad] + [shift(grad, "y", k) for k in (1, 2, 3)]
    own = jnp.stack([g[:TR] for g in grads])
    up, down, far = [shift(own, "x", by) for by in (1, 3, 2)]
    bands = [lax.all_gather(v, "core") for v in (own, up, down, far)]
    part = sum_along_z(cut(shard, region, grads, bands)).astype(BF)
    return (spread(part, region), resist[None])


def solution(mesh):
    fine = Mesh(mesh.devices.reshape(NX, NC, NZ, NY), ("x", "core", "z", "y"))
    master, region = ("x", "core"), ("z", "y")
    return jax.shard_map(
        body,
        mesh=fine,
        in_specs=(
            P(master, None, None),
            P(None, region, None),
            P(None, region, None),
            P(None, region, None),
            P(region),
            P(),
            P(),
            P(region, master, None),
        ),
        out_specs=(P(master, None, None), P(region, master, None)),
        check_vma=False,
    )
```

```python
import functools
import jax, jax.numpy as jnp
from jax import lax
from jax.experimental import pallas as pl
from jax.sharding import Mesh, PartitionSpec as P
from jax.experimental.pallas import tpu as pltpu

TC = 1024; TR = 48; KS = 15; KERN = 12; P_SIZE = 128; MAS_DEV = 128; INST_DEV = 16
STEEP = 1.5; THRESH = 3.0
BR, BC = 8, 16
H = 7
ROWB = 8
MROWB = ROWB + 2
COLB = TC // BC
M = ROWB * COLB
K = 6 * 128
F32, BF = jnp.float32, jnp.bfloat16
NX, NC, NY, NZ = 4, 2, 4, 8
LEAD = 16
EXT = TR + 2 * LEAD


def swap_chunks(x):
    n = x.shape[0]
    row = lax.broadcasted_iota(jnp.int32, (n, 128), 0)
    chunk = lax.broadcasted_iota(jnp.int32, (n, 128), 1) // BC

    def sub(v, k):
        return pltpu.roll(v.reshape(n // 8, 8, 128), k, 1).reshape(n, 128)

    for k in (1, 2, 4):
        rbit = (row & k) != 0
        cbit = (chunk & k) != 0
        up = sub(pltpu.roll(x, 128 - BC * k, 1), k)
        if k == 4:
            dn = up
        else:
            dn = sub(pltpu.roll(x, BC * k, 1), 8 - k)
        x = jnp.where(rbit == cbit, x, jnp.where(rbit, up, dn))
    return x


def to_blocks(x):
    a, b = x.shape[0] // 8, x.shape[1] // 128
    tiles = [x[8 * i : 8 * i + 8, 128 * t : 128 * t + 128] for i in range(a) for t in range(b)]
    return swap_chunks(jnp.concatenate(tiles, axis=0))


def from_blocks(v, a, b):
    x = swap_chunks(v)
    rows = []
    for i in range(a):
        rows.append(jnp.concatenate([x[(i * b + t) * 8 : (i * b + t) * 8 + 8] for t in range(b)], axis=1))
    return jnp.concatenate(rows, axis=0)


def table_kernel(v_ref, w_ref):
    lane = lax.broadcasted_iota(jnp.int32, (16, 512), 1) % BC
    row = lax.broadcasted_iota(jnp.int32, (16, 512), 0)
    low = lane <= row

    def one(c, carry):
        at = pl.ds(pl.multiple_of(c * 128, 128), 128)
        x = jnp.broadcast_to(v_ref[c], (16, 512))
        r = pltpu.roll(x, 1, 1, stride=1, stride_axis=0)
        for p in range(8):
            rp = pltpu.roll(r, 512 - 16 * p, 1) if p else r
            lp = jnp.where(low, rp, 0.0).astype(BF)
            hp = jnp.where(low, 0.0, rp).astype(BF)
            for wy in range(24):
                dy, yw = wy // 8, wy % 8
                if (24 - wy) % 8 == p:
                    q = (24 - wy) // 8
                    w_ref[(dy * 2) * 128 + yw * 16 : (dy * 2) * 128 + yw * 16 + 16, at] = lp[:, 128 * q : 128 * q + 128]
                if (23 - wy) % 8 == p:
                    q = (23 - wy) // 8
                    w_ref[(dy * 2 + 1) * 128 + yw * 16 : (dy * 2 + 1) * 128 + yw * 16 + 16, at] = hp[:, 128 * q : 128 * q + 128]
        return carry

    lax.fori_loop(0, 2 * KERN, one, 0)


def taps_rows(kernels):
    k = kernels.astype(F32).reshape(2, KERN, KS, KS).swapaxes(0, 1).reshape(2 * KERN, KS, KS)
    k = k[:, ::-1, ::-1]
    k = jnp.pad(k, ((0, 0), (9, 32 - 9 - KS), (1, 0)))
    return k.reshape(2 * KERN, 1, 512)


def make_table(kernels):
    return pl.pallas_call(
        table_kernel,
        out_shape=jax.ShapeDtypeStruct((K, 2 * KERN * 128), BF),
        in_specs=[pl.BlockSpec(memory_space=pltpu.VMEM)],
        out_specs=pl.BlockSpec(memory_space=pltpu.VMEM),
        compiler_params=pltpu.CompilerParams(vmem_limit_bytes=32 * 1024 * 1024),
        cost_estimate=pl.CostEstimate(flops=20_000_000, bytes_accessed=10_000_000, transcendentals=0),
        name="taps_table",
    )(taps_rows(kernels))


def image_kernel(level_ref, shard_ref, wgt_ref, m0_ref, m1_ref, m2_ref, m3_ref, rims_ref, tmid_ref, info_ref, w_ref,
                 resist_ref, grad_ref, lhs_ref, fields_ref, cot_ref):
    level_at = level_ref[0]
    m1, m3 = m1_ref[...].astype(F32), m3_ref[...].astype(F32)
    x = m0_ref[...] + m1[:EXT] + m2_ref[...].astype(F32) + m3[:EXT]
    x = x.astype(BF).astype(F32)
    x = pltpu.roll(x, 8 * MROWB - 1, 0)
    x = jnp.concatenate([x, jnp.zeros((8 * MROWB, 128), F32)], axis=1)
    x = pltpu.roll(x, H, 1)
    mb = to_blocks(x).reshape(MROWB, 72, 128)
    for dy in range(3):
        for dx in range(2):
            part = mb[dy : dy + ROWB, dx : dx + COLB, :]
            lhs_ref[:, (dy * 2 + dx) * 128 : (dy * 2 + dx) * 128 + 128] = part.reshape(M, 128).astype(BF)
    intensity = jnp.zeros((M, 128), F32)
    for c in range(KERN):
        f = jnp.dot(lhs_ref[...], w_ref[:, c * 256 : c * 256 + 256], preferred_element_type=F32)
        fields_ref[c] = f
        f = f * f
        intensity = intensity + wgt_ref[level_at, c] * (f[:, :128] + f[:, 128:])
    level = 1.0 / (1.0 + jnp.exp(-STEEP * (intensity - THRESH)))
    resist_ref[...] = from_blocks(level, ROWB, 8)[8 : 8 + TR].astype(BF)
    rims = rims_ref[...].astype(F32)
    first = shard_ref[0] % NC == 0
    above = jnp.where(first, m1[EXT + 8 :], rims[8:])
    below = jnp.where(first, rims[:8], m3[EXT : EXT + 8])
    goal = jnp.concatenate([above, tmid_ref[...].astype(F32), below], axis=0)
    goal = to_blocks(goal)
    slope = STEEP * (level - goal) * level * (1.0 - level)
    row_block = lax.broadcasted_iota(jnp.int32, (M, 128), 0) // COLB
    in_block = lax.broadcasted_iota(jnp.int32, (M, 128), 1) // BC
    at = shard_ref[0] * TR - 8 + row_block * 8 + in_block
    slope = jnp.where((at >= 0) & (at < 8 * TR), slope, 0.0)
    for c in range(KERN):
        s = 2.0 * wgt_ref[level_at, c] * slope
        cot_ref[:, c * 256 : c * 256 + 256] = (jnp.concatenate([s, s], axis=1) * fields_ref[c]).astype(BF)
    out = [None] * 7
    for dy in range(3):
        acc = lax.dot_general(cot_ref[...], w_ref[dy * 256 : dy * 256 + 256, :], (((1,), (1,)), ((), ())), preferred_element_type=F32)
        for dx in range(2):
            for i in range(ROWB):
                j = i + dy
                if 1 <= j <= 7:
                    piece = acc[i * COLB : i * COLB + COLB, dx * 128 : dx * 128 + 128]
                    piece = jnp.concatenate([piece, jnp.zeros((8, 128), F32)], axis=0)
                    if dx:
                        piece = pltpu.roll(piece, 1, 0)
                    out[j - 1] = piece if out[j - 1] is None else out[j - 1] + piece
    nat = from_blocks(jnp.concatenate(out, axis=0), 7, 9)
    nat = pltpu.roll(nat, 9 * 128 - H, 1)
    grad_ref[:TR] = nat[H : H + TR, :TC].astype(BF)
    info = jnp.broadcast_to(info_ref[...], (16, 128))
    row = lax.broadcasted_iota(jnp.int32, (16, 128), 0)
    digits = jnp.where(row == 0, info >> 7, jnp.where(row == 1, info & 127, 0)).astype(F32)
    grad_ref[TR:] = jnp.concatenate([digits, jnp.zeros((16, TC - 128), F32)], axis=1).astype(BF)


def image(level, shard, weights, parts, rims, tmid, info, table):
    vm = pl.BlockSpec(memory_space=pltpu.VMEM)
    sm = pl.BlockSpec(memory_space=pltpu.SMEM)
    return pl.pallas_call(
        image_kernel,
        out_shape=(jax.ShapeDtypeStruct((TR, TC), BF), jax.ShapeDtypeStruct((TR + 16, TC), BF)),
        in_specs=[sm] * 3 + [vm] * 8,
        out_specs=(vm, vm),
        scratch_shapes=[pltpu.VMEM((M, K), BF), pltpu.VMEM((KERN, M, 256), F32), pltpu.VMEM((M, 2 * KERN * 128), BF)],
        compiler_params=pltpu.CompilerParams(vmem_limit_bytes=28 * 1024 * 1024),
        cost_estimate=pl.CostEstimate(flops=5_000_000_000, bytes_accessed=8_000_000, transcendentals=65536),
        name="image",
    )(level, shard, weights, *parts, rims, tmid, info, table)


WIDE = TC + 128
INFO = 128
PLACE_GRANT = 56


def place_kernel(shard_ref, ids_hbm, rows_hbm, cols_hbm, masters_hbm, target_ref, mine_ref, theirs_ref, info_ref, scalars, panels, canvas, sem, info_sem):
    shard = shard_ref[0]
    loads = [pltpu.make_async_copy(ref.at[shard], scalars.at[j], info_sem.at[j]) for j, ref in enumerate((ids_hbm, rows_hbm, cols_hbm))]
    for cp in loads:
        cp.start()
    for cp in loads:
        cp.wait()
    copies = []
    for i in range(INST_DEV):
        cp = pltpu.make_async_copy(masters_hbm.at[scalars[0, 0, i]], panels.at[i], sem.at[i])
        cp.start()
        copies.append(cp)
        for j in range(3):
            info_ref[0, j * INST_DEV + i] = scalars[j, 0, i]
    for i in range(3 * INST_DEV, INFO):
        info_ref[0, i] = 0
    canvas[...] = jnp.zeros(canvas.shape, F32)
    lane = lax.broadcasted_iota(jnp.int32, (P_SIZE, 128), 1)
    sub = lax.broadcasted_iota(jnp.int32, (P_SIZE // 8 + 1, 8, 256), 1)
    none = jnp.zeros((1, 8, 256), F32)
    for i in range(INST_DEV):
        copies[i].wait()
        p = panels[i].astype(BF).astype(F32)
        c = scalars[2, 0, i]
        c0 = (c // 128) * 128
        d = c - c0
        p = pltpu.roll(p, d, 1)
        left = jnp.where(lane >= d, p, 0.0)
        right = jnp.where(lane >= d, 0.0, p)
        r = scalars[1, 0, i] + LEAD
        r0 = (r // 8) * 8
        full = jnp.concatenate([left, right], axis=1).reshape(P_SIZE // 8, 8, 256)
        full = pltpu.roll(full, r - r0, 1)
        full = jnp.where(sub >= r - r0, jnp.concatenate([full, none], axis=0), jnp.concatenate([none, full], axis=0))
        full = full.reshape(P_SIZE + 8, 256)
        at = (pl.ds(pl.multiple_of(r0, 8), P_SIZE + 8), pl.ds(pl.multiple_of(c0, 128), 256))
        canvas[at] = canvas[at] + full
    core = shard % NC
    for d in range(NX):
        x = (shard // NC + d) % NX
        mine_ref[d] = canvas[pl.ds(pl.multiple_of((x * NC + core) * TR, 8), EXT), :TC]
        theirs_ref[EXT * d : EXT * d + EXT] = canvas[pl.ds(pl.multiple_of((x * NC + 1 - core) * TR, 8), EXT), :TC].astype(BF)
    goal = target_ref[...].astype(F32)
    theirs_ref[EXT * NX :] = jnp.concatenate([goal[:8], goal[TR - 8 :]], axis=0).astype(BF)


def place(shard, ids, rows, cols, masters, target):
    vm = pl.BlockSpec(memory_space=pltpu.VMEM)
    sm = pl.BlockSpec(memory_space=pltpu.SMEM)
    hbm = pl.BlockSpec(memory_space=pltpu.HBM)
    bands = (NX, EXT, TC)
    return pl.pallas_call(
        place_kernel,
        out_shape=(jax.ShapeDtypeStruct(bands, F32), jax.ShapeDtypeStruct((NX * EXT + 16, TC), BF), jax.ShapeDtypeStruct((1, INFO), jnp.int32)),
        in_specs=[sm] + [hbm] * 4 + [vm],
        out_specs=(vm, vm, sm),
        scratch_shapes=[
            pltpu.SMEM((3, 1, INST_DEV), jnp.int32),
            pltpu.VMEM((INST_DEV, P_SIZE, P_SIZE), F32),
            pltpu.VMEM((LEAD + 8 * TR + LEAD, WIDE), F32),
            pltpu.SemaphoreType.DMA((INST_DEV,)),
            pltpu.SemaphoreType.DMA((3,)),
        ],
        compiler_params=pltpu.CompilerParams(vmem_limit_bytes=PLACE_GRANT * 1024 * 1024),
        cost_estimate=pl.CostEstimate(flops=1_000_000, bytes_accessed=12_000_000, transcendentals=0),
        name="place",
    )(shard, ids, rows, cols, masters, target)


def cut_kernel(shard_ref, region_ref, g0, g1, g2, g3, own_ref, up_ref, down_ref, far_ref, *rest):
    outs, (canvas, sums, digits, lists, list_sem) = rest[: NZ + 1], rest[NZ + 1 :]
    digits[...] = jnp.zeros(digits.shape, jnp.int32)
    for k, g in enumerate((g0, g1, g2, g3)):
        tile = g[TR:, :128].astype(F32)
        digits[k : k + 1] = (tile[0:1] * 128.0 + tile[1:2]).astype(jnp.int32)
    load = pltpu.make_async_copy(digits, lists, list_sem)
    load.start()
    x = shard_ref[0] // NC
    z, y = region_ref[0] // NY, region_ref[0] % NY
    sums[...] = jnp.zeros(sums.shape, F32)

    def lay(ref, n, at):
        for core in range(NC):
            row = ((x + n) % NX * NC + core) * TR
            canvas[at, pl.ds(pl.multiple_of(row, 8), TR), :TC] = ref[core, at].astype(F32)

    for k in range(NY):
        lay(own_ref, 0, k)
        lay(up_ref, 3, k)
        lay(down_ref, 1, k)
        lay(far_ref, 2, k)
    load.wait()
    sub = lax.broadcasted_iota(jnp.int32, (P_SIZE // 8, 8, 128), 1)
    for k in range(NY):

        def one(i, carry, k=k):
            m = lists[k, i]

            @pl.when((m // 4) % NY == y)
            def _():
                r, c = lists[k, INST_DEV + i], lists[k, 2 * INST_DEV + i]
                r0, c0 = (r // 8) * 8, (c // 128) * 128
                full = canvas[k, pl.ds(pl.multiple_of(r0, 8), P_SIZE + 8), pl.ds(pl.multiple_of(c0, 128), 256)]
                full = pltpu.roll(full, 256 - (c - c0), 1)[:, :128]
                full = pltpu.roll(full.reshape(P_SIZE // 8 + 1, 8, 128), 8 - (r - r0), 1)
                full = jnp.where(sub < 8 - (r - r0), full[:-1], full[1:]).reshape(P_SIZE, 128)
                slot = (m // 16 - z + NZ) % NZ
                sums[slot, m % 4] = sums[slot, m % 4] + full

            return carry

        lax.fori_loop(0, INST_DEV, one, 0)
    for d in range(NZ):
        if d == 4:
            outs[4][...] = sums[4, :2].astype(BF)
            outs[NZ][...] = sums[4, 2:].astype(BF)
        else:
            outs[d][...] = sums[d].astype(outs[d].dtype)


def cut(shard, region, grads, bands):
    vm = pl.BlockSpec(memory_space=pltpu.VMEM)
    sm = pl.BlockSpec(memory_space=pltpu.SMEM)
    slot = (4, P_SIZE, P_SIZE)
    half = jax.ShapeDtypeStruct((2, P_SIZE, P_SIZE), BF)
    return pl.pallas_call(
        cut_kernel,
        out_shape=[jax.ShapeDtypeStruct(slot, F32 if d in (0, 2, 6) else BF) if d != 4 else half for d in range(NZ)] + [half],
        in_specs=[sm] * 2 + [vm] * 8,
        out_specs=[vm] * (NZ + 1),
        scratch_shapes=[
            pltpu.VMEM((NY, 8 * TR + 8, WIDE), F32),
            pltpu.VMEM((NZ, 4, P_SIZE, P_SIZE), F32),
            pltpu.VMEM((8, 128), jnp.int32),
            pltpu.SMEM((8, 128), jnp.int32),
            pltpu.SemaphoreType.DMA,
        ],
        compiler_params=pltpu.CompilerParams(vmem_limit_bytes=40 * 1024 * 1024),
        cost_estimate=pl.CostEstimate(flops=1_000_000, bytes_accessed=12_000_000, transcendentals=0),
        name="cut",
    )(shard, region, *grads, *bands)


def deposit_kernel(places, n_in, region_ref, *refs):
    blocks, (out_ref, wide, sem) = refs[: len(places)], refs[n_in:]
    z, y = region_ref[0] // NY, region_ref[0] % NY
    copies = []
    for block, (dz, ys) in zip(blocks, places):
        for j, k in enumerate(ys):
            at = len(copies)
            wide[at] = block[4 * j : 4 * j + 4].astype(F32)
            cp = pltpu.make_async_copy(wide.at[at], out_ref.at[(z + dz + NZ) % NZ, (y - k + NY) % NY], sem.at[at])
            cp.start()
            copies.append(cp)
    for cp in copies:
        cp.wait()


def deposit(region, out, items):
    places = [item[1:] for item in items]
    blocks = [item[0] for item in items]
    n, total = len(items), sum(len(item[2]) for item in items)
    hbm = pl.BlockSpec(memory_space=pltpu.HBM)
    old = [] if out is None else [out]
    return pl.pallas_call(
        functools.partial(deposit_kernel, places, n + len(old)),
        out_shape=jax.ShapeDtypeStruct((NZ, NY, 4, P_SIZE, P_SIZE), F32),
        in_specs=[pl.BlockSpec(memory_space=pltpu.SMEM)] + [pl.BlockSpec(memory_space=pltpu.VMEM)] * n + [hbm] * len(old),
        out_specs=hbm,
        input_output_aliases={n + 1: 0} if old else {},
        scratch_shapes=[pltpu.VMEM((total, 4, P_SIZE, P_SIZE), F32), pltpu.SemaphoreType.DMA((total,))],
        compiler_params=pltpu.CompilerParams(vmem_limit_bytes=16 * 1024 * 1024),
        cost_estimate=pl.CostEstimate(flops=200_000 * total, bytes_accessed=400_000 * total, transcendentals=0),
        name="deposit",
    )(region, *blocks, *old)


def shift(v, axis, by):
    n = lax.axis_size(axis)
    return lax.ppermute(v, axis, [(i, (i + by) % n) for i in range(n)])


def sum_along_z(slots):
    own, one, two, three, low, five, six, seven, high = slots
    three, five = shift(three, "z", 1), shift(five, "z", -1)
    low, high = shift(low, "z", 2).astype(F32), shift(high, "z", -2).astype(F32)
    three, one, seven = lax.optimization_barrier((three, one, seven))
    two, six = two + three.astype(F32), six + five.astype(F32)
    two = jnp.concatenate([two[:2] + low, two[2:]])
    six = jnp.concatenate([six[:2], six[2:] + high])
    near = shift(one, "z", 1).astype(F32) + shift(seven, "z", -1).astype(F32)
    return own + near + shift(two.astype(BF), "z", 2).astype(F32) + shift(six.astype(BF), "z", -2).astype(F32)


def spread(part, region):
    own = jnp.concatenate([part, shift(part, "y", 2)])
    ups, downs = shift(own, "z", 1), shift(own, "z", -1)
    came = [(shift(own, "y", 1), 0, (1, 3))]
    out = deposit(region, None, [(own, 0, (0, 2))])
    for d in (1, 2, 3):
        ups, downs, out = lax.optimization_barrier((ups, downs, out))
        here = [(ups, -d, (0, 2)), (downs, d, (0, 2))]
        ups = shift(ups, "z", 1)
        if d < 3:
            downs = shift(downs, "z", -1)
        side = [(shift(here[0][0], "y", 1), -d, (1, 3)), (shift(here[1][0], "y", -1), d, (3, 1))]
        out = deposit(region, out, here + came)
        came = side
    ups, out = lax.optimization_barrier((ups, out))
    side = shift(ups, "y", 1)
    out = deposit(region, out, [(ups, -4, (0, 2))] + came)
    out = deposit(region, out, [(side, -4, (1, 3))])
    return out.reshape(MAS_DEV, P_SIZE, P_SIZE)


def body(masters, inst_master, inst_row, inst_col, def_index, def_weights, kernels, target):
    shard = lax.axis_index(("x", "core")).reshape(1)
    region = lax.axis_index(("z", "y")).reshape(1)
    tmid = target[0]
    mine, theirs, info = place(shard, inst_master, inst_row, inst_col, masters, tmid)
    other = shift(theirs, "core", 1)
    rims = other[NX * EXT :]
    sums = [mine[d] + other[EXT * d : EXT * d + EXT].astype(F32) for d in range(NX)]
    sends = [jnp.concatenate([sums[d].astype(BF), rims]) if d != 2 else sums[d].astype(BF) for d in range(NX)]
    parts = [sums[0]] + [shift(sends[d], "x", d) for d in (1, 2, 3)]
    table = make_table(kernels)
    tmid = target[0]
    resist, grad = image(def_index, shard, def_weights, parts, rims, tmid, info, table)
    grads = [grad] + [shift(grad, "y", k) for k in (1, 2, 3)]
    own = jnp.stack([g[:TR] for g in grads])
    up, down, far = [shift(own, "x", by) for by in (1, 3, 2)]
    bands = [lax.all_gather(v, "core") for v in (own, up, down, far)]
    part = sum_along_z(cut(shard, region, grads, bands)).astype(BF)
    return (spread(part, region), resist[None])


def solution(mesh):
    fine = Mesh(mesh.devices.reshape(NX, NC, NZ, NY), ("x", "core", "z", "y"))
    master, region = ("x", "core"), ("z", "y")
    return jax.shard_map(
        body,
        mesh=fine,
        in_specs=(
            P(master, None, None),
            P(None, region, None),
            P(None, region, None),
            P(None, region, None),
            P(region),
            P(),
            P(),
            P(region, master, None),
        ),
        out_specs=(P(master, None, None), P(region, master, None)),
        check_vma=False,
    )
```

```python
import functools
import jax, jax.numpy as jnp
from jax import lax
from jax.experimental import pallas as pl
from jax.sharding import Mesh, PartitionSpec as P
from jax.experimental.pallas import tpu as pltpu

TC = 1024; TR = 48; KS = 15; KERN = 12; P_SIZE = 128; MAS_DEV = 128; INST_DEV = 16
STEEP = 1.5; THRESH = 3.0
BR, BC = 8, 16
H = 7
ROWB = 8
MROWB = ROWB + 2
COLB = TC // BC
M = ROWB * COLB
K = 6 * 128
F32, BF = jnp.float32, jnp.bfloat16
NX, NC, NY, NZ = 4, 2, 4, 8
LEAD = 16
EXT = TR + 2 * LEAD


def swap_chunks(x):
    n = x.shape[0]
    row = lax.broadcasted_iota(jnp.int32, (n, 128), 0)
    chunk = lax.broadcasted_iota(jnp.int32, (n, 128), 1) // BC

    def sub(v, k):
        return pltpu.roll(v.reshape(n // 8, 8, 128), k, 1).reshape(n, 128)

    for k in (1, 2, 4):
        rbit = (row & k) != 0
        cbit = (chunk & k) != 0
        up = sub(pltpu.roll(x, 128 - BC * k, 1), k)
        if k == 4:
            dn = up
        else:
            dn = sub(pltpu.roll(x, BC * k, 1), 8 - k)
        x = jnp.where(rbit == cbit, x, jnp.where(rbit, up, dn))
    return x


def to_blocks(x):
    a, b = x.shape[0] // 8, x.shape[1] // 128
    tiles = [x[8 * i : 8 * i + 8, 128 * t : 128 * t + 128] for i in range(a) for t in range(b)]
    return swap_chunks(jnp.concatenate(tiles, axis=0))


def from_blocks(v, a, b):
    x = swap_chunks(v)
    rows = []
    for i in range(a):
        rows.append(jnp.concatenate([x[(i * b + t) * 8 : (i * b + t) * 8 + 8] for t in range(b)], axis=1))
    return jnp.concatenate(rows, axis=0)


def table_kernel(v_ref, w_ref):
    lane = lax.broadcasted_iota(jnp.int32, (16, 512), 1) % BC
    row = lax.broadcasted_iota(jnp.int32, (16, 512), 0)
    low = lane <= row

    def one(c, carry):
        at = pl.ds(pl.multiple_of(c * 128, 128), 128)
        x = jnp.broadcast_to(v_ref[c], (16, 512))
        r = pltpu.roll(x, 1, 1, stride=1, stride_axis=0)
        for p in range(8):
            rp = pltpu.roll(r, 512 - 16 * p, 1) if p else r
            lp = jnp.where(low, rp, 0.0).astype(BF)
            hp = jnp.where(low, 0.0, rp).astype(BF)
            for wy in range(24):
                dy, yw = wy // 8, wy % 8
                if (24 - wy) % 8 == p:
                    q = (24 - wy) // 8
                    w_ref[(dy * 2) * 128 + yw * 16 : (dy * 2) * 128 + yw * 16 + 16, at] = lp[:, 128 * q : 128 * q + 128]
                if (23 - wy) % 8 == p:
                    q = (23 - wy) // 8
                    w_ref[(dy * 2 + 1) * 128 + yw * 16 : (dy * 2 + 1) * 128 + yw * 16 + 16, at] = hp[:, 128 * q : 128 * q + 128]
        return carry

    lax.fori_loop(0, 2 * KERN, one, 0)


def taps_rows(kernels):
    k = kernels.astype(F32).reshape(2, KERN, KS, KS).swapaxes(0, 1).reshape(2 * KERN, KS, KS)
    k = k[:, ::-1, ::-1]
    k = jnp.pad(k, ((0, 0), (9, 32 - 9 - KS), (1, 0)))
    return k.reshape(2 * KERN, 1, 512)


def make_table(kernels):
    return pl.pallas_call(
        table_kernel,
        out_shape=jax.ShapeDtypeStruct((K, 2 * KERN * 128), BF),
        in_specs=[pl.BlockSpec(memory_space=pltpu.VMEM)],
        out_specs=pl.BlockSpec(memory_space=pltpu.VMEM),
        compiler_params=pltpu.CompilerParams(vmem_limit_bytes=32 * 1024 * 1024),
        cost_estimate=pl.CostEstimate(flops=20_000_000, bytes_accessed=10_000_000, transcendentals=0),
        name="taps_table",
    )(taps_rows(kernels))


def image_kernel(level_ref, shard_ref, wgt_ref, m0_ref, m1_ref, m2_ref, m3_ref, rims_ref, tmid_ref, info_ref, w_ref,
                 resist_ref, grad_ref, lhs_ref, fields_ref, cot_ref):
    level_at = level_ref[0]
    m1 = m1_ref[...].astype(F32)
    x = m0_ref[...] + m1[:EXT] + m2_ref[...].astype(F32) + m3_ref[...].astype(F32)
    x = x.astype(BF).astype(F32)
    x = pltpu.roll(x, 8 * MROWB - 1, 0)
    x = jnp.concatenate([x, jnp.zeros((8 * MROWB, 128), F32)], axis=1)
    x = pltpu.roll(x, H, 1)
    mb = to_blocks(x).reshape(MROWB, 72, 128)
    for dy in range(3):
        for dx in range(2):
            part = mb[dy : dy + ROWB, dx : dx + COLB, :]
            lhs_ref[:, (dy * 2 + dx) * 128 : (dy * 2 + dx) * 128 + 128] = part.reshape(M, 128).astype(BF)
    intensity = jnp.zeros((M, 128), F32)
    for c in range(KERN):
        f = jnp.dot(lhs_ref[...], w_ref[:, c * 256 : c * 256 + 256], preferred_element_type=F32)
        fields_ref[c] = f
        f = f * f
        intensity = intensity + wgt_ref[level_at, c] * (f[:, :128] + f[:, 128:])
    level = 1.0 / (1.0 + jnp.exp(-STEEP * (intensity - THRESH)))
    resist_ref[...] = from_blocks(level, ROWB, 8)[8 : 8 + TR].astype(BF)
    rims = rims_ref[...].astype(F32)
    first = shard_ref[0] % NC == 0
    above = jnp.where(first, m1[EXT + 8 :], rims[8:])
    below = jnp.where(first, rims[:8], m1[EXT : EXT + 8])
    goal = jnp.concatenate([above, tmid_ref[...].astype(F32), below], axis=0)
    goal = to_blocks(goal)
    slope = STEEP * (level - goal) * level * (1.0 - level)
    row_block = lax.broadcasted_iota(jnp.int32, (M, 128), 0) // COLB
    in_block = lax.broadcasted_iota(jnp.int32, (M, 128), 1) // BC
    at = shard_ref[0] * TR - 8 + row_block * 8 + in_block
    slope = jnp.where((at >= 0) & (at < 8 * TR), slope, 0.0)
    for c in range(KERN):
        s = 2.0 * wgt_ref[level_at, c] * slope
        cot_ref[:, c * 256 : c * 256 + 256] = (jnp.concatenate([s, s], axis=1) * fields_ref[c]).astype(BF)
    out = [None] * 7
    for dy in range(3):
        acc = lax.dot_general(cot_ref[...], w_ref[dy * 256 : dy * 256 + 256, :], (((1,), (1,)), ((), ())), preferred_element_type=F32)
        for dx in range(2):
            for i in range(ROWB):
                j = i + dy
                if 1 <= j <= 7:
                    piece = acc[i * COLB : i * COLB + COLB, dx * 128 : dx * 128 + 128]
                    piece = jnp.concatenate([piece, jnp.zeros((8, 128), F32)], axis=0)
                    if dx:
                        piece = pltpu.roll(piece, 1, 0)
                    out[j - 1] = piece if out[j - 1] is None else out[j - 1] + piece
    nat = from_blocks(jnp.concatenate(out, axis=0), 7, 9)
    nat = pltpu.roll(nat, 9 * 128 - H, 1)
    grad_ref[:TR] = nat[H : H + TR, :TC].astype(BF)
    info = jnp.broadcast_to(info_ref[...], (16, 128))
    row = lax.broadcasted_iota(jnp.int32, (16, 128), 0)
    digits = jnp.where(row == 0, info >> 7, jnp.where(row == 1, info & 127, 0)).astype(F32)
    grad_ref[TR:] = jnp.concatenate([digits, jnp.zeros((16, TC - 128), F32)], axis=1).astype(BF)


def image(level, shard, weights, parts, rims, tmid, info, table):
    vm = pl.BlockSpec(memory_space=pltpu.VMEM)
    sm = pl.BlockSpec(memory_space=pltpu.SMEM)
    return pl.pallas_call(
        image_kernel,
        out_shape=(jax.ShapeDtypeStruct((TR, TC), BF), jax.ShapeDtypeStruct((TR + 16, TC), BF)),
        in_specs=[sm] * 3 + [vm] * 8,
        out_specs=(vm, vm),
        scratch_shapes=[pltpu.VMEM((M, K), BF), pltpu.VMEM((KERN, M, 256), F32), pltpu.VMEM((M, 2 * KERN * 128), BF)],
        compiler_params=pltpu.CompilerParams(vmem_limit_bytes=28 * 1024 * 1024),
        cost_estimate=pl.CostEstimate(flops=5_000_000_000, bytes_accessed=8_000_000, transcendentals=65536),
        name="image",
    )(level, shard, weights, *parts, rims, tmid, info, table)


WIDE = TC + 128
INFO = 128


def direction(shard):
    return 1 - 2 * (shard % NC)


PLACE_GRANT = 56


def place_kernel(shard_ref, ids_hbm, rows_hbm, cols_hbm, masters_hbm, target_hbm, mine_ref, theirs_ref, info_ref, scalars, panels, canvas, goal_buf, sem, info_sem, rim_sem):
    shard = shard_ref[0]
    loads = [pltpu.make_async_copy(ref.at[shard], scalars.at[j], info_sem.at[j]) for j, ref in enumerate((ids_hbm, rows_hbm, cols_hbm))]
    rim_load = pltpu.make_async_copy(target_hbm, goal_buf, rim_sem)
    for cp in loads + [rim_load]:
        cp.start()
    for cp in loads:
        cp.wait()
    copies = []
    for i in range(INST_DEV):
        cp = pltpu.make_async_copy(masters_hbm.at[scalars[0, 0, i]], panels.at[i], sem.at[i])
        cp.start()
        copies.append(cp)
        for j in range(3):
            info_ref[0, j * INST_DEV + i] = scalars[j, 0, i]
    for i in range(3 * INST_DEV, INFO):
        info_ref[0, i] = 0
    canvas[...] = jnp.zeros(canvas.shape, F32)
    lane = lax.broadcasted_iota(jnp.int32, (P_SIZE, 128), 1)
    sub = lax.broadcasted_iota(jnp.int32, (P_SIZE // 8 + 1, 8, 256), 1)
    none = jnp.zeros((1, 8, 256), F32)
    for i in range(INST_DEV):
        copies[i].wait()
        p = panels[i].astype(BF).astype(F32)
        c = scalars[2, 0, i]
        c0 = (c // 128) * 128
        d = c - c0
        p = pltpu.roll(p, d, 1)
        left = jnp.where(lane >= d, p, 0.0)
        right = jnp.where(lane >= d, 0.0, p)
        r = scalars[1, 0, i] + LEAD
        r0 = (r // 8) * 8
        full = jnp.concatenate([left, right], axis=1).reshape(P_SIZE // 8, 8, 256)
        full = pltpu.roll(full, r - r0, 1)
        full = jnp.where(sub >= r - r0, jnp.concatenate([full, none], axis=0), jnp.concatenate([none, full], axis=0))
        full = full.reshape(P_SIZE + 8, 256)
        at = (pl.ds(pl.multiple_of(r0, 8), P_SIZE + 8), pl.ds(pl.multiple_of(c0, 128), 256))
        canvas[at] = canvas[at] + full
    core = shard % NC
    way = direction(shard)
    for d in range(NX):
        x = (shard // NC + way * d + NX) % NX
        mine_ref[d] = canvas[pl.ds(pl.multiple_of((x * NC + core) * TR, 8), EXT), :TC]
        x = (shard // NC - way * d + NX) % NX
        theirs_ref[EXT * d : EXT * d + EXT] = canvas[pl.ds(pl.multiple_of((x * NC + 1 - core) * TR, 8), EXT), :TC].astype(BF)
    rim_load.wait()
    goal = goal_buf[...].astype(F32)
    theirs_ref[EXT * NX :] = jnp.concatenate([goal[:8], goal[TR - 8 :]], axis=0).astype(BF)


def place(shard, ids, rows, cols, masters, target):
    vm = pl.BlockSpec(memory_space=pltpu.VMEM)
    sm = pl.BlockSpec(memory_space=pltpu.SMEM)
    hbm = pl.BlockSpec(memory_space=pltpu.HBM)
    bands = (NX, EXT, TC)
    return pl.pallas_call(
        place_kernel,
        out_shape=(jax.ShapeDtypeStruct(bands, F32), jax.ShapeDtypeStruct((NX * EXT + 16, TC), BF), jax.ShapeDtypeStruct((1, INFO), jnp.int32)),
        in_specs=[sm] + [hbm] * 5,
        out_specs=(vm, vm, sm),
        scratch_shapes=[
            pltpu.SMEM((3, 1, INST_DEV), jnp.int32),
            pltpu.VMEM((INST_DEV, P_SIZE, P_SIZE), F32),
            pltpu.VMEM((LEAD + 8 * TR + LEAD, WIDE), F32),
            pltpu.VMEM((TR, TC), BF),
            pltpu.SemaphoreType.DMA((INST_DEV,)),
            pltpu.SemaphoreType.DMA((3,)),
            pltpu.SemaphoreType.DMA,
        ],
        compiler_params=pltpu.CompilerParams(vmem_limit_bytes=PLACE_GRANT * 1024 * 1024),
        cost_estimate=pl.CostEstimate(flops=1_000_000, bytes_accessed=12_000_000, transcendentals=0),
        name="place",
    )(shard, ids, rows, cols, masters, target)


def cut_kernel(shard_ref, region_ref, g0, g1, g2, g3, own_ref, up_ref, down_ref, far_ref, *rest):
    outs, (canvas, sums, digits, lists, list_sem) = rest[: NZ + 1], rest[NZ + 1 :]
    digits[...] = jnp.zeros(digits.shape, jnp.int32)
    for k, g in enumerate((g0, g1, g2, g3)):
        tile = g[TR:, :128].astype(F32)
        digits[k : k + 1] = (tile[0:1] * 128.0 + tile[1:2]).astype(jnp.int32)
    load = pltpu.make_async_copy(digits, lists, list_sem)
    load.start()
    x = shard_ref[0] // NC + NX
    z, y = region_ref[0] // NY, region_ref[0] % NY
    sums[...] = jnp.zeros(sums.shape, F32)

    for core in range(NC):
        way = 1 - 2 * core
        for ref, n in ((own_ref, 0), (up_ref, -way), (down_ref, way), (far_ref, 2)):
            row = pl.multiple_of(((x + n) % NX * NC + core) * TR, 8)
            for k in range(NY):
                canvas[-way * k % NY, pl.ds(row, TR), :TC] = ref[core, k].astype(F32)
    load.wait()
    sub = lax.broadcasted_iota(jnp.int32, (P_SIZE // 8, 8, 128), 1)
    way = direction(shard_ref[0])
    for k in range(NY):
        tile = (NY - way * k) % NY

        def one(i, carry, k=k, tile=tile):
            m = lists[k, i]

            @pl.when((m // 4) % NY == y)
            def _():
                r, c = lists[k, INST_DEV + i], lists[k, 2 * INST_DEV + i]
                r0, c0 = (r // 8) * 8, (c // 128) * 128
                full = canvas[tile, pl.ds(pl.multiple_of(r0, 8), P_SIZE + 8), pl.ds(pl.multiple_of(c0, 128), 256)]
                full = pltpu.roll(full, 256 - (c - c0), 1)[:, :128]
                full = pltpu.roll(full.reshape(P_SIZE // 8 + 1, 8, 128), 8 - (r - r0), 1)
                full = jnp.where(sub < 8 - (r - r0), full[:-1], full[1:]).reshape(P_SIZE, 128)
                slot = (way * (m // 16 - z) + NZ) % NZ
                sums[slot, m % 4] = sums[slot, m % 4] + full

            return carry

        lax.fori_loop(0, INST_DEV, one, 0)
    for d in range(NZ):
        if d == 4:
            outs[4][...] = sums[4, :2].astype(BF)
            outs[NZ][...] = sums[4, 2:].astype(BF)
        else:
            outs[d][...] = sums[d].astype(outs[d].dtype)


def cut(shard, region, grads, bands):
    vm = pl.BlockSpec(memory_space=pltpu.VMEM)
    sm = pl.BlockSpec(memory_space=pltpu.SMEM)
    slot = (4, P_SIZE, P_SIZE)
    half = jax.ShapeDtypeStruct((2, P_SIZE, P_SIZE), BF)
    return pl.pallas_call(
        cut_kernel,
        out_shape=[jax.ShapeDtypeStruct(slot, F32 if d in (0, 2, 6) else BF) if d != 4 else half for d in range(NZ)] + [half],
        in_specs=[sm] * 2 + [vm] * 8,
        out_specs=[vm] * (NZ + 1),
        scratch_shapes=[
            pltpu.VMEM((NY, 8 * TR + 8, WIDE), F32),
            pltpu.VMEM((NZ, 4, P_SIZE, P_SIZE), F32),
            pltpu.VMEM((8, 128), jnp.int32),
            pltpu.SMEM((8, 128), jnp.int32),
            pltpu.SemaphoreType.DMA,
        ],
        compiler_params=pltpu.CompilerParams(vmem_limit_bytes=40 * 1024 * 1024),
        cost_estimate=pl.CostEstimate(flops=1_000_000, bytes_accessed=12_000_000, transcendentals=0),
        name="cut",
    )(shard, region, *grads, *bands)


def deposit_kernel(places, n_in, shard_ref, region_ref, *refs):
    way = direction(shard_ref[0])
    blocks, (out_ref, wide, sem) = refs[: len(places)], refs[n_in:]
    z, y = region_ref[0] // NY, region_ref[0] % NY
    copies = []
    for block, (dz, ys) in zip(blocks, places):
        for j, k in enumerate(ys):
            at = len(copies)
            wide[at] = block[4 * j : 4 * j + 4].astype(F32)
            cp = pltpu.make_async_copy(wide.at[at], out_ref.at[(z + way * dz + NZ) % NZ, (y - way * k + NY) % NY], sem.at[at])
            cp.start()
            copies.append(cp)
    for cp in copies:
        cp.wait()


def deposit(shard, region, out, items):
    places = [item[1:] for item in items]
    blocks = [item[0] for item in items]
    n, total = len(items), sum(len(item[2]) for item in items)
    hbm = pl.BlockSpec(memory_space=pltpu.HBM)
    old = [] if out is None else [out]
    return pl.pallas_call(
        functools.partial(deposit_kernel, places, n + len(old)),
        out_shape=jax.ShapeDtypeStruct((NZ, NY, 4, P_SIZE, P_SIZE), F32),
        in_specs=[pl.BlockSpec(memory_space=pltpu.SMEM)] * 2 + [pl.BlockSpec(memory_space=pltpu.VMEM)] * n + [hbm] * len(old),
        out_specs=hbm,
        input_output_aliases={n + 2: 0} if old else {},
        scratch_shapes=[pltpu.VMEM((total, 4, P_SIZE, P_SIZE), F32), pltpu.SemaphoreType.DMA((total,))],
        compiler_params=pltpu.CompilerParams(vmem_limit_bytes=16 * 1024 * 1024),
        cost_estimate=pl.CostEstimate(flops=200_000 * total, bytes_accessed=400_000 * total, transcendentals=0),
        name="deposit",
    )(shard, region, *blocks, *old)


def shift(v, axis, by):
    n = lax.axis_size(axis)
    first = axis == "x"
    place_of = (lambda core, i: i * NC + core) if first else (lambda core, i: core * n + i)
    ring = [(place_of(core, i), place_of(core, (i + (by if core == 0 else -by)) % n)) for core in range(NC) for i in range(n)]
    return lax.ppermute(v, ("x", "core") if first else ("core", axis), ring)


def sum_along_z(slots):
    own, one, two, three, low, five, six, seven, high = slots
    three, five = shift(three, "z", 1), shift(five, "z", -1)
    low, high = shift(low, "z", 2).astype(F32), shift(high, "z", -2).astype(F32)
    three, one, seven = lax.optimization_barrier((three, one, seven))
    two, six = two + three.astype(F32), six + five.astype(F32)
    two = jnp.concatenate([two[:2] + low, two[2:]])
    six = jnp.concatenate([six[:2], six[2:] + high])
    near = shift(one, "z", 1).astype(F32) + shift(seven, "z", -1).astype(F32)
    return own + near + shift(two.astype(BF), "z", 2).astype(F32) + shift(six.astype(BF), "z", -2).astype(F32)


def spread(part, shard, region):
    own = jnp.concatenate([part, shift(part, "y", 2)])
    ups, downs = shift(own, "z", 1), shift(own, "z", -1)
    came = [(shift(own, "y", 1), 0, (1, 3))]
    out = deposit(shard, region, None, [(own, 0, (0, 2))])
    for d in (1, 2, 3):
        ups, downs, out = lax.optimization_barrier((ups, downs, out))
        here = [(ups, -d, (0, 2)), (downs, d, (0, 2))]
        ups = shift(ups, "z", 1)
        if d < 3:
            downs = shift(downs, "z", -1)
        side = [(shift(here[0][0], "y", 1), -d, (1, 3)), (shift(here[1][0], "y", -1), d, (3, 1))]
        out = deposit(shard, region, out, here + came)
        came = side
    ups, out = lax.optimization_barrier((ups, out))
    side = shift(ups, "y", 1)
    out = deposit(shard, region, out, [(ups, -4, (0, 2))] + came)
    out = deposit(shard, region, out, [(side, -4, (1, 3))])
    return out.reshape(MAS_DEV, P_SIZE, P_SIZE)


def body(masters, inst_master, inst_row, inst_col, def_index, def_weights, kernels, target):
    shard = lax.axis_index(("x", "core")).reshape(1)
    region = lax.axis_index(("z", "y")).reshape(1)
    tmid = target[0]
    mine, theirs, info = place(shard, inst_master, inst_row, inst_col, masters, tmid)
    other = lax.ppermute(theirs, "core", [(0, 1), (1, 0)])
    rims = other[NX * EXT :]
    sums = [mine[d] + other[EXT * d : EXT * d + EXT].astype(F32) for d in range(NX)]
    sends = [jnp.concatenate([sums[d].astype(BF), rims]) if d == 1 else sums[d].astype(BF) for d in range(NX)]
    parts = [sums[0]] + [shift(sends[d], "x", d) for d in (1, 2, 3)]
    table = make_table(kernels)
    tmid = target[0]
    resist, grad = image(def_index, shard, def_weights, parts, rims, tmid, info, table)
    across, before, after = [shift(grad, "y", k) for k in (2, 1, 3)]
    grads = [grad, before, across, after]
    own = jnp.stack([g[:TR] for g in grads])
    up, down, far = [shift(own, "x", by) for by in (1, 3, 2)]
    bands = [lax.all_gather(v, "core") for v in (own, up, down, far)]
    part = sum_along_z(cut(shard, region, grads, bands)).astype(BF)
    return (spread(part, shard, region), resist[None])


def solution(mesh):
    fine = Mesh(mesh.devices.reshape(NX, NC, NZ, NY), ("x", "core", "z", "y"))
    master, region = ("x", "core"), ("z", "y")
    return jax.shard_map(
        body,
        mesh=fine,
        in_specs=(
            P(master, None, None),
            P(None, region, None),
            P(None, region, None),
            P(None, region, None),
            P(region),
            P(),
            P(),
            P(region, master, None),
        ),
        out_specs=(P(master, None, None), P(region, master, None)),
        check_vma=False,
    )
```

```python
import functools
import jax, jax.numpy as jnp
from jax import lax
from jax.experimental import pallas as pl
from jax.sharding import Mesh, PartitionSpec as P
from jax.experimental.pallas import tpu as pltpu

TC = 1024; TR = 48; KS = 15; KERN = 12; P_SIZE = 128; MAS_DEV = 128; INST_DEV = 16
STEEP = 1.5; THRESH = 3.0
BR, BC = 8, 16
H = 7
ROWB = 8
MROWB = ROWB + 2
COLB = TC // BC
M = ROWB * COLB
K = 6 * 128
F32, BF = jnp.float32, jnp.bfloat16
NX, NC, NY, NZ = 4, 2, 4, 8
LEAD = 16
EXT = TR + 2 * LEAD


def swap_chunks(x):
    n = x.shape[0]
    row = lax.broadcasted_iota(jnp.int32, (n, 128), 0)
    chunk = lax.broadcasted_iota(jnp.int32, (n, 128), 1) // BC

    def sub(v, k):
        return pltpu.roll(v.reshape(n // 8, 8, 128), k, 1).reshape(n, 128)

    for k in (1, 2, 4):
        rbit = (row & k) != 0
        cbit = (chunk & k) != 0
        up = sub(pltpu.roll(x, 128 - BC * k, 1), k)
        if k == 4:
            dn = up
        else:
            dn = sub(pltpu.roll(x, BC * k, 1), 8 - k)
        x = jnp.where(rbit == cbit, x, jnp.where(rbit, up, dn))
    return x


def to_blocks(x):
    a, b = x.shape[0] // 8, x.shape[1] // 128
    tiles = [x[8 * i : 8 * i + 8, 128 * t : 128 * t + 128] for i in range(a) for t in range(b)]
    return swap_chunks(jnp.concatenate(tiles, axis=0))


def from_blocks(v, a, b):
    x = swap_chunks(v)
    rows = []
    for i in range(a):
        rows.append(jnp.concatenate([x[(i * b + t) * 8 : (i * b + t) * 8 + 8] for t in range(b)], axis=1))
    return jnp.concatenate(rows, axis=0)


def table_kernel(v_ref, w_ref):
    lane = lax.broadcasted_iota(jnp.int32, (16, 512), 1) % BC
    row = lax.broadcasted_iota(jnp.int32, (16, 512), 0)
    low = lane <= row

    def one(c, carry):
        at = pl.ds(pl.multiple_of(c * 128, 128), 128)
        x = jnp.broadcast_to(v_ref[c], (16, 512))
        r = pltpu.roll(x, 1, 1, stride=1, stride_axis=0)
        for p in range(8):
            rp = pltpu.roll(r, 512 - 16 * p, 1) if p else r
            lp = jnp.where(low, rp, 0.0).astype(BF)
            hp = jnp.where(low, 0.0, rp).astype(BF)
            for wy in range(24):
                dy, yw = wy // 8, wy % 8
                if (24 - wy) % 8 == p:
                    q = (24 - wy) // 8
                    w_ref[(dy * 2) * 128 + yw * 16 : (dy * 2) * 128 + yw * 16 + 16, at] = lp[:, 128 * q : 128 * q + 128]
                if (23 - wy) % 8 == p:
                    q = (23 - wy) // 8
                    w_ref[(dy * 2 + 1) * 128 + yw * 16 : (dy * 2 + 1) * 128 + yw * 16 + 16, at] = hp[:, 128 * q : 128 * q + 128]
        return carry

    def four(i, carry):
        for j in range(4):
            one(4 * i + j, carry)
        return carry

    lax.fori_loop(0, KERN // 2, four, 0)


def taps_rows(kernels):
    k = kernels.astype(F32).reshape(2, KERN, KS, KS).swapaxes(0, 1).reshape(2 * KERN, KS, KS)
    k = k[:, ::-1, ::-1]
    k = jnp.pad(k, ((0, 0), (9, 32 - 9 - KS), (1, 0)))
    return k.reshape(2 * KERN, 1, 512)


def make_table(kernels):
    return pl.pallas_call(
        table_kernel,
        out_shape=jax.ShapeDtypeStruct((K, 2 * KERN * 128), BF),
        in_specs=[pl.BlockSpec(memory_space=pltpu.VMEM)],
        out_specs=pl.BlockSpec(memory_space=pltpu.VMEM),
        compiler_params=pltpu.CompilerParams(vmem_limit_bytes=32 * 1024 * 1024),
        cost_estimate=pl.CostEstimate(flops=20_000_000, bytes_accessed=10_000_000, transcendentals=0),
        name="taps_table",
    )(taps_rows(kernels))


def image_kernel(level_ref, shard_ref, wgt_ref, m0_ref, m1_ref, m2_ref, m3_ref, rims_ref, tmid_ref, info_ref, w_ref,
                 resist_ref, grad_ref, lhs_ref, fields_ref, cot_ref):
    level_at = level_ref[0]
    m1 = m1_ref[...].astype(F32)
    x = m0_ref[...] + m1[:EXT] + m2_ref[...].astype(F32) + m3_ref[...].astype(F32)
    x = x.astype(BF).astype(F32)
    x = pltpu.roll(x, 8 * MROWB - 1, 0)
    x = jnp.concatenate([x, jnp.zeros((8 * MROWB, 128), F32)], axis=1)
    x = pltpu.roll(x, H, 1)
    mb = to_blocks(x).reshape(MROWB, 72, 128)
    for dy in range(3):
        for dx in range(2):
            part = mb[dy : dy + ROWB, dx : dx + COLB, :]
            lhs_ref[:, (dy * 2 + dx) * 128 : (dy * 2 + dx) * 128 + 128] = part.reshape(M, 128).astype(BF)
    intensity = jnp.zeros((M, 128), F32)
    for c in range(KERN):
        f = jnp.dot(lhs_ref[...], w_ref[:, c * 256 : c * 256 + 256], preferred_element_type=F32)
        fields_ref[c] = f
        f = f * f
        intensity = intensity + wgt_ref[level_at, c] * (f[:, :128] + f[:, 128:])
    level = 1.0 / (1.0 + jnp.exp(-STEEP * (intensity - THRESH)))
    resist_ref[...] = from_blocks(level, ROWB, 8)[8 : 8 + TR].astype(BF)
    rims = rims_ref[...].astype(F32)
    first = shard_ref[0] % NC == 0
    above = jnp.where(first, m1[EXT + 8 :], rims[8:])
    below = jnp.where(first, rims[:8], m1[EXT : EXT + 8])
    goal = jnp.concatenate([above, tmid_ref[...].astype(F32), below], axis=0)
    goal = to_blocks(goal)
    slope = STEEP * (level - goal) * level * (1.0 - level)
    row_block = lax.broadcasted_iota(jnp.int32, (M, 128), 0) // COLB
    in_block = lax.broadcasted_iota(jnp.int32, (M, 128), 1) // BC
    at = shard_ref[0] * TR - 8 + row_block * 8 + in_block
    slope = jnp.where((at >= 0) & (at < 8 * TR), slope, 0.0)
    for c in range(KERN):
        s = 2.0 * wgt_ref[level_at, c] * slope
        cot_ref[:, c * 256 : c * 256 + 256] = (jnp.concatenate([s, s], axis=1) * fields_ref[c]).astype(BF)
    out = [None] * 7
    for dy in range(3):
        acc = lax.dot_general(cot_ref[...], w_ref[dy * 256 : dy * 256 + 256, :], (((1,), (1,)), ((), ())), preferred_element_type=F32)
        for dx in range(2):
            for i in range(ROWB):
                j = i + dy
                if 1 <= j <= 7:
                    piece = acc[i * COLB : i * COLB + COLB, dx * 128 : dx * 128 + 128]
                    piece = jnp.concatenate([piece, jnp.zeros((8, 128), F32)], axis=0)
                    if dx:
                        piece = pltpu.roll(piece, 1, 0)
                    out[j - 1] = piece if out[j - 1] is None else out[j - 1] + piece
    nat = from_blocks(jnp.concatenate(out, axis=0), 7, 9)
    nat = pltpu.roll(nat, 9 * 128 - H, 1)
    grad_ref[:TR] = nat[H : H + TR, :TC].astype(BF)
    info = jnp.broadcast_to(info_ref[...], (16, 128))
    row = lax.broadcasted_iota(jnp.int32, (16, 128), 0)
    digits = jnp.where(row == 0, info >> 7, jnp.where(row == 1, info & 127, 0)).astype(F32)
    grad_ref[TR:] = jnp.concatenate([digits, jnp.zeros((16, TC - 128), F32)], axis=1).astype(BF)


def image(level, shard, weights, parts, rims, tmid, info, table):
    vm = pl.BlockSpec(memory_space=pltpu.VMEM)
    sm = pl.BlockSpec(memory_space=pltpu.SMEM)
    return pl.pallas_call(
        image_kernel,
        out_shape=(jax.ShapeDtypeStruct((TR, TC), BF), jax.ShapeDtypeStruct((TR + 16, TC), BF)),
        in_specs=[sm] * 3 + [vm] * 8,
        out_specs=(vm, vm),
        scratch_shapes=[pltpu.VMEM((M, K), BF), pltpu.VMEM((KERN, M, 256), F32), pltpu.VMEM((M, 2 * KERN * 128), BF)],
        compiler_params=pltpu.CompilerParams(vmem_limit_bytes=28 * 1024 * 1024),
        cost_estimate=pl.CostEstimate(flops=5_000_000_000, bytes_accessed=8_000_000, transcendentals=65536),
        name="image",
    )(level, shard, weights, *parts, rims, tmid, info, table)


WIDE = TC + 128
INFO = 128


def direction(shard):
    return 1 - 2 * (shard % NC)


PLACE_GRANT = 56


def place_kernel(shard_ref, ids_hbm, rows_hbm, cols_hbm, masters_hbm, target_hbm, mine_ref, theirs_ref, info_ref, scalars, panels, canvas, goal_buf, sem, info_sem, rim_sem):
    shard = shard_ref[0]
    loads = [pltpu.make_async_copy(ref.at[shard], scalars.at[j], info_sem.at[j]) for j, ref in enumerate((ids_hbm, rows_hbm, cols_hbm))]
    rim_load = pltpu.make_async_copy(target_hbm, goal_buf, rim_sem)
    for cp in loads + [rim_load]:
        cp.start()
    for cp in loads:
        cp.wait()
    copies = []
    for i in range(INST_DEV):
        cp = pltpu.make_async_copy(masters_hbm.at[scalars[0, 0, i]], panels.at[i], sem.at[i])
        cp.start()
        copies.append(cp)
        for j in range(3):
            info_ref[0, j * INST_DEV + i] = scalars[j, 0, i]
    for i in range(3 * INST_DEV, INFO):
        info_ref[0, i] = 0
    canvas[...] = jnp.zeros(canvas.shape, F32)
    lane = lax.broadcasted_iota(jnp.int32, (P_SIZE, 128), 1)
    sub = lax.broadcasted_iota(jnp.int32, (P_SIZE // 8 + 1, 8, 256), 1)
    none = jnp.zeros((1, 8, 256), F32)
    for i in range(INST_DEV):
        copies[i].wait()
        p = panels[i].astype(BF).astype(F32)
        c = scalars[2, 0, i]
        c0 = (c // 128) * 128
        d = c - c0
        p = pltpu.roll(p, d, 1)
        left = jnp.where(lane >= d, p, 0.0)
        right = jnp.where(lane >= d, 0.0, p)
        r = scalars[1, 0, i] + LEAD
        r0 = (r // 8) * 8
        full = jnp.concatenate([left, right], axis=1).reshape(P_SIZE // 8, 8, 256)
        full = pltpu.roll(full, r - r0, 1)
        full = jnp.where(sub >= r - r0, jnp.concatenate([full, none], axis=0), jnp.concatenate([none, full], axis=0))
        full = full.reshape(P_SIZE + 8, 256)
        at = (pl.ds(pl.multiple_of(r0, 8), P_SIZE + 8), pl.ds(pl.multiple_of(c0, 128), 256))
        canvas[at] = canvas[at] + full
    core = shard % NC
    way = direction(shard)
    for d in range(NX):
        x = (shard // NC + way * d + NX) % NX
        mine_ref[d] = canvas[pl.ds(pl.multiple_of((x * NC + core) * TR, 8), EXT), :TC]
        x = (shard // NC - way * d + NX) % NX
        theirs_ref[EXT * d : EXT * d + EXT] = canvas[pl.ds(pl.multiple_of((x * NC + 1 - core) * TR, 8), EXT), :TC].astype(BF)
    rim_load.wait()
    goal = goal_buf[...].astype(F32)
    theirs_ref[EXT * NX :] = jnp.concatenate([goal[:8], goal[TR - 8 :]], axis=0).astype(BF)


def place(shard, ids, rows, cols, masters, target):
    vm = pl.BlockSpec(memory_space=pltpu.VMEM)
    sm = pl.BlockSpec(memory_space=pltpu.SMEM)
    hbm = pl.BlockSpec(memory_space=pltpu.HBM)
    bands = (NX, EXT, TC)
    return pl.pallas_call(
        place_kernel,
        out_shape=(jax.ShapeDtypeStruct(bands, F32), jax.ShapeDtypeStruct((NX * EXT + 16, TC), BF), jax.ShapeDtypeStruct((1, INFO), jnp.int32)),
        in_specs=[sm] + [hbm] * 5,
        out_specs=(vm, vm, sm),
        scratch_shapes=[
            pltpu.SMEM((3, 1, INST_DEV), jnp.int32),
            pltpu.VMEM((INST_DEV, P_SIZE, P_SIZE), F32),
            pltpu.VMEM((LEAD + 8 * TR + LEAD, WIDE), F32),
            pltpu.VMEM((TR, TC), BF),
            pltpu.SemaphoreType.DMA((INST_DEV,)),
            pltpu.SemaphoreType.DMA((3,)),
            pltpu.SemaphoreType.DMA,
        ],
        compiler_params=pltpu.CompilerParams(vmem_limit_bytes=PLACE_GRANT * 1024 * 1024),
        cost_estimate=pl.CostEstimate(flops=1_000_000, bytes_accessed=12_000_000, transcendentals=0),
        name="place",
    )(shard, ids, rows, cols, masters, target)


def cut_kernel(shard_ref, region_ref, g0, g1, g2, g3, *rest):
    mine, theirs, rest = rest[:4], rest[4:8], rest[8:]
    outs, (canvas, sums, digits, lists, list_sem) = rest[: NZ + 1], rest[NZ + 1 :]
    digits[...] = jnp.zeros(digits.shape, jnp.int32)
    for k, g in enumerate((g0, g1, g2, g3)):
        tile = g[TR:, :128].astype(F32)
        digits[k : k + 1] = (tile[0:1] * 128.0 + tile[1:2]).astype(jnp.int32)
    load = pltpu.make_async_copy(digits, lists, list_sem)
    load.start()
    x = shard_ref[0] // NC + NX
    z, y = region_ref[0] // NY, region_ref[0] % NY
    sums[...] = jnp.zeros(sums.shape, F32)

    core = shard_ref[0] % NC
    for refs, c in ((mine, core), (theirs, 1 - core)):
        way = direction(c)
        for ref, n in zip(refs, (0, -way, way, 2)):
            row = pl.multiple_of(((x + n) % NX * NC + c) * TR, 8)
            for k in range(NY):
                canvas[(NY - way * k) % NY, pl.ds(row, TR), :TC] = ref[k].astype(F32)
    load.wait()
    sub = lax.broadcasted_iota(jnp.int32, (P_SIZE // 8, 8, 128), 1)
    way = direction(shard_ref[0])
    for k in range(NY):
        tile = (NY - way * k) % NY

        def one(i, carry, k=k, tile=tile):
            m = lists[k, i]

            @pl.when((m // 4) % NY == y)
            def _():
                r, c = lists[k, INST_DEV + i], lists[k, 2 * INST_DEV + i]
                r0, c0 = (r // 8) * 8, (c // 128) * 128
                full = canvas[tile, pl.ds(pl.multiple_of(r0, 8), P_SIZE + 8), pl.ds(pl.multiple_of(c0, 128), 256)]
                full = pltpu.roll(full, 256 - (c - c0), 1)[:, :128]
                full = pltpu.roll(full.reshape(P_SIZE // 8 + 1, 8, 128), 8 - (r - r0), 1)
                full = jnp.where(sub < 8 - (r - r0), full[:-1], full[1:]).reshape(P_SIZE, 128)
                slot = (way * (m // 16 - z) + NZ) % NZ
                sums[slot, m % 4] = sums[slot, m % 4] + full

            return carry

        lax.fori_loop(0, INST_DEV, one, 0)
    for d in range(NZ):
        if d == 4:
            outs[4][...] = sums[4, :2].astype(BF)
            outs[NZ][...] = sums[4, 2:].astype(BF)
        else:
            outs[d][...] = sums[d].astype(outs[d].dtype)


def cut(shard, region, grads, mine, theirs):
    vm = pl.BlockSpec(memory_space=pltpu.VMEM)
    sm = pl.BlockSpec(memory_space=pltpu.SMEM)
    slot = (4, P_SIZE, P_SIZE)
    half = jax.ShapeDtypeStruct((2, P_SIZE, P_SIZE), BF)
    return pl.pallas_call(
        cut_kernel,
        out_shape=[jax.ShapeDtypeStruct(slot, F32 if d in (0, 2, 6) else BF) if d != 4 else half for d in range(NZ)] + [half],
        in_specs=[sm] * 2 + [vm] * 12,
        out_specs=[vm] * (NZ + 1),
        scratch_shapes=[
            pltpu.VMEM((NY, 8 * TR + 8, WIDE), F32),
            pltpu.VMEM((NZ, 4, P_SIZE, P_SIZE), F32),
            pltpu.VMEM((8, 128), jnp.int32),
            pltpu.SMEM((8, 128), jnp.int32),
            pltpu.SemaphoreType.DMA,
        ],
        compiler_params=pltpu.CompilerParams(vmem_limit_bytes=20 * 1024 * 1024),
        cost_estimate=pl.CostEstimate(flops=1_000_000, bytes_accessed=12_000_000, transcendentals=0),
        name="cut",
    )(shard, region, *grads, *mine, *theirs)


def deposit_kernel(places, n_in, shard_ref, region_ref, *refs):
    way = direction(shard_ref[0])
    blocks, (out_ref, wide, sem) = refs[: len(places)], refs[n_in:]
    z, y = region_ref[0] // NY, region_ref[0] % NY
    copies = []
    for block, (dz, ys) in zip(blocks, places):
        for j, k in enumerate(ys):
            at = len(copies)
            wide[at] = block[4 * j : 4 * j + 4].astype(F32)
            cp = pltpu.make_async_copy(wide.at[at], out_ref.at[(z + way * dz + NZ) % NZ, (y - way * k + NY) % NY], sem.at[at])
            cp.start()
            copies.append(cp)
    for cp in copies:
        cp.wait()


def deposit(shard, region, out, items):
    places = [item[1:] for item in items]
    blocks = [item[0] for item in items]
    n, total = len(items), sum(len(item[2]) for item in items)
    hbm = pl.BlockSpec(memory_space=pltpu.HBM)
    old = [] if out is None else [out]
    return pl.pallas_call(
        functools.partial(deposit_kernel, places, n + len(old)),
        out_shape=jax.ShapeDtypeStruct((NZ, NY, 4, P_SIZE, P_SIZE), F32),
        in_specs=[pl.BlockSpec(memory_space=pltpu.SMEM)] * 2 + [pl.BlockSpec(memory_space=pltpu.VMEM)] * n + [hbm] * len(old),
        out_specs=hbm,
        input_output_aliases={n + 2: 0} if old else {},
        scratch_shapes=[pltpu.VMEM((total, 4, P_SIZE, P_SIZE), F32), pltpu.SemaphoreType.DMA((total,))],
        compiler_params=pltpu.CompilerParams(vmem_limit_bytes=16 * 1024 * 1024),
        cost_estimate=pl.CostEstimate(flops=200_000 * total, bytes_accessed=400_000 * total, transcendentals=0),
        name="deposit",
    )(shard, region, *blocks, *old)


def shift(v, axis, by):
    n = lax.axis_size(axis)
    first = axis == "x"
    place_of = (lambda core, i: i * NC + core) if first else (lambda core, i: core * n + i)
    ring = [(place_of(core, i), place_of(core, (i + (by if core == 0 else -by)) % n)) for core in range(NC) for i in range(n)]
    return lax.ppermute(v, ("x", "core") if first else ("core", axis), ring)


def swap(v):
    return lax.ppermute(v, "core", [(0, 1), (1, 0)])


def sum_along_z(slots):
    own, one, two, three, low, five, six, seven, high = slots
    three, five = shift(three, "z", 1), shift(five, "z", -1)
    low, high = shift(low, "z", 2).astype(F32), shift(high, "z", -2).astype(F32)
    three, one, seven = lax.optimization_barrier((three, one, seven))
    two, six = two + three.astype(F32), six + five.astype(F32)
    two = jnp.concatenate([two[:2] + low, two[2:]])
    six = jnp.concatenate([six[:2], six[2:] + high])
    near = shift(one, "z", 1).astype(F32) + shift(seven, "z", -1).astype(F32)
    return own + near + shift(two.astype(BF), "z", 2).astype(F32) + shift(six.astype(BF), "z", -2).astype(F32)


def spread(part, shard, region):
    own = jnp.concatenate([part, shift(part, "y", 2)])
    ups, downs = shift(own, "z", 1), shift(own, "z", -1)
    came = [(shift(own, "y", 1), 0, (1, 3))]
    out = deposit(shard, region, None, [(own, 0, (0, 2))])
    for d in (1, 2, 3):
        ups, downs, out = lax.optimization_barrier((ups, downs, out))
        here = [(ups, -d, (0, 2)), (downs, d, (0, 2))]
        ups = shift(ups, "z", 1)
        if d < 3:
            downs = shift(downs, "z", -1)
        side = [(shift(here[0][0], "y", 1), -d, (1, 3)), (shift(here[1][0], "y", -1), d, (3, 1))]
        out = deposit(shard, region, out, here + came)
        came = side
    ups, out = lax.optimization_barrier((ups, out))
    side = shift(ups, "y", 1)
    out = deposit(shard, region, out, [(ups, -4, (0, 2))] + came)
    out = deposit(shard, region, out, [(side, -4, (1, 3))])
    return out.reshape(MAS_DEV, P_SIZE, P_SIZE)


def body(masters, inst_master, inst_row, inst_col, def_index, def_weights, kernels, target):
    shard = lax.axis_index(("x", "core")).reshape(1)
    region = lax.axis_index(("z", "y")).reshape(1)
    tmid = target[0]
    mine, theirs, info = place(shard, inst_master, inst_row, inst_col, masters, tmid)
    other = swap(theirs)
    rims = other[NX * EXT :]
    sums = [mine[d] + other[EXT * d : EXT * d + EXT].astype(F32) for d in range(NX)]
    sends = [jnp.concatenate([sums[d].astype(BF), rims]) if d == 1 else sums[d].astype(BF) for d in range(NX)]
    parts = [sums[0]] + [shift(sends[d], "x", d) for d in (1, 2, 3)]
    table = make_table(kernels)
    tmid = target[0]
    resist, grad = image(def_index, shard, def_weights, parts, rims, tmid, info, table)
    across, before, after = [shift(grad, "y", k) for k in (2, 1, 3)]
    grads = [grad, before, across, after]
    own = jnp.stack([g[:TR] for g in grads])
    up, down, far = [shift(own, "x", by) for by in (1, 3, 2)]
    bands = (own, up, down, far)
    swapped = [swap(v) for v in bands]
    part = sum_along_z(cut(shard, region, grads, bands, swapped)).astype(BF)
    return (spread(part, shard, region), resist[None])


def solution(mesh):
    fine = Mesh(mesh.devices.reshape(NX, NC, NZ, NY), ("x", "core", "z", "y"))
    master, region = ("x", "core"), ("z", "y")
    return jax.shard_map(
        body,
        mesh=fine,
        in_specs=(
            P(master, None, None),
            P(None, region, None),
            P(None, region, None),
            P(None, region, None),
            P(region),
            P(),
            P(),
            P(region, master, None),
        ),
        out_specs=(P(master, None, None), P(region, master, None)),
        check_vma=False,
    )
```

```python
import functools
import jax, jax.numpy as jnp
from jax import lax
from jax.experimental import pallas as pl
from jax.sharding import Mesh, PartitionSpec as P
from jax.experimental.pallas import tpu as pltpu

TC = 1024; TR = 48; KS = 15; KERN = 12; P_SIZE = 128; MAS_DEV = 128; INST_DEV = 16
STEEP = 1.5; THRESH = 3.0
BR, BC = 8, 16
H = 7
ROWB = 8
MROWB = ROWB + 2
COLB = TC // BC
M = ROWB * COLB
K = 6 * 128
F32, BF = jnp.float32, jnp.bfloat16
NX, NC, NY, NZ = 4, 2, 4, 8
LEAD = 16
EXT = TR + 2 * LEAD


def swap_chunks(x):
    n = x.shape[0]
    row = lax.broadcasted_iota(jnp.int32, (n, 128), 0)
    chunk = lax.broadcasted_iota(jnp.int32, (n, 128), 1) // BC

    def sub(v, k):
        return pltpu.roll(v.reshape(n // 8, 8, 128), k, 1).reshape(n, 128)

    for k in (1, 2, 4):
        rbit = (row & k) != 0
        cbit = (chunk & k) != 0
        up = sub(pltpu.roll(x, 128 - BC * k, 1), k)
        if k == 4:
            dn = up
        else:
            dn = sub(pltpu.roll(x, BC * k, 1), 8 - k)
        x = jnp.where(rbit == cbit, x, jnp.where(rbit, up, dn))
    return x


def to_blocks(x):
    a, b = x.shape[0] // 8, x.shape[1] // 128
    tiles = [x[8 * i : 8 * i + 8, 128 * t : 128 * t + 128] for i in range(a) for t in range(b)]
    return swap_chunks(jnp.concatenate(tiles, axis=0))


def from_blocks(v, a, b):
    x = swap_chunks(v)
    rows = []
    for i in range(a):
        rows.append(jnp.concatenate([x[(i * b + t) * 8 : (i * b + t) * 8 + 8] for t in range(b)], axis=1))
    return jnp.concatenate(rows, axis=0)


def table_kernel(v_ref, w_ref):
    lane = lax.broadcasted_iota(jnp.int32, (16, 512), 1) % BC
    row = lax.broadcasted_iota(jnp.int32, (16, 512), 0)
    low = lane <= row

    def one(c, carry):
        at = pl.ds(pl.multiple_of(c * 128, 128), 128)
        x = jnp.broadcast_to(v_ref[c], (16, 512))
        r = pltpu.roll(x, 1, 1, stride=1, stride_axis=0)
        for p in range(8):
            rp = pltpu.roll(r, 512 - 16 * p, 1) if p else r
            lp = jnp.where(low, rp, 0.0).astype(BF)
            hp = jnp.where(low, 0.0, rp).astype(BF)
            for wy in range(24):
                dy, yw = wy // 8, wy % 8
                if (24 - wy) % 8 == p:
                    q = (24 - wy) // 8
                    w_ref[(dy * 2) * 128 + yw * 16 : (dy * 2) * 128 + yw * 16 + 16, at] = lp[:, 128 * q : 128 * q + 128]
                if (23 - wy) % 8 == p:
                    q = (23 - wy) // 8
                    w_ref[(dy * 2 + 1) * 128 + yw * 16 : (dy * 2 + 1) * 128 + yw * 16 + 16, at] = hp[:, 128 * q : 128 * q + 128]
        return carry

    def four(i, carry):
        for j in range(4):
            one(4 * i + j, carry)
        return carry

    lax.fori_loop(0, KERN // 2, four, 0)


def taps_rows(kernels):
    k = kernels.astype(F32).reshape(2, KERN, KS, KS).swapaxes(0, 1).reshape(2 * KERN, KS, KS)
    k = k[:, ::-1, ::-1]
    k = jnp.pad(k, ((0, 0), (9, 32 - 9 - KS), (1, 0)))
    return k.reshape(2 * KERN, 1, 512)


def make_table(kernels):
    return pl.pallas_call(
        table_kernel,
        out_shape=jax.ShapeDtypeStruct((K, 2 * KERN * 128), BF),
        in_specs=[pl.BlockSpec(memory_space=pltpu.VMEM)],
        out_specs=pl.BlockSpec(memory_space=pltpu.VMEM),
        compiler_params=pltpu.CompilerParams(vmem_limit_bytes=32 * 1024 * 1024),
        cost_estimate=pl.CostEstimate(flops=20_000_000, bytes_accessed=10_000_000, transcendentals=0),
        name="taps_table",
    )(taps_rows(kernels))


def image_kernel(level_ref, shard_ref, wgt_ref, m0_ref, m1_ref, m2_ref, m3_ref, rims_ref, tmid_ref, info_ref, w_ref,
                 resist_ref, grad_ref, lhs_ref, fields_ref, cot_ref):
    level_at = level_ref[0]
    m1 = m1_ref[...].astype(F32)
    x = m0_ref[...] + m1[:EXT] + m2_ref[...].astype(F32) + m3_ref[...].astype(F32)
    x = x.astype(BF).astype(F32)
    x = pltpu.roll(x, 8 * MROWB - 1, 0)
    x = jnp.concatenate([x, jnp.zeros((8 * MROWB, 128), F32)], axis=1)
    x = pltpu.roll(x, H, 1)
    mb = to_blocks(x).reshape(MROWB, 72, 128)
    for dy in range(3):
        for dx in range(2):
            part = mb[dy : dy + ROWB, dx : dx + COLB, :]
            lhs_ref[:, (dy * 2 + dx) * 128 : (dy * 2 + dx) * 128 + 128] = part.reshape(M, 128).astype(BF)
    intensity = jnp.zeros((M, 128), F32)
    for c in range(KERN):
        f = jnp.dot(lhs_ref[...], w_ref[:, c * 256 : c * 256 + 256], preferred_element_type=F32)
        fields_ref[c] = f
        f = f * f
        intensity = intensity + wgt_ref[level_at, c] * (f[:, :128] + f[:, 128:])
    level = 1.0 / (1.0 + jnp.exp(-STEEP * (intensity - THRESH)))
    resist_ref[...] = from_blocks(level, ROWB, 8)[8 : 8 + TR].astype(BF)
    rims = rims_ref[...].astype(F32)
    first = shard_ref[0] % NC == 0
    above = jnp.where(first, m1[EXT + 8 :], rims[8:])
    below = jnp.where(first, rims[:8], m1[EXT : EXT + 8])
    goal = jnp.concatenate([above, tmid_ref[...].astype(F32), below], axis=0)
    goal = to_blocks(goal)
    slope = STEEP * (level - goal) * level * (1.0 - level)
    row_block = lax.broadcasted_iota(jnp.int32, (M, 128), 0) // COLB
    in_block = lax.broadcasted_iota(jnp.int32, (M, 128), 1) // BC
    at = shard_ref[0] * TR - 8 + row_block * 8 + in_block
    slope = jnp.where((at >= 0) & (at < 8 * TR), slope, 0.0)
    for c in range(KERN):
        s = 2.0 * wgt_ref[level_at, c] * slope
        cot_ref[:, c * 256 : c * 256 + 256] = (jnp.concatenate([s, s], axis=1) * fields_ref[c]).astype(BF)
    out = [None] * 7
    for dy in range(3):
        acc = lax.dot_general(cot_ref[...], w_ref[dy * 256 : dy * 256 + 256, :], (((1,), (1,)), ((), ())), preferred_element_type=F32)
        for dx in range(2):
            for i in range(ROWB):
                j = i + dy
                if 1 <= j <= 7:
                    piece = acc[i * COLB : i * COLB + COLB, dx * 128 : dx * 128 + 128]
                    piece = jnp.concatenate([piece, jnp.zeros((8, 128), F32)], axis=0)
                    if dx:
                        piece = pltpu.roll(piece, 1, 0)
                    out[j - 1] = piece if out[j - 1] is None else out[j - 1] + piece
    nat = from_blocks(jnp.concatenate(out, axis=0), 7, 9)
    nat = pltpu.roll(nat, 9 * 128 - H, 1)
    grad_ref[:TR] = nat[H : H + TR, :TC].astype(BF)
    info = jnp.broadcast_to(info_ref[...], (16, 128))
    row = lax.broadcasted_iota(jnp.int32, (16, 128), 0)
    digits = jnp.where(row == 0, info >> 7, jnp.where(row == 1, info & 127, 0)).astype(F32)
    grad_ref[TR:] = jnp.concatenate([digits, jnp.zeros((16, TC - 128), F32)], axis=1).astype(BF)


def image(level, shard, weights, parts, rims, tmid, info, table):
    vm = pl.BlockSpec(memory_space=pltpu.VMEM)
    sm = pl.BlockSpec(memory_space=pltpu.SMEM)
    return pl.pallas_call(
        image_kernel,
        out_shape=(jax.ShapeDtypeStruct((TR, TC), BF), jax.ShapeDtypeStruct((TR + 16, TC), BF)),
        in_specs=[sm] * 3 + [vm] * 8,
        out_specs=(vm, vm),
        scratch_shapes=[pltpu.VMEM((M, K), BF), pltpu.VMEM((KERN, M, 256), F32), pltpu.VMEM((M, 2 * KERN * 128), BF)],
        compiler_params=pltpu.CompilerParams(vmem_limit_bytes=28 * 1024 * 1024),
        cost_estimate=pl.CostEstimate(flops=5_000_000_000, bytes_accessed=8_000_000, transcendentals=65536),
        name="image",
    )(level, shard, weights, *parts, rims, tmid, info, table)


WIDE = TC + 128
INFO = 128


def direction(shard):
    return 1 - 2 * (shard % NC)


PLACE_GRANT = 56


def place_kernel(shard_ref, ids_hbm, rows_hbm, cols_hbm, masters_hbm, target_hbm, mine_ref, theirs_ref, info_ref, scalars, panels, canvas, goal_buf, sem, info_sem, rim_sem):
    shard = shard_ref[0]
    loads = [pltpu.make_async_copy(ref.at[shard], scalars.at[j], info_sem.at[j]) for j, ref in enumerate((ids_hbm, rows_hbm, cols_hbm))]
    rim_load = pltpu.make_async_copy(target_hbm, goal_buf, rim_sem)
    for cp in loads + [rim_load]:
        cp.start()
    for cp in loads:
        cp.wait()
    copies = []
    for i in range(INST_DEV):
        cp = pltpu.make_async_copy(masters_hbm.at[scalars[0, 0, i]], panels.at[i], sem.at[i])
        cp.start()
        copies.append(cp)
        for j in range(3):
            info_ref[0, j * INST_DEV + i] = scalars[j, 0, i]
    for i in range(3 * INST_DEV, INFO):
        info_ref[0, i] = 0
    canvas[...] = jnp.zeros(canvas.shape, F32)
    lane = lax.broadcasted_iota(jnp.int32, (P_SIZE, 128), 1)
    sub = lax.broadcasted_iota(jnp.int32, (P_SIZE // 8 + 1, 8, 256), 1)
    none = jnp.zeros((1, 8, 256), F32)
    for i in range(INST_DEV):
        copies[i].wait()
        p = panels[i].astype(BF).astype(F32)
        c = scalars[2, 0, i]
        c0 = (c // 128) * 128
        d = c - c0
        p = pltpu.roll(p, d, 1)
        left = jnp.where(lane >= d, p, 0.0)
        right = jnp.where(lane >= d, 0.0, p)
        r = scalars[1, 0, i] + LEAD
        r0 = (r // 8) * 8
        full = jnp.concatenate([left, right], axis=1).reshape(P_SIZE // 8, 8, 256)
        full = pltpu.roll(full, r - r0, 1)
        full = jnp.where(sub >= r - r0, jnp.concatenate([full, none], axis=0), jnp.concatenate([none, full], axis=0))
        full = full.reshape(P_SIZE + 8, 256)
        at = (pl.ds(pl.multiple_of(r0, 8), P_SIZE + 8), pl.ds(pl.multiple_of(c0, 128), 256))
        canvas[at] = canvas[at] + full
    core = shard % NC
    way = direction(shard)
    for d in range(NX):
        x = (shard // NC + way * d + NX) % NX
        mine_ref[d] = canvas[pl.ds(pl.multiple_of((x * NC + core) * TR, 8), EXT), :TC]
        x = (shard // NC - way * d + NX) % NX
        theirs_ref[EXT * d : EXT * d + EXT] = canvas[pl.ds(pl.multiple_of((x * NC + 1 - core) * TR, 8), EXT), :TC].astype(BF)
    rim_load.wait()
    goal = goal_buf[...].astype(F32)
    theirs_ref[EXT * NX :] = jnp.concatenate([goal[:8], goal[TR - 8 :]], axis=0).astype(BF)


def place(shard, ids, rows, cols, masters, target):
    vm = pl.BlockSpec(memory_space=pltpu.VMEM)
    sm = pl.BlockSpec(memory_space=pltpu.SMEM)
    hbm = pl.BlockSpec(memory_space=pltpu.HBM)
    bands = (NX, EXT, TC)
    return pl.pallas_call(
        place_kernel,
        out_shape=(jax.ShapeDtypeStruct(bands, F32), jax.ShapeDtypeStruct((NX * EXT + 16, TC), BF), jax.ShapeDtypeStruct((1, INFO), jnp.int32)),
        in_specs=[sm] + [hbm] * 5,
        out_specs=(vm, vm, sm),
        scratch_shapes=[
            pltpu.SMEM((3, 1, INST_DEV), jnp.int32),
            pltpu.VMEM((INST_DEV, P_SIZE, P_SIZE), F32),
            pltpu.VMEM((LEAD + 8 * TR + LEAD, WIDE), F32),
            pltpu.VMEM((TR, TC), BF),
            pltpu.SemaphoreType.DMA((INST_DEV,)),
            pltpu.SemaphoreType.DMA((3,)),
            pltpu.SemaphoreType.DMA,
        ],
        compiler_params=pltpu.CompilerParams(vmem_limit_bytes=PLACE_GRANT * 1024 * 1024),
        cost_estimate=pl.CostEstimate(flops=1_000_000, bytes_accessed=12_000_000, transcendentals=0),
        name="place",
    )(shard, ids, rows, cols, masters, target)


def cut_kernel(shard_ref, region_ref, g0, g1, g2, g3, *rest):
    mine, theirs, rest = rest[:4], rest[4:8], rest[8:]
    outs, (canvas, sums, digits, lists, list_sem) = rest[: NZ + 1], rest[NZ + 1 :]
    digits[...] = jnp.zeros(digits.shape, jnp.int32)
    for k, g in enumerate((g0, g1, g2, g3)):
        tile = g[TR:, :128].astype(F32)
        digits[k : k + 1] = (tile[0:1] * 128.0 + tile[1:2]).astype(jnp.int32)
    load = pltpu.make_async_copy(digits, lists, list_sem)
    load.start()
    x = shard_ref[0] // NC + NX
    z, y = region_ref[0] // NY, region_ref[0] % NY
    sums[...] = jnp.zeros(sums.shape, F32)

    core = shard_ref[0] % NC
    for refs, c in ((mine, core), (theirs, 1 - core)):
        way = direction(c)
        for ref, n in zip(refs, (0, -way, way, 2)):
            row = pl.multiple_of(((x + n) % NX * NC + c) * TR, 8)
            for k in range(NY):
                canvas[(NY - way * k) % NY, pl.ds(row, TR), :TC] = ref[k].astype(F32)
    load.wait()
    sub = lax.broadcasted_iota(jnp.int32, (P_SIZE // 8, 8, 128), 1)
    way = direction(shard_ref[0])
    for k in range(NY):
        tile = (NY - way * k) % NY

        def one(i, carry, k=k, tile=tile):
            m = lists[k, i]

            @pl.when((m // 4) % NY == y)
            def _():
                r, c = lists[k, INST_DEV + i], lists[k, 2 * INST_DEV + i]
                r0, c0 = (r // 8) * 8, (c // 128) * 128
                full = canvas[tile, pl.ds(pl.multiple_of(r0, 8), P_SIZE + 8), pl.ds(pl.multiple_of(c0, 128), 256)]
                full = pltpu.roll(full, 256 - (c - c0), 1)[:, :128]
                full = pltpu.roll(full.reshape(P_SIZE // 8 + 1, 8, 128), 8 - (r - r0), 1)
                full = jnp.where(sub < 8 - (r - r0), full[:-1], full[1:]).reshape(P_SIZE, 128)
                slot = (way * (m // 16 - z) + NZ) % NZ
                sums[slot, m % 4] = sums[slot, m % 4] + full

            return carry

        lax.fori_loop(0, INST_DEV, one, 0)
    for d in range(NZ):
        if d == 4:
            outs[4][...] = sums[4, :2].astype(BF)
            outs[NZ][...] = sums[4, 2:].astype(BF)
        else:
            outs[d][...] = sums[d].astype(outs[d].dtype)


def cut(shard, region, grads, mine, theirs):
    vm = pl.BlockSpec(memory_space=pltpu.VMEM)
    sm = pl.BlockSpec(memory_space=pltpu.SMEM)
    slot = (4, P_SIZE, P_SIZE)
    half = jax.ShapeDtypeStruct((2, P_SIZE, P_SIZE), BF)
    return pl.pallas_call(
        cut_kernel,
        out_shape=[jax.ShapeDtypeStruct(slot, F32 if d in (0, 2, 6) else BF) if d != 4 else half for d in range(NZ)] + [half],
        in_specs=[sm] * 2 + [vm] * 12,
        out_specs=[vm] * (NZ + 1),
        scratch_shapes=[
            pltpu.VMEM((NY, 8 * TR + 8, WIDE), F32),
            pltpu.VMEM((NZ, 4, P_SIZE, P_SIZE), F32),
            pltpu.VMEM((8, 128), jnp.int32),
            pltpu.SMEM((8, 128), jnp.int32),
            pltpu.SemaphoreType.DMA,
        ],
        compiler_params=pltpu.CompilerParams(vmem_limit_bytes=20 * 1024 * 1024),
        cost_estimate=pl.CostEstimate(flops=1_000_000, bytes_accessed=12_000_000, transcendentals=0),
        name="cut",
    )(shard, region, *grads, *mine, *theirs)


def deposit_kernel(places, n_in, shard_ref, region_ref, *refs):
    way = direction(shard_ref[0])
    blocks, (out_ref, wide, sem) = refs[: len(places)], refs[n_in:]
    z, y = region_ref[0] // NY, region_ref[0] % NY
    copies = []
    for block, (dz, ys) in zip(blocks, places):
        for j, k in enumerate(ys):
            at = len(copies)
            wide[at] = block[4 * j : 4 * j + 4].astype(F32)
            cp = pltpu.make_async_copy(wide.at[at], out_ref.at[(z + way * dz + NZ) % NZ, (y - way * k + NY) % NY], sem.at[at])
            cp.start()
            copies.append(cp)
    for cp in copies:
        cp.wait()


def deposit(shard, region, out, items):
    places = [item[1:] for item in items]
    blocks = [item[0] for item in items]
    n, total = len(items), sum(len(item[2]) for item in items)
    hbm = pl.BlockSpec(memory_space=pltpu.HBM)
    old = [] if out is None else [out]
    return pl.pallas_call(
        functools.partial(deposit_kernel, places, n + len(old)),
        out_shape=jax.ShapeDtypeStruct((NZ, NY, 4, P_SIZE, P_SIZE), F32),
        in_specs=[pl.BlockSpec(memory_space=pltpu.SMEM)] * 2 + [pl.BlockSpec(memory_space=pltpu.VMEM)] * n + [hbm] * len(old),
        out_specs=hbm,
        input_output_aliases={n + 2: 0} if old else {},
        scratch_shapes=[pltpu.VMEM((total, 4, P_SIZE, P_SIZE), F32), pltpu.SemaphoreType.DMA((total,))],
        compiler_params=pltpu.CompilerParams(vmem_limit_bytes=16 * 1024 * 1024),
        cost_estimate=pl.CostEstimate(flops=200_000 * total, bytes_accessed=400_000 * total, transcendentals=0),
        name="deposit",
    )(shard, region, *blocks, *old)


def shift(v, axis, by):
    n = lax.axis_size(axis)
    first = axis == "x"
    place_of = (lambda core, i: i * NC + core) if first else (lambda core, i: core * n + i)
    ring = [(place_of(core, i), place_of(core, (i + (by if core == 0 else -by)) % n)) for core in range(NC) for i in range(n)]
    return lax.ppermute(v, ("x", "core") if first else ("core", axis), ring)


def swap(v):
    return lax.ppermute(v, "core", [(0, 1), (1, 0)])


def sum_along_z(slots):
    own, one, two, three, low, five, six, seven, high = slots
    three, five = shift(three, "z", 1), shift(five, "z", -1)
    low, high = shift(low, "z", 2).astype(F32), shift(high, "z", -2).astype(F32)
    three, one, seven = lax.optimization_barrier((three, one, seven))
    two, six = two + three.astype(F32), six + five.astype(F32)
    two = jnp.concatenate([two[:2] + low, two[2:]])
    six = jnp.concatenate([six[:2], six[2:] + high])
    near = shift(one, "z", 1).astype(F32) + shift(seven, "z", -1).astype(F32)
    return own + near + shift(two.astype(BF), "z", 2).astype(F32) + shift(six.astype(BF), "z", -2).astype(F32)


def spread(part, shard, region):
    far = shift(part, "y", 2)
    own = jnp.concatenate([part, far])
    ups, downs = [jnp.concatenate([shift(part, "z", by), shift(far, "z", by)]) for by in (1, -1)]
    came = [(shift(own, "y", 1), 0, (1, 3))]
    out = deposit(shard, region, None, [(own, 0, (0, 2))])
    for d in (1, 2, 3):
        ups, downs, out = lax.optimization_barrier((ups, downs, out))
        here = [(ups, -d, (0, 2)), (downs, d, (0, 2))]
        ups = shift(ups, "z", 1)
        if d < 3:
            downs = shift(downs, "z", -1)
        side = [(shift(here[0][0], "y", 1), -d, (1, 3)), (shift(here[1][0], "y", -1), d, (3, 1))]
        out = deposit(shard, region, out, here + came)
        came = side
    ups, out = lax.optimization_barrier((ups, out))
    side = shift(ups, "y", 1)
    out = deposit(shard, region, out, [(ups, -4, (0, 2))] + came)
    out = deposit(shard, region, out, [(side, -4, (1, 3))])
    return out.reshape(MAS_DEV, P_SIZE, P_SIZE)


def body(masters, inst_master, inst_row, inst_col, def_index, def_weights, kernels, target):
    shard = lax.axis_index(("x", "core")).reshape(1)
    region = lax.axis_index(("z", "y")).reshape(1)
    tmid = target[0]
    mine, theirs, info = place(shard, inst_master, inst_row, inst_col, masters, tmid)
    other = swap(theirs)
    rims = other[NX * EXT :]
    sums = [mine[d] + other[EXT * d : EXT * d + EXT].astype(F32) for d in range(NX)]
    sends = [jnp.concatenate([sums[d].astype(BF), rims]) if d == 1 else sums[d].astype(BF) for d in range(NX)]
    parts = [sums[0]] + [shift(sends[d], "x", d) for d in (1, 2, 3)]
    table = make_table(kernels)
    tmid = target[0]
    resist, grad = image(def_index, shard, def_weights, parts, rims, tmid, info, table)
    across, before, after = [shift(grad, "y", k) for k in (2, 1, 3)]
    grads = [grad, before, across, after]
    own = jnp.stack([g[:TR] for g in grads])
    up, down, far = [shift(own, "x", by) for by in (1, 3, 2)]
    bands = (own, up, down, far)
    swapped = [swap(v) for v in bands]
    part = sum_along_z(cut(shard, region, grads, bands, swapped)).astype(BF)
    return (spread(part, shard, region), resist[None])


def solution(mesh):
    fine = Mesh(mesh.devices.reshape(NX, NC, NZ, NY), ("x", "core", "z", "y"))
    master, region = ("x", "core"), ("z", "y")
    return jax.shard_map(
        body,
        mesh=fine,
        in_specs=(
            P(master, None, None),
            P(None, region, None),
            P(None, region, None),
            P(None, region, None),
            P(region),
            P(),
            P(),
            P(region, master, None),
        ),
        out_specs=(P(master, None, None), P(region, master, None)),
        check_vma=False,
    )
```

```python
import functools
import jax, jax.numpy as jnp
from jax import lax
from jax.experimental import pallas as pl
from jax.sharding import Mesh, PartitionSpec as P
from jax.experimental.pallas import tpu as pltpu

TC = 1024; TR = 48; KS = 15; KERN = 12; P_SIZE = 128; MAS_DEV = 128; INST_DEV = 16
STEEP = 1.5; THRESH = 3.0
BR, BC = 8, 16
H = 7
ROWB = 8
MROWB = ROWB + 2
COLB = TC // BC
M = ROWB * COLB
K = 6 * 128
F32, BF = jnp.float32, jnp.bfloat16
NX, NC, NY, NZ = 4, 2, 4, 8
LEAD = 16
EXT = TR + 2 * LEAD


def swap_chunks(x):
    n = x.shape[0]
    row = lax.broadcasted_iota(jnp.int32, (n, 128), 0)
    chunk = lax.broadcasted_iota(jnp.int32, (n, 128), 1) // BC

    def sub(v, k):
        return pltpu.roll(v.reshape(n // 8, 8, 128), k, 1).reshape(n, 128)

    for k in (1, 2, 4):
        rbit = (row & k) != 0
        cbit = (chunk & k) != 0
        up = sub(pltpu.roll(x, 128 - BC * k, 1), k)
        if k == 4:
            dn = up
        else:
            dn = sub(pltpu.roll(x, BC * k, 1), 8 - k)
        x = jnp.where(rbit == cbit, x, jnp.where(rbit, up, dn))
    return x


def to_blocks(x):
    a, b = x.shape[0] // 8, x.shape[1] // 128
    tiles = [x[8 * i : 8 * i + 8, 128 * t : 128 * t + 128] for i in range(a) for t in range(b)]
    return swap_chunks(jnp.concatenate(tiles, axis=0))


def from_blocks(v, a, b):
    x = swap_chunks(v)
    rows = []
    for i in range(a):
        rows.append(jnp.concatenate([x[(i * b + t) * 8 : (i * b + t) * 8 + 8] for t in range(b)], axis=1))
    return jnp.concatenate(rows, axis=0)


def table_kernel(v_ref, w_ref):
    lane = lax.broadcasted_iota(jnp.int32, (16, 512), 1) % BC
    row = lax.broadcasted_iota(jnp.int32, (16, 512), 0)
    low = lane <= row

    def one(c, carry):
        at = pl.ds(pl.multiple_of(c * 128, 128), 128)
        x = jnp.broadcast_to(v_ref[c], (16, 512))
        r = pltpu.roll(x, 1, 1, stride=1, stride_axis=0)
        for p in range(8):
            rp = pltpu.roll(r, 512 - 16 * p, 1) if p else r
            lp = jnp.where(low, rp, 0.0).astype(BF)
            hp = jnp.where(low, 0.0, rp).astype(BF)
            for wy in range(24):
                dy, yw = wy // 8, wy % 8
                if (24 - wy) % 8 == p:
                    q = (24 - wy) // 8
                    w_ref[(dy * 2) * 128 + yw * 16 : (dy * 2) * 128 + yw * 16 + 16, at] = lp[:, 128 * q : 128 * q + 128]
                if (23 - wy) % 8 == p:
                    q = (23 - wy) // 8
                    w_ref[(dy * 2 + 1) * 128 + yw * 16 : (dy * 2 + 1) * 128 + yw * 16 + 16, at] = hp[:, 128 * q : 128 * q + 128]
        return carry

    def four(i, carry):
        for j in range(4):
            one(4 * i + j, carry)
        return carry

    lax.fori_loop(0, KERN // 2, four, 0)


def taps_rows(kernels):
    k = kernels.astype(F32).reshape(2, KERN, KS, KS).swapaxes(0, 1).reshape(2 * KERN, KS, KS)
    k = k[:, ::-1, ::-1]
    k = jnp.pad(k, ((0, 0), (9, 32 - 9 - KS), (1, 0)))
    return k.reshape(2 * KERN, 1, 512)


def make_table(kernels):
    return pl.pallas_call(
        table_kernel,
        out_shape=jax.ShapeDtypeStruct((K, 2 * KERN * 128), BF),
        in_specs=[pl.BlockSpec(memory_space=pltpu.VMEM)],
        out_specs=pl.BlockSpec(memory_space=pltpu.VMEM),
        compiler_params=pltpu.CompilerParams(vmem_limit_bytes=32 * 1024 * 1024),
        cost_estimate=pl.CostEstimate(flops=20_000_000, bytes_accessed=10_000_000, transcendentals=0),
        name="taps_table",
    )(taps_rows(kernels))


def image_kernel(level_ref, shard_ref, wgt_ref, m0_ref, m1_ref, m2_ref, m3_ref, rims_ref, tmid_ref, info_ref, w_ref,
                 resist_ref, grad_ref, lhs_ref, fields_ref, cot_ref):
    level_at = level_ref[0]
    m1 = m1_ref[...].astype(F32)
    x = m0_ref[...] + m1[:EXT] + m2_ref[...].astype(F32) + m3_ref[...].astype(F32)
    x = x.astype(BF).astype(F32)
    x = pltpu.roll(x, 8 * MROWB - 1, 0)
    x = jnp.concatenate([x, jnp.zeros((8 * MROWB, 128), F32)], axis=1)
    x = pltpu.roll(x, H, 1)
    mb = to_blocks(x).reshape(MROWB, 72, 128)
    for dy in range(3):
        for dx in range(2):
            part = mb[dy : dy + ROWB, dx : dx + COLB, :]
            lhs_ref[:, (dy * 2 + dx) * 128 : (dy * 2 + dx) * 128 + 128] = part.reshape(M, 128).astype(BF)
    intensity = jnp.zeros((M, 128), F32)
    for c in range(KERN):
        f = jnp.dot(lhs_ref[...], w_ref[:, c * 256 : c * 256 + 256], preferred_element_type=F32)
        fields_ref[c] = f
        f = f * f
        intensity = intensity + wgt_ref[level_at, c] * (f[:, :128] + f[:, 128:])
    level = 1.0 / (1.0 + jnp.exp(-STEEP * (intensity - THRESH)))
    resist_ref[...] = from_blocks(level, ROWB, 8)[8 : 8 + TR].astype(BF)
    rims = rims_ref[...].astype(F32)
    first = shard_ref[0] % NC == 0
    above = jnp.where(first, m1[EXT + 8 :], rims[8:])
    below = jnp.where(first, rims[:8], m1[EXT : EXT + 8])
    goal = jnp.concatenate([above, tmid_ref[...].astype(F32), below], axis=0)
    goal = to_blocks(goal)
    slope = STEEP * (level - goal) * level * (1.0 - level)
    row_block = lax.broadcasted_iota(jnp.int32, (M, 128), 0) // COLB
    in_block = lax.broadcasted_iota(jnp.int32, (M, 128), 1) // BC
    at = shard_ref[0] * TR - 8 + row_block * 8 + in_block
    slope = jnp.where((at >= 0) & (at < 8 * TR), slope, 0.0)
    for c in range(KERN):
        s = 2.0 * wgt_ref[level_at, c] * slope
        cot_ref[:, c * 256 : c * 256 + 256] = (jnp.concatenate([s, s], axis=1) * fields_ref[c]).astype(BF)
    out = [None] * 7
    for dy in range(3):
        acc = lax.dot_general(cot_ref[...], w_ref[dy * 256 : dy * 256 + 256, :], (((1,), (1,)), ((), ())), preferred_element_type=F32)
        for dx in range(2):
            for i in range(ROWB):
                j = i + dy
                if 1 <= j <= 7:
                    piece = acc[i * COLB : i * COLB + COLB, dx * 128 : dx * 128 + 128]
                    piece = jnp.concatenate([piece, jnp.zeros((8, 128), F32)], axis=0)
                    if dx:
                        piece = pltpu.roll(piece, 1, 0)
                    out[j - 1] = piece if out[j - 1] is None else out[j - 1] + piece
    nat = from_blocks(jnp.concatenate(out, axis=0), 7, 9)
    nat = pltpu.roll(nat, 9 * 128 - H, 1)
    grad_ref[:TR] = nat[H : H + TR, :TC].astype(BF)
    info = jnp.broadcast_to(info_ref[...], (16, 128))
    row = lax.broadcasted_iota(jnp.int32, (16, 128), 0)
    digits = jnp.where(row == 0, info >> 7, jnp.where(row == 1, info & 127, 0)).astype(F32)
    grad_ref[TR:] = jnp.concatenate([digits, jnp.zeros((16, TC - 128), F32)], axis=1).astype(BF)


def image(level, shard, weights, parts, rims, tmid, info, table):
    vm = pl.BlockSpec(memory_space=pltpu.VMEM)
    sm = pl.BlockSpec(memory_space=pltpu.SMEM)
    return pl.pallas_call(
        image_kernel,
        out_shape=(jax.ShapeDtypeStruct((TR, TC), BF), jax.ShapeDtypeStruct((TR + 16, TC), BF)),
        in_specs=[sm] * 3 + [vm] * 8,
        out_specs=(vm, vm),
        scratch_shapes=[pltpu.VMEM((M, K), BF), pltpu.VMEM((KERN, M, 256), F32), pltpu.VMEM((M, 2 * KERN * 128), BF)],
        compiler_params=pltpu.CompilerParams(vmem_limit_bytes=28 * 1024 * 1024),
        cost_estimate=pl.CostEstimate(flops=5_000_000_000, bytes_accessed=8_000_000, transcendentals=65536),
        name="image",
    )(level, shard, weights, *parts, rims, tmid, info, table)


WIDE = TC + 128
INFO = 128


def direction(shard):
    return 1 - 2 * (shard % NC)


PLACE_GRANT = 56


def place_kernel(shard_ref, ids_hbm, rows_hbm, cols_hbm, masters_hbm, target_hbm, mine_ref, theirs_ref, info_ref, scalars, panels, canvas, goal_buf, sem, info_sem, rim_sem):
    shard = shard_ref[0]
    loads = [pltpu.make_async_copy(ref.at[shard], scalars.at[j], info_sem.at[j]) for j, ref in enumerate((ids_hbm, rows_hbm, cols_hbm))]
    rim_load = pltpu.make_async_copy(target_hbm, goal_buf, rim_sem)
    for cp in loads + [rim_load]:
        cp.start()
    for cp in loads:
        cp.wait()
    copies = []
    for i in range(INST_DEV):
        cp = pltpu.make_async_copy(masters_hbm.at[scalars[0, 0, i]], panels.at[i], sem.at[i])
        cp.start()
        copies.append(cp)
        for j in range(3):
            info_ref[0, j * INST_DEV + i] = scalars[j, 0, i]
    for i in range(3 * INST_DEV, INFO):
        info_ref[0, i] = 0
    canvas[...] = jnp.zeros(canvas.shape, F32)
    lane = lax.broadcasted_iota(jnp.int32, (P_SIZE, 128), 1)
    sub = lax.broadcasted_iota(jnp.int32, (P_SIZE // 8 + 1, 8, 256), 1)
    none = jnp.zeros((1, 8, 256), F32)
    for i in range(INST_DEV):
        copies[i].wait()
        p = panels[i].astype(BF).astype(F32)
        c = scalars[2, 0, i]
        c0 = (c // 128) * 128
        d = c - c0
        p = pltpu.roll(p, d, 1)
        left = jnp.where(lane >= d, p, 0.0)
        right = jnp.where(lane >= d, 0.0, p)
        r = scalars[1, 0, i] + LEAD
        r0 = (r // 8) * 8
        full = jnp.concatenate([left, right], axis=1).reshape(P_SIZE // 8, 8, 256)
        full = pltpu.roll(full, r - r0, 1)
        full = jnp.where(sub >= r - r0, jnp.concatenate([full, none], axis=0), jnp.concatenate([none, full], axis=0))
        full = full.reshape(P_SIZE + 8, 256)
        at = (pl.ds(pl.multiple_of(r0, 8), P_SIZE + 8), pl.ds(pl.multiple_of(c0, 128), 256))
        canvas[at] = canvas[at] + full
    core = shard % NC
    way = direction(shard)
    for d in range(NX):
        x = (shard // NC + way * d + NX) % NX
        mine_ref[d] = canvas[pl.ds(pl.multiple_of((x * NC + core) * TR, 8), EXT), :TC]
        x = (shard // NC - way * d + NX) % NX
        theirs_ref[EXT * d : EXT * d + EXT] = canvas[pl.ds(pl.multiple_of((x * NC + 1 - core) * TR, 8), EXT), :TC].astype(BF)
    rim_load.wait()
    goal = goal_buf[...].astype(F32)
    theirs_ref[EXT * NX :] = jnp.concatenate([goal[:8], goal[TR - 8 :]], axis=0).astype(BF)


def place(shard, ids, rows, cols, masters, target):
    vm = pl.BlockSpec(memory_space=pltpu.VMEM)
    sm = pl.BlockSpec(memory_space=pltpu.SMEM)
    hbm = pl.BlockSpec(memory_space=pltpu.HBM)
    bands = (NX, EXT, TC)
    return pl.pallas_call(
        place_kernel,
        out_shape=(jax.ShapeDtypeStruct(bands, F32), jax.ShapeDtypeStruct((NX * EXT + 16, TC), BF), jax.ShapeDtypeStruct((1, INFO), jnp.int32)),
        in_specs=[sm] + [hbm] * 5,
        out_specs=(vm, vm, sm),
        scratch_shapes=[
            pltpu.SMEM((3, 1, INST_DEV), jnp.int32),
            pltpu.VMEM((INST_DEV, P_SIZE, P_SIZE), F32),
            pltpu.VMEM((LEAD + 8 * TR + LEAD, WIDE), F32),
            pltpu.VMEM((TR, TC), BF),
            pltpu.SemaphoreType.DMA((INST_DEV,)),
            pltpu.SemaphoreType.DMA((3,)),
            pltpu.SemaphoreType.DMA,
        ],
        compiler_params=pltpu.CompilerParams(vmem_limit_bytes=PLACE_GRANT * 1024 * 1024),
        cost_estimate=pl.CostEstimate(flops=1_000_000, bytes_accessed=12_000_000, transcendentals=0),
        name="place",
    )(shard, ids, rows, cols, masters, target)


def cut_kernel(shard_ref, region_ref, g0, g1, g2, g3, *rest):
    mine, theirs, rest = rest[:4], rest[4:8], rest[8:]
    outs, (canvas, sums, digits, lists, list_sem) = rest[: NZ + 1], rest[NZ + 1 :]
    digits[...] = jnp.zeros(digits.shape, jnp.int32)
    for k, g in enumerate((g0, g1, g2, g3)):
        tile = g[TR:, :128].astype(F32)
        digits[k : k + 1] = (tile[0:1] * 128.0 + tile[1:2]).astype(jnp.int32)
    load = pltpu.make_async_copy(digits, lists, list_sem)
    load.start()
    x = shard_ref[0] // NC + NX
    z, y = region_ref[0] // NY, region_ref[0] % NY
    sums[...] = jnp.zeros(sums.shape, F32)

    core = shard_ref[0] % NC
    for refs, c in ((mine, core), (theirs, 1 - core)):
        way = direction(c)
        for ref, n in zip(refs, (0, -way, way, 2)):
            row = pl.multiple_of(((x + n) % NX * NC + c) * TR, 8)
            for k in range(NY):
                band = ref[c, k] if len(ref.shape) == 4 else ref[k]
                canvas[(NY - way * k) % NY, pl.ds(row, TR), :TC] = band.astype(F32)
    load.wait()
    sub = lax.broadcasted_iota(jnp.int32, (P_SIZE // 8, 8, 128), 1)
    way = direction(shard_ref[0])
    for k in range(NY):
        tile = (NY - way * k) % NY

        def one(i, carry, k=k, tile=tile):
            m = lists[k, i]

            @pl.when((m // 4) % NY == y)
            def _():
                r, c = lists[k, INST_DEV + i], lists[k, 2 * INST_DEV + i]
                r0, c0 = (r // 8) * 8, (c // 128) * 128
                full = canvas[tile, pl.ds(pl.multiple_of(r0, 8), P_SIZE + 8), pl.ds(pl.multiple_of(c0, 128), 256)]
                full = pltpu.roll(full, 256 - (c - c0), 1)[:, :128]
                full = pltpu.roll(full.reshape(P_SIZE // 8 + 1, 8, 128), 8 - (r - r0), 1)
                full = jnp.where(sub < 8 - (r - r0), full[:-1], full[1:]).reshape(P_SIZE, 128)
                slot = (way * (m // 16 - z) + NZ) % NZ
                sums[slot, m % 4] = sums[slot, m % 4] + full

            return carry

        lax.fori_loop(0, INST_DEV, one, 0)
    for d in range(NZ):
        if d == 4:
            outs[4][...] = sums[4, :2].astype(BF)
            outs[NZ][...] = sums[4, 2:].astype(BF)
        else:
            outs[d][...] = sums[d].astype(outs[d].dtype)


def cut(shard, region, grads, mine, theirs):
    vm = pl.BlockSpec(memory_space=pltpu.VMEM)
    sm = pl.BlockSpec(memory_space=pltpu.SMEM)
    slot = (4, P_SIZE, P_SIZE)
    half = jax.ShapeDtypeStruct((2, P_SIZE, P_SIZE), BF)
    return pl.pallas_call(
        cut_kernel,
        out_shape=[jax.ShapeDtypeStruct(slot, F32 if d in (0, 2, 6) else BF) if d != 4 else half for d in range(NZ)] + [half],
        in_specs=[sm] * 2 + [vm] * 12,
        out_specs=[vm] * (NZ + 1),
        scratch_shapes=[
            pltpu.VMEM((NY, 8 * TR + 8, WIDE), F32),
            pltpu.VMEM((NZ, 4, P_SIZE, P_SIZE), F32),
            pltpu.VMEM((8, 128), jnp.int32),
            pltpu.SMEM((8, 128), jnp.int32),
            pltpu.SemaphoreType.DMA,
        ],
        compiler_params=pltpu.CompilerParams(vmem_limit_bytes=20 * 1024 * 1024),
        cost_estimate=pl.CostEstimate(flops=1_000_000, bytes_accessed=12_000_000, transcendentals=0),
        name="cut",
    )(shard, region, *grads, *mine, *theirs)


def deposit_kernel(places, n_in, shard_ref, region_ref, *refs):
    way = direction(shard_ref[0])
    blocks, (out_ref, wide, sem) = refs[: len(places)], refs[n_in:]
    z, y = region_ref[0] // NY, region_ref[0] % NY
    copies = []
    for block, (dz, ys) in zip(blocks, places):
        for j, k in enumerate(ys):
            at = len(copies)
            wide[at] = block[4 * j : 4 * j + 4].astype(F32)
            cp = pltpu.make_async_copy(wide.at[at], out_ref.at[(z + way * dz + NZ) % NZ, (y - way * k + NY) % NY], sem.at[at])
            cp.start()
            copies.append(cp)
    for cp in copies:
        cp.wait()


def deposit(shard, region, out, items):
    places = [item[1:] for item in items]
    blocks = [item[0] for item in items]
    n, total = len(items), sum(len(item[2]) for item in items)
    hbm = pl.BlockSpec(memory_space=pltpu.HBM)
    old = [] if out is None else [out]
    return pl.pallas_call(
        functools.partial(deposit_kernel, places, n + len(old)),
        out_shape=jax.ShapeDtypeStruct((NZ, NY, 4, P_SIZE, P_SIZE), F32),
        in_specs=[pl.BlockSpec(memory_space=pltpu.SMEM)] * 2 + [pl.BlockSpec(memory_space=pltpu.VMEM)] * n + [hbm] * len(old),
        out_specs=hbm,
        input_output_aliases={n + 2: 0} if old else {},
        scratch_shapes=[pltpu.VMEM((total, 4, P_SIZE, P_SIZE), F32), pltpu.SemaphoreType.DMA((total,))],
        compiler_params=pltpu.CompilerParams(vmem_limit_bytes=16 * 1024 * 1024),
        cost_estimate=pl.CostEstimate(flops=200_000 * total, bytes_accessed=400_000 * total, transcendentals=0),
        name="deposit",
    )(shard, region, *blocks, *old)


def shift(v, axis, by):
    n = lax.axis_size(axis)
    first = axis == "x"
    place_of = (lambda core, i: i * NC + core) if first else (lambda core, i: core * n + i)
    ring = [(place_of(core, i), place_of(core, (i + (by if core == 0 else -by)) % n)) for core in range(NC) for i in range(n)]
    return lax.ppermute(v, ("x", "core") if first else ("core", axis), ring)


def swap(v):
    return lax.ppermute(v, "core", [(0, 1), (1, 0)])


def sum_along_z(slots):
    own, one, two, three, low, five, six, seven, high = slots
    three, five = shift(three, "z", 1), shift(five, "z", -1)
    low, high = shift(low, "z", 2).astype(F32), shift(high, "z", -2).astype(F32)
    three, one, seven = lax.optimization_barrier((three, one, seven))
    two, six = two + three.astype(F32), six + five.astype(F32)
    two = jnp.concatenate([two[:2] + low, two[2:]])
    six = jnp.concatenate([six[:2], six[2:] + high])
    near = shift(one, "z", 1).astype(F32) + shift(seven, "z", -1).astype(F32)
    return own + near + shift(two.astype(BF), "z", 2).astype(F32) + shift(six.astype(BF), "z", -2).astype(F32)


def spread(part, shard, region):
    far = shift(part, "y", 2)
    own = jnp.concatenate([part, far])
    ups, downs = [jnp.concatenate([shift(part, "z", by), shift(far, "z", by)]) for by in (1, -1)]
    came = [(shift(own, "y", 1), 0, (1, 3))]
    out = deposit(shard, region, None, [(own, 0, (0, 2))])
    for d in (1, 2, 3):
        ups, downs, out = lax.optimization_barrier((ups, downs, out))
        here = [(ups, -d, (0, 2)), (downs, d, (0, 2))]
        ups = shift(ups, "z", 1)
        if d < 3:
            downs = shift(downs, "z", -1)
        side = [(shift(here[0][0], "y", 1), -d, (1, 3)), (shift(here[1][0], "y", -1), d, (3, 1))]
        out = deposit(shard, region, out, here + came)
        came = side
    ups, out = lax.optimization_barrier((ups, out))
    side = shift(ups, "y", 1)
    out = deposit(shard, region, out, [(ups, -4, (0, 2))] + came)
    out = deposit(shard, region, out, [(side, -4, (1, 3))])
    return out.reshape(MAS_DEV, P_SIZE, P_SIZE)


def body(masters, inst_master, inst_row, inst_col, def_index, def_weights, kernels, target):
    shard = lax.axis_index(("x", "core")).reshape(1)
    region = lax.axis_index(("z", "y")).reshape(1)
    tmid = target[0]
    mine, theirs, info = place(shard, inst_master, inst_row, inst_col, masters, tmid)
    other = swap(theirs)
    rims = other[NX * EXT :]
    sums = [mine[d] + other[EXT * d : EXT * d + EXT].astype(F32) for d in range(NX)]
    sends = [jnp.concatenate([sums[d].astype(BF), rims]) if d == 1 else sums[d].astype(BF) for d in range(NX)]
    parts = [sums[0]] + [shift(sends[d], "x", d) for d in (1, 2, 3)]
    table = make_table(kernels)
    tmid = target[0]
    resist, grad = image(def_index, shard, def_weights, parts, rims, tmid, info, table)
    across, before, after = [shift(grad, "y", k) for k in (2, 1, 3)]
    grads = [grad, before, across, after]
    own = jnp.stack([g[:TR] for g in grads])
    up, down, far = [shift(own, "x", by) for by in (1, 3, 2)]
    bands = (own, up, down, far)
    swapped = [lax.all_gather(own, "core")] + [swap(v) for v in (up, down, far)]
    part = sum_along_z(cut(shard, region, grads, bands, swapped)).astype(BF)
    return (spread(part, shard, region), resist[None])


def solution(mesh):
    fine = Mesh(mesh.devices.reshape(NX, NC, NZ, NY), ("x", "core", "z", "y"))
    master, region = ("x", "core"), ("z", "y")
    return jax.shard_map(
        body,
        mesh=fine,
        in_specs=(
            P(master, None, None),
            P(None, region, None),
            P(None, region, None),
            P(None, region, None),
            P(region),
            P(),
            P(),
            P(region, master, None),
        ),
        out_specs=(P(master, None, None), P(region, master, None)),
        check_vma=False,
    )
```

```python
import functools
import jax, jax.numpy as jnp
from jax import lax
from jax.experimental import pallas as pl
from jax.sharding import Mesh, PartitionSpec as P
from jax.experimental.pallas import tpu as pltpu

TC = 1024; TR = 48; KS = 15; KERN = 12; P_SIZE = 128; MAS_DEV = 128; INST_DEV = 16
STEEP = 1.5; THRESH = 3.0
BR, BC = 8, 16
H = 7
ROWB = 8
MROWB = ROWB + 2
COLB = TC // BC
M = ROWB * COLB
K = 6 * 128
F32, BF = jnp.float32, jnp.bfloat16
NX, NC, NY, NZ = 4, 2, 4, 8
LEAD = 16
EXT = TR + 2 * LEAD


def swap_chunks(x):
    n = x.shape[0]
    row = lax.broadcasted_iota(jnp.int32, (n, 128), 0)
    chunk = lax.broadcasted_iota(jnp.int32, (n, 128), 1) // BC

    def sub(v, k):
        return pltpu.roll(v.reshape(n // 8, 8, 128), k, 1).reshape(n, 128)

    for k in (1, 2, 4):
        rbit = (row & k) != 0
        cbit = (chunk & k) != 0
        up = sub(pltpu.roll(x, 128 - BC * k, 1), k)
        if k == 4:
            dn = up
        else:
            dn = sub(pltpu.roll(x, BC * k, 1), 8 - k)
        x = jnp.where(rbit == cbit, x, jnp.where(rbit, up, dn))
    return x


def to_blocks(x):
    a, b = x.shape[0] // 8, x.shape[1] // 128
    tiles = [x[8 * i : 8 * i + 8, 128 * t : 128 * t + 128] for i in range(a) for t in range(b)]
    return swap_chunks(jnp.concatenate(tiles, axis=0))


def from_blocks(v, a, b):
    x = swap_chunks(v)
    rows = []
    for i in range(a):
        rows.append(jnp.concatenate([x[(i * b + t) * 8 : (i * b + t) * 8 + 8] for t in range(b)], axis=1))
    return jnp.concatenate(rows, axis=0)


def table_kernel(v_ref, w_ref):
    lane = lax.broadcasted_iota(jnp.int32, (16, 512), 1) % BC
    row = lax.broadcasted_iota(jnp.int32, (16, 512), 0)
    low = lane <= row

    def one(c, carry):
        at = pl.ds(pl.multiple_of(c * 128, 128), 128)
        x = jnp.broadcast_to(v_ref[c], (16, 512))
        r = pltpu.roll(x, 1, 1, stride=1, stride_axis=0)
        for p in range(8):
            rp = pltpu.roll(r, 512 - 16 * p, 1) if p else r
            lp = jnp.where(low, rp, 0.0).astype(BF)
            hp = jnp.where(low, 0.0, rp).astype(BF)
            for wy in range(24):
                dy, yw = wy // 8, wy % 8
                if (24 - wy) % 8 == p:
                    q = (24 - wy) // 8
                    w_ref[(dy * 2) * 128 + yw * 16 : (dy * 2) * 128 + yw * 16 + 16, at] = lp[:, 128 * q : 128 * q + 128]
                if (23 - wy) % 8 == p:
                    q = (23 - wy) // 8
                    w_ref[(dy * 2 + 1) * 128 + yw * 16 : (dy * 2 + 1) * 128 + yw * 16 + 16, at] = hp[:, 128 * q : 128 * q + 128]
        return carry

    def four(i, carry):
        for j in range(4):
            one(4 * i + j, carry)
        return carry

    lax.fori_loop(0, KERN // 2, four, 0)


def taps_rows(kernels):
    k = kernels.astype(F32).reshape(2, KERN, KS, KS).swapaxes(0, 1).reshape(2 * KERN, KS, KS)
    k = k[:, ::-1, ::-1]
    k = jnp.pad(k, ((0, 0), (9, 32 - 9 - KS), (1, 0)))
    return k.reshape(2 * KERN, 1, 512)


def make_table(kernels):
    return pl.pallas_call(
        table_kernel,
        out_shape=jax.ShapeDtypeStruct((K, 2 * KERN * 128), BF),
        in_specs=[pl.BlockSpec(memory_space=pltpu.VMEM)],
        out_specs=pl.BlockSpec(memory_space=pltpu.VMEM),
        compiler_params=pltpu.CompilerParams(vmem_limit_bytes=32 * 1024 * 1024),
        cost_estimate=pl.CostEstimate(flops=20_000_000, bytes_accessed=10_000_000, transcendentals=0),
        name="taps_table",
    )(taps_rows(kernels))


def image_kernel(level_ref, shard_ref, wgt_ref, m0_ref, m1_ref, m2_ref, m3_ref, rims_ref, tmid_ref, info_ref, w_ref,
                 resist_ref, grad_ref, lhs_ref, fields_ref, cot_ref):
    level_at = level_ref[0]
    m1 = m1_ref[...].astype(F32)
    x = m0_ref[...] + m1[:EXT] + m2_ref[...].astype(F32) + m3_ref[...].astype(F32)
    x = x.astype(BF).astype(F32)
    x = pltpu.roll(x, 8 * MROWB - 1, 0)
    x = jnp.concatenate([x, jnp.zeros((8 * MROWB, 128), F32)], axis=1)
    x = pltpu.roll(x, H, 1)
    mb = to_blocks(x).reshape(MROWB, 72, 128)
    for dy in range(3):
        for dx in range(2):
            part = mb[dy : dy + ROWB, dx : dx + COLB, :]
            lhs_ref[:, (dy * 2 + dx) * 128 : (dy * 2 + dx) * 128 + 128] = part.reshape(M, 128).astype(BF)
    intensity = jnp.zeros((M, 128), F32)

    def expose(i, intensity):
        for j in range(4):
            c = 4 * i + j
            f = jnp.dot(lhs_ref[...], w_ref[:, pl.ds(pl.multiple_of(c * 256, 256), 256)], preferred_element_type=F32)
            fields_ref[c] = f
            f = f * f
            intensity = intensity + wgt_ref[level_at, c] * (f[:, :128] + f[:, 128:])
        return intensity

    intensity = lax.fori_loop(0, KERN // 4, expose, intensity)
    level = 1.0 / (1.0 + jnp.exp(-STEEP * (intensity - THRESH)))
    resist_ref[...] = from_blocks(level, ROWB, 8)[8 : 8 + TR].astype(BF)
    rims = rims_ref[...].astype(F32)
    first = shard_ref[0] % NC == 0
    above = jnp.where(first, m1[EXT + 8 :], rims[8:])
    below = jnp.where(first, rims[:8], m1[EXT : EXT + 8])
    goal = jnp.concatenate([above, tmid_ref[...].astype(F32), below], axis=0)
    goal = to_blocks(goal)
    slope = STEEP * (level - goal) * level * (1.0 - level)
    row_block = lax.broadcasted_iota(jnp.int32, (M, 128), 0) // COLB
    in_block = lax.broadcasted_iota(jnp.int32, (M, 128), 1) // BC
    at = shard_ref[0] * TR - 8 + row_block * 8 + in_block
    slope = jnp.where((at >= 0) & (at < 8 * TR), slope, 0.0)

    def weigh(c, carry):
        s = 2.0 * wgt_ref[level_at, c] * slope
        cot_ref[:, pl.ds(pl.multiple_of(c * 256, 256), 256)] = (jnp.concatenate([s, s], axis=1) * fields_ref[c]).astype(BF)
        return carry

    lax.fori_loop(0, KERN, weigh, 0)
    out = [None] * 7
    for dy in range(3):
        acc = lax.dot_general(cot_ref[...], w_ref[dy * 256 : dy * 256 + 256, :], (((1,), (1,)), ((), ())), preferred_element_type=F32)
        for dx in range(2):
            for i in range(ROWB):
                j = i + dy
                if 1 <= j <= 7:
                    piece = acc[i * COLB : i * COLB + COLB, dx * 128 : dx * 128 + 128]
                    piece = jnp.concatenate([piece, jnp.zeros((8, 128), F32)], axis=0)
                    if dx:
                        piece = pltpu.roll(piece, 1, 0)
                    out[j - 1] = piece if out[j - 1] is None else out[j - 1] + piece
    nat = from_blocks(jnp.concatenate(out, axis=0), 7, 9)
    nat = pltpu.roll(nat, 9 * 128 - H, 1)
    grad_ref[:TR] = nat[H : H + TR, :TC].astype(BF)
    info = jnp.broadcast_to(info_ref[...], (16, 128))
    row = lax.broadcasted_iota(jnp.int32, (16, 128), 0)
    digits = jnp.where(row == 0, info >> 7, jnp.where(row == 1, info & 127, 0)).astype(F32)
    grad_ref[TR:] = jnp.concatenate([digits, jnp.zeros((16, TC - 128), F32)], axis=1).astype(BF)


def image(level, shard, weights, parts, rims, tmid, info, table):
    vm = pl.BlockSpec(memory_space=pltpu.VMEM)
    sm = pl.BlockSpec(memory_space=pltpu.SMEM)
    return pl.pallas_call(
        image_kernel,
        out_shape=(jax.ShapeDtypeStruct((TR, TC), BF), jax.ShapeDtypeStruct((TR + 16, TC), BF)),
        in_specs=[sm] * 3 + [vm] * 8,
        out_specs=(vm, vm),
        scratch_shapes=[pltpu.VMEM((M, K), BF), pltpu.VMEM((KERN, M, 256), F32), pltpu.VMEM((M, 2 * KERN * 128), BF)],
        compiler_params=pltpu.CompilerParams(vmem_limit_bytes=28 * 1024 * 1024),
        cost_estimate=pl.CostEstimate(flops=5_000_000_000, bytes_accessed=8_000_000, transcendentals=65536),
        name="image",
    )(level, shard, weights, *parts, rims, tmid, info, table)


WIDE = TC + 128
INFO = 128


def direction(shard):
    return 1 - 2 * (shard % NC)


PLACE_GRANT = 56


def place_kernel(shard_ref, ids_hbm, rows_hbm, cols_hbm, masters_hbm, target_hbm, mine_ref, theirs_ref, info_ref, scalars, panels, canvas, goal_buf, sem, info_sem, rim_sem):
    shard = shard_ref[0]
    loads = [pltpu.make_async_copy(ref.at[shard], scalars.at[j], info_sem.at[j]) for j, ref in enumerate((ids_hbm, rows_hbm, cols_hbm))]
    rim_load = pltpu.make_async_copy(target_hbm, goal_buf, rim_sem)
    for cp in loads + [rim_load]:
        cp.start()
    for cp in loads:
        cp.wait()
    copies = []
    for i in range(INST_DEV):
        cp = pltpu.make_async_copy(masters_hbm.at[scalars[0, 0, i]], panels.at[i], sem.at[i])
        cp.start()
        copies.append(cp)
        for j in range(3):
            info_ref[0, j * INST_DEV + i] = scalars[j, 0, i]

    def clear(i, carry):
        info_ref[0, i] = 0
        return carry

    lax.fori_loop(3 * INST_DEV, INFO, clear, 0)
    canvas[...] = jnp.zeros(canvas.shape, F32)
    lane = lax.broadcasted_iota(jnp.int32, (P_SIZE, 128), 1)
    sub = lax.broadcasted_iota(jnp.int32, (P_SIZE // 8 + 1, 8, 256), 1)
    none = jnp.zeros((1, 8, 256), F32)
    def put(i, carry):
        pltpu.make_async_copy(masters_hbm.at[scalars[0, 0, i]], panels.at[i], sem.at[i]).wait()
        p = panels[i].astype(BF).astype(F32)
        c = scalars[2, 0, i]
        c0 = (c // 128) * 128
        d = c - c0
        p = pltpu.roll(p, d, 1)
        left = jnp.where(lane >= d, p, 0.0)
        right = jnp.where(lane >= d, 0.0, p)
        r = scalars[1, 0, i] + LEAD
        r0 = (r // 8) * 8
        full = jnp.concatenate([left, right], axis=1).reshape(P_SIZE // 8, 8, 256)
        full = pltpu.roll(full, r - r0, 1)
        full = jnp.where(sub >= r - r0, jnp.concatenate([full, none], axis=0), jnp.concatenate([none, full], axis=0))
        full = full.reshape(P_SIZE + 8, 256)
        at = (pl.ds(pl.multiple_of(r0, 8), P_SIZE + 8), pl.ds(pl.multiple_of(c0, 128), 256))
        canvas[at] = canvas[at] + full
        return carry

    lax.fori_loop(0, INST_DEV, put, 0)
    core = shard % NC
    way = direction(shard)
    for d in range(NX):
        x = (shard // NC + way * d + NX) % NX
        mine_ref[d] = canvas[pl.ds(pl.multiple_of((x * NC + core) * TR, 8), EXT), :TC]
        x = (shard // NC - way * d + NX) % NX
        theirs_ref[EXT * d : EXT * d + EXT] = canvas[pl.ds(pl.multiple_of((x * NC + 1 - core) * TR, 8), EXT), :TC].astype(BF)
    rim_load.wait()
    goal = goal_buf[...].astype(F32)
    theirs_ref[EXT * NX :] = jnp.concatenate([goal[:8], goal[TR - 8 :]], axis=0).astype(BF)


def place(shard, ids, rows, cols, masters, target):
    vm = pl.BlockSpec(memory_space=pltpu.VMEM)
    sm = pl.BlockSpec(memory_space=pltpu.SMEM)
    hbm = pl.BlockSpec(memory_space=pltpu.HBM)
    bands = (NX, EXT, TC)
    return pl.pallas_call(
        place_kernel,
        out_shape=(jax.ShapeDtypeStruct(bands, F32), jax.ShapeDtypeStruct((NX * EXT + 16, TC), BF), jax.ShapeDtypeStruct((1, INFO), jnp.int32)),
        in_specs=[sm] + [hbm] * 5,
        out_specs=(vm, vm, sm),
        scratch_shapes=[
            pltpu.SMEM((3, 1, INST_DEV), jnp.int32),
            pltpu.VMEM((INST_DEV, P_SIZE, P_SIZE), F32),
            pltpu.VMEM((LEAD + 8 * TR + LEAD, WIDE), F32),
            pltpu.VMEM((TR, TC), BF),
            pltpu.SemaphoreType.DMA((INST_DEV,)),
            pltpu.SemaphoreType.DMA((3,)),
            pltpu.SemaphoreType.DMA,
        ],
        compiler_params=pltpu.CompilerParams(vmem_limit_bytes=PLACE_GRANT * 1024 * 1024),
        cost_estimate=pl.CostEstimate(flops=1_000_000, bytes_accessed=12_000_000, transcendentals=0),
        name="place",
    )(shard, ids, rows, cols, masters, target)


def cut_kernel(shard_ref, region_ref, g0, g1, g2, g3, *rest):
    mine, theirs, rest = rest[:4], rest[4:8], rest[8:]
    outs, (canvas, sums, digits, lists, list_sem) = rest[: NZ + 1], rest[NZ + 1 :]
    digits[...] = jnp.zeros(digits.shape, jnp.int32)
    for k, g in enumerate((g0, g1, g2, g3)):
        tile = g[TR:, :128].astype(F32)
        digits[k : k + 1] = (tile[0:1] * 128.0 + tile[1:2]).astype(jnp.int32)
    load = pltpu.make_async_copy(digits, lists, list_sem)
    load.start()
    x = shard_ref[0] // NC + NX
    z, y = region_ref[0] // NY, region_ref[0] % NY
    sums[...] = jnp.zeros(sums.shape, F32)

    core = shard_ref[0] % NC
    for refs, c in ((mine, core), (theirs, 1 - core)):
        way = direction(c)
        for ref, n in zip(refs, (0, -way, way, 2)):
            row = pl.multiple_of(((x + n) % NX * NC + c) * TR, 8)

            def lay(k, carry, ref=ref, row=row, way=way):
                canvas[(NY - way * k) % NY, pl.ds(row, TR), :TC] = ref[k].astype(F32)
                return carry

            lax.fori_loop(0, NY, lay, 0)
    load.wait()
    sub = lax.broadcasted_iota(jnp.int32, (P_SIZE // 8, 8, 128), 1)
    way = direction(shard_ref[0])
    def one(n, carry):
        k, i = n // INST_DEV, n % INST_DEV
        tile = (NY - way * k) % NY
        m = lists[k, i]

        @pl.when((m // 4) % NY == y)
        def _():
            r, c = lists[k, INST_DEV + i], lists[k, 2 * INST_DEV + i]
            r0, c0 = (r // 8) * 8, (c // 128) * 128
            full = canvas[tile, pl.ds(pl.multiple_of(r0, 8), P_SIZE + 8), pl.ds(pl.multiple_of(c0, 128), 256)]
            full = pltpu.roll(full, 256 - (c - c0), 1)[:, :128]
            full = pltpu.roll(full.reshape(P_SIZE // 8 + 1, 8, 128), 8 - (r - r0), 1)
            full = jnp.where(sub < 8 - (r - r0), full[:-1], full[1:]).reshape(P_SIZE, 128)
            slot = (way * (m // 16 - z) + NZ) % NZ
            sums[slot, m % 4] = sums[slot, m % 4] + full

        return carry

    lax.fori_loop(0, NY * INST_DEV, one, 0)
    for d in range(NZ):
        if d == 4:
            outs[4][...] = sums[4, :2].astype(BF)
            outs[NZ][...] = sums[4, 2:].astype(BF)
        else:
            outs[d][...] = sums[d].astype(outs[d].dtype)


def cut(shard, region, grads, mine, theirs):
    vm = pl.BlockSpec(memory_space=pltpu.VMEM)
    sm = pl.BlockSpec(memory_space=pltpu.SMEM)
    slot = (4, P_SIZE, P_SIZE)
    half = jax.ShapeDtypeStruct((2, P_SIZE, P_SIZE), BF)
    return pl.pallas_call(
        cut_kernel,
        out_shape=[jax.ShapeDtypeStruct(slot, F32 if d in (0, 2, 6) else BF) if d != 4 else half for d in range(NZ)] + [half],
        in_specs=[sm] * 2 + [vm] * 12,
        out_specs=[vm] * (NZ + 1),
        scratch_shapes=[
            pltpu.VMEM((NY, 8 * TR + 8, WIDE), F32),
            pltpu.VMEM((NZ, 4, P_SIZE, P_SIZE), F32),
            pltpu.VMEM((8, 128), jnp.int32),
            pltpu.SMEM((8, 128), jnp.int32),
            pltpu.SemaphoreType.DMA,
        ],
        compiler_params=pltpu.CompilerParams(vmem_limit_bytes=20 * 1024 * 1024),
        cost_estimate=pl.CostEstimate(flops=1_000_000, bytes_accessed=12_000_000, transcendentals=0),
        name="cut",
    )(shard, region, *grads, *mine, *theirs)


def deposit_kernel(places, n_in, shard_ref, region_ref, *refs):
    way = direction(shard_ref[0])
    blocks, (out_ref, wide, sem) = refs[: len(places)], refs[n_in:]
    z, y = region_ref[0] // NY, region_ref[0] % NY
    copies = []
    for block, (dz, ys) in zip(blocks, places):
        for j, k in enumerate(ys):
            at = len(copies)

            def widen(q, carry, block=block, j=j, at=at):
                wide[at, q] = block[4 * j + q].astype(F32)
                return carry

            lax.fori_loop(0, 4, widen, 0)
            cp = pltpu.make_async_copy(wide.at[at], out_ref.at[(z + way * dz + NZ) % NZ, (y - way * k + NY) % NY], sem.at[at])
            cp.start()
            copies.append(cp)
    for cp in copies:
        cp.wait()


def deposit(shard, region, out, items):
    places = [item[1:] for item in items]
    blocks = [item[0] for item in items]
    n, total = len(items), sum(len(item[2]) for item in items)
    hbm = pl.BlockSpec(memory_space=pltpu.HBM)
    old = [] if out is None else [out]
    return pl.pallas_call(
        functools.partial(deposit_kernel, places, n + len(old)),
        out_shape=jax.ShapeDtypeStruct((NZ, NY, 4, P_SIZE, P_SIZE), F32),
        in_specs=[pl.BlockSpec(memory_space=pltpu.SMEM)] * 2 + [pl.BlockSpec(memory_space=pltpu.VMEM)] * n + [hbm] * len(old),
        out_specs=hbm,
        input_output_aliases={n + 2: 0} if old else {},
        scratch_shapes=[pltpu.VMEM((total, 4, P_SIZE, P_SIZE), F32), pltpu.SemaphoreType.DMA((total,))],
        compiler_params=pltpu.CompilerParams(vmem_limit_bytes=16 * 1024 * 1024),
        cost_estimate=pl.CostEstimate(flops=200_000 * total, bytes_accessed=400_000 * total, transcendentals=0),
        name="deposit",
    )(shard, region, *blocks, *old)


def shift(v, axis, by):
    n = lax.axis_size(axis)
    first = axis == "x"
    place_of = (lambda core, i: i * NC + core) if first else (lambda core, i: core * n + i)
    ring = [(place_of(core, i), place_of(core, (i + (by if core == 0 else -by)) % n)) for core in range(NC) for i in range(n)]
    return lax.ppermute(v, ("x", "core") if first else ("core", axis), ring)


def swap(v):
    return lax.ppermute(v, "core", [(0, 1), (1, 0)])


def sum_along_z(slots):
    own, one, two, three, low, five, six, seven, high = slots
    three, five = shift(three, "z", 1), shift(five, "z", -1)
    low, high = shift(low, "z", 2).astype(F32), shift(high, "z", -2).astype(F32)
    three, one, seven = lax.optimization_barrier((three, one, seven))
    two, six = two + three.astype(F32), six + five.astype(F32)
    two = jnp.concatenate([two[:2] + low, two[2:]])
    six = jnp.concatenate([six[:2], six[2:] + high])
    near = shift(one, "z", 1).astype(F32) + shift(seven, "z", -1).astype(F32)
    return own + near + shift(two.astype(BF), "z", 2).astype(F32) + shift(six.astype(BF), "z", -2).astype(F32)


def spread(part, shard, region):
    far = shift(part, "y", 2)
    own = jnp.concatenate([part, far])
    ups, downs = [jnp.concatenate([shift(part, "z", by), shift(far, "z", by)]) for by in (1, -1)]
    came = [(shift(own, "y", 1), 0, (1, 3))]
    out = deposit(shard, region, None, [(own, 0, (0, 2))])
    for d in (1, 2, 3):
        ups, downs, out = lax.optimization_barrier((ups, downs, out))
        here = [(ups, -d, (0, 2)), (downs, d, (0, 2))]
        ups = shift(ups, "z", 1)
        if d < 3:
            downs = shift(downs, "z", -1)
        side = [(shift(here[0][0], "y", 1), -d, (1, 3)), (shift(here[1][0], "y", -1), d, (3, 1))]
        out = deposit(shard, region, out, here + came)
        came = side
    ups, out = lax.optimization_barrier((ups, out))
    side = shift(ups, "y", 1)
    out = deposit(shard, region, out, [(ups, -4, (0, 2))] + came)
    out = deposit(shard, region, out, [(side, -4, (1, 3))])
    return out.reshape(MAS_DEV, P_SIZE, P_SIZE)


def body(masters, inst_master, inst_row, inst_col, def_index, def_weights, kernels, target):
    shard = lax.axis_index(("x", "core")).reshape(1)
    region = lax.axis_index(("z", "y")).reshape(1)
    tmid = target[0]
    mine, theirs, info = place(shard, inst_master, inst_row, inst_col, masters, tmid)
    other = swap(theirs)
    rims = other[NX * EXT :]
    sums = [mine[d] + other[EXT * d : EXT * d + EXT].astype(F32) for d in range(NX)]
    sends = [jnp.concatenate([sums[d].astype(BF), rims]) if d == 1 else sums[d].astype(BF) for d in range(NX)]
    parts = [sums[0]] + [shift(sends[d], "x", d) for d in (1, 2, 3)]
    table = make_table(kernels)
    tmid = target[0]
    resist, grad = image(def_index, shard, def_weights, parts, rims, tmid, info, table)
    across, before, after = [shift(grad, "y", k) for k in (2, 1, 3)]
    grads = [grad, before, across, after]
    own = jnp.stack([g[:TR] for g in grads])
    up, down, far = [shift(own, "x", by) for by in (1, 3, 2)]
    bands = (own, up, down, far)
    swapped = [swap(v) for v in bands]
    part = sum_along_z(cut(shard, region, grads, bands, swapped)).astype(BF)
    return (spread(part, shard, region), resist[None])


def solution(mesh):
    fine = Mesh(mesh.devices.reshape(NX, NC, NZ, NY), ("x", "core", "z", "y"))
    master, region = ("x", "core"), ("z", "y")
    return jax.shard_map(
        body,
        mesh=fine,
        in_specs=(
            P(master, None, None),
            P(None, region, None),
            P(None, region, None),
            P(None, region, None),
            P(region),
            P(),
            P(),
            P(region, master, None),
        ),
        out_specs=(P(master, None, None), P(region, master, None)),
        check_vma=False,
    )
```
